256 devices in a mesh: rows: 16 (over x, z_hi), cols: 16 (over z_lo, y, core).
Axes of the slice: x: 4, y: 4, z: 8 (z_hi: 4, z_lo: 2; z = z_hi * 2 + z_lo), core: 2. Of those that a mesh axis runs over, the one named last changes fastest.
Arguments:
- rainfall: float32 [256, 256], P(('rows', 'cols')), may hold values from 2 to 60
- infil_rate: float32 [256, 256], P(('rows', 'cols')), may hold values from 5 to 80
- porosity: float32 [256, 256], P(('rows', 'cols')), may hold values from 0.38 to 0.5
- soil_liquid: float32 [4, 256, 256], P(None, ('rows', 'cols')), may hold values from 0.1 to 0.3
- soil_ice: float32 [4, 256, 256], P(None, ('rows', 'cols')), may hold values from 0 to 0.15
- flow_dir: int32 [2560, 2560], P('rows', 'cols'), may hold values from 0 to 7
- routing_class: int32 [2560, 2560], P('rows', 'cols'), may hold values from 0 to 2, as said below
- overland_rate: bfloat16 [2560, 2560], P('rows', 'cols'), may hold values from 0.049804688 to 0.44921875
- lateral_rate: bfloat16 [2560, 2560], P('rows', 'cols'), may hold values from 0.049804688 to 0.5
- subgrid_weight: bfloat16 [2560, 2560], P('rows', 'cols'), may hold values from 0.29882812 to 3
Outputs:
- new_liquid: float32 [4, 256, 256], P(None, ('rows', 'cols'))
- ponded: float32 [256, 256], P(('rows', 'cols'))
- channel_water: float32 [256, 256], P(('rows', 'cols'))
The draws below stay inside these ranges and needn't reach their ends.
Inputs may be any that keep to these rules, and one draw needn't show every extreme that they name: `routing_class`: 0 marks land, 1 channel, 2 lake.
All inputs are finite; a program needn't handle non-finite values.
Results may differ from the reference program's by a relative error of at most 0.0003.
Values sent between devices are 32-bit elements; how exact they have to be, the bound alone decides.
A program may use at most 64 MiB of HBM per device.

```python
import math
import jax
import jax.numpy as jnp

REFINE = 10
LAYERS = 4
NSUB = 3
NCR = 256
NCC = 256
NFR = 2560
NFC = 2560


def draw_routing_class(key, part):
    key = jax.random.fold_in(key, 7)
    value = jax.random.randint(key, (NFR, NFC), 0, 100)
    return (value >= 85).astype(jnp.int32) + (value >= 96).astype(jnp.int32)


def set_ends(entries, key, low, largest):
    longest = entries.shape.index(max(entries.shape))
    spots = []
    for shift in (0, 1):
        where = [jax.random.randint(jax.random.fold_in(key, axis), (), 0, length) for axis, length in enumerate(entries.shape)]
        where[longest] = (where[longest] + shift) % entries.shape[longest]
        spots.append(tuple(where))
    return entries.at[spots[0]].set(low).at[spots[1]].set(largest)


def shard_levels(stream_key, shape, shards, smallest, top_value):
    factor_of, own = 1.0, jax.random.fold_in(stream_key, 6)
    for axis_at, shards_of in shards:
        heights = jnp.exp(jax.random.uniform(jax.random.fold_in(own, axis_at), (shards_of,), jnp.float32, smallest / len(shards), top_value / len(shards)))
        factor_of = factor_of * jnp.repeat(heights, shape[axis_at] // shards_of).reshape([-1 if axis == axis_at else 1 for axis in range(len(shape))])
    return factor_of


def setup_inputs(seed: int = 0) -> dict:
    arg_keys = jax.random.split(jax.random.key(seed), 11)
    return {
        "rainfall": jnp.clip(jnp.exp(math.log(60.0) - 3.4011974 * jax.random.uniform(arg_keys[0], (NCR, NCC), jnp.float32) ** shard_levels(arg_keys[0], (NCR, NCC), ((0, 256),), -0.2, 0.2)), 2.0, 60.0),
        "infil_rate": jnp.clip(jnp.exp(math.log(80.0) - 2.7725887 * jax.random.uniform(arg_keys[1], (NCR, NCC), jnp.float32) ** shard_levels(arg_keys[1], (NCR, NCC), ((0, 256),), -0.2, 0.2)), 5.0, 80.0),
        "porosity": jnp.clip(0.38 + 0.120000005 * jax.random.uniform(arg_keys[2], (NCR, NCC), jnp.float32) ** shard_levels(arg_keys[2], (NCR, NCC), ((0, 256),), -0.2, 0.2), 0.38, 0.5),
        "soil_liquid": jnp.clip(0.1 + 0.20000001043081284 * jax.random.uniform(arg_keys[3], (LAYERS, NCR, NCC), jnp.float32) ** shard_levels(arg_keys[3], (LAYERS, NCR, NCC), ((1, 256),), -0.2, 0.2), 0.1, 0.3),
        "soil_ice": jnp.clip(0.15 * jax.random.uniform(arg_keys[4], (LAYERS, NCR, NCC), jnp.float32) ** shard_levels(arg_keys[4], (LAYERS, NCR, NCC), ((1, 256),), -0.2, 0.2), 0.0, 0.15),
        "flow_dir": set_ends(jax.random.randint(arg_keys[5], (NFR, NFC), 0, 8), jax.random.fold_in(arg_keys[5], 1), 0, 7).astype(jnp.int32),
        "routing_class": draw_routing_class(jax.random.fold_in(arg_keys[10], 71), 0),
        "overland_rate": jnp.clip(jnp.exp(math.log(0.44921875) - 2.199401 * jax.random.uniform(arg_keys[7], (NFR, NFC), jnp.float32) ** shard_levels(arg_keys[7], (NFR, NFC), ((0, 16), (1, 16)), -0.2, 0.2)), 0.049804688, 0.44921875).astype(jnp.bfloat16),
        "lateral_rate": jnp.clip(jnp.exp(math.log(0.5) - 2.306499 * jax.random.uniform(arg_keys[8], (NFR, NFC), jnp.float32) ** shard_levels(arg_keys[8], (NFR, NFC), ((0, 16), (1, 16)), -0.2, 0.2)), 0.049804688, 0.5).astype(jnp.bfloat16),
        "subgrid_weight": jnp.clip(jnp.exp(math.log(3.0) - 2.306499 * jax.random.uniform(arg_keys[9], (NFR, NFC), jnp.float32) ** shard_levels(arg_keys[9], (NFR, NFC), ((0, 16), (1, 16)), -0.2, 0.2)), 0.29882812, 3.0).astype(jnp.bfloat16),
    }


thickness = (0.1, 0.3, 0.6, 1.0)
layer_speed = (1.0, 0.8, 0.6, 0.4)
steps_d8 = ((0, 1), (1, 1), (1, 0), (1, -1), (0, -1), (-1, -1), (-1, 0), (-1, 1))


def expand_coarse(coarse):
    lead = coarse.shape[:-2]
    nrow, ncol = coarse.shape[-2:]
    grown = jnp.broadcast_to(coarse[..., :, None, :, None], lead + (nrow, REFINE, ncol, REFINE))
    return grown.reshape(lead + (nrow * REFINE, ncol * REFINE))


def block_mean(fine):
    lead = fine.shape[:-2]
    nrow, ncol = fine.shape[-2:]
    split = fine.reshape(lead + (nrow // REFINE, REFINE, ncol // REFINE, REFINE))
    return jnp.mean(split, axis=(-3, -1))


def infiltrate(rainfall, infil_rate, porosity, soil_liquid, soil_ice):
    top_sat = (soil_liquid[0] + soil_ice[0]) / porosity
    capacity = infil_rate * jnp.maximum(1.0 - top_sat, 0.1)
    excess = rainfall * rainfall / (rainfall + capacity)
    top = soil_liquid[0] + (rainfall - excess) / (1000.0 * thickness[0])
    return excess, jnp.concatenate([top[None], soil_liquid[1:]], 0)


def outflow_volumes(ponded_depth, liquid_water, frozen_water, inverse_porosity, overland_flux_rate, lateral_flux_rate, cell_kind):
    q_raw = overland_flux_rate * ponded_depth * ponded_depth / (ponded_depth + 2.0)
    discharge_out = jnp.where(cell_kind == 2, 0.0, q_raw)
    routed = jnp.where(cell_kind == 0, discharge_out, 0.0)
    channel_flags = jnp.where(cell_kind == 1, discharge_out, 0.0)
    speed = jnp.array(layer_speed, jnp.float32)[:, None, None]
    saturation = jnp.minimum((liquid_water + frozen_water) * inverse_porosity, 1.0)
    lateral_flux = lateral_flux_rate * speed * liquid_water * saturation * saturation
    return discharge_out, jnp.concatenate([routed[None], lateral_flux], 0), channel_flags


def gather_inflow(moving_water, dirs):
    nrow = moving_water.shape[-2] - 2
    ncol = moving_water.shape[-1] - 2
    total = jnp.zeros(moving_water.shape[:-2] + (nrow, ncol), jnp.float32)
    for code, (d_row, d_col) in enumerate(steps_d8):
        sent = jnp.where(dirs == code, moving_water, 0.0)
        total = total + sent[:, 1 - d_row:1 - d_row + nrow, 1 - d_col:1 - d_col + ncol]
    return total


def settle_water(ponded_depth, liquid_water, frozen_water, pore_fraction, discharge_out, lateral_flux, inflow_volume):
    depth_new = ponded_depth - discharge_out + inflow_volume[0]
    updated_liquid = liquid_water - lateral_flux + inflow_volume[1:]
    spill_volume = jnp.maximum(updated_liquid + frozen_water - pore_fraction, 0.0)
    layer_mm = 1000.0 * jnp.array(thickness, jnp.float32)[:, None, None]
    return depth_new + jnp.sum(spill_volume * layer_mm, 0), updated_liquid - spill_volume


def reference(rainfall, infil_rate, porosity, soil_liquid, soil_ice, flow_dir, routing_class, overland_rate, lateral_rate, subgrid_weight):
    excess, liquid_c = infiltrate(rainfall, infil_rate, porosity, soil_liquid, soil_ice)
    weight = subgrid_weight.astype(jnp.float32)
    ponded_depth = expand_coarse(excess) * weight / expand_coarse(block_mean(weight))
    liquid_water = expand_coarse(liquid_c)
    frozen_water = expand_coarse(soil_ice)
    pore_fraction = expand_coarse(porosity)
    inverse_porosity = 1.0 / pore_fraction
    overland_flux_rate = overland_rate.astype(jnp.float32)
    lateral_flux_rate = lateral_rate.astype(jnp.float32)
    dirs = jnp.pad(flow_dir, 1)
    channel_total = jnp.zeros(ponded_depth.shape, jnp.float32)
    for step in range(NSUB):
        discharge_out, moving_water, channel_flags = outflow_volumes(ponded_depth, liquid_water, frozen_water, inverse_porosity, overland_flux_rate, lateral_flux_rate, routing_class)
        padded = jnp.pad(moving_water, ((0, 0), (1, 1), (1, 1)))
        inflow_volume = gather_inflow(padded, dirs)
        ponded_depth, liquid_water = settle_water(ponded_depth, liquid_water, frozen_water, pore_fraction, discharge_out, moving_water[1:], inflow_volume)
        channel_total = channel_total + channel_flags
    return block_mean(liquid_water), block_mean(ponded_depth), block_mean(channel_total)
```

```python
import functools

import jax
import jax.numpy as jnp
from jax import lax
from jax.experimental import pallas as pl
from jax.experimental.pallas import tpu as pltpu
from jax.sharding import PartitionSpec as P

MESH = pl.DeviceIdType.MESH
REFINE = 10
LAYERS = 4
TILE = 160
CR = 16
W = 256
HALO = 3

thickness = (0.1, 0.3, 0.6, 1.0)
layer_speed = (1.0, 0.8, 0.6, 0.4)

DIR, ORATE, KIND, LRATE, SHARE = range(5)
FIELDS = 5
COARSE = 10


def iota(shape, dim):
    return lax.broadcasted_iota(jnp.int32, shape, dim)


def take(x, index):
    return jnp.take_along_axis(x, index, axis=1, mode="promise_in_bounds")


def tenth(x):
    return lax.shift_right_logical(x * 6554, 16)


def split3(x):
    hi = x.astype(jnp.bfloat16)
    r = x - hi.astype(jnp.float32)
    mid = r.astype(jnp.bfloat16)
    lo = (r - mid.astype(jnp.float32)).astype(jnp.bfloat16)
    return jnp.concatenate([hi, mid, lo], 0)


def dot3(x, ones):
    n = x.shape[0]
    y = jnp.dot(split3(x), ones, preferred_element_type=jnp.float32)
    return y[:n] + y[n : 2 * n] + y[2 * n :]


def inflow_masks(d_up, d_mid, d_down):
    return (
        d_up == 1.0,
        d_mid == 0.0,
        d_down == 7.0,
        d_up == 3.0,
        d_mid == 4.0,
        d_down == 5.0,
        d_up == 2.0,
        d_down == 6.0,
    )


def inflow(masks, up, mid, down):
    e0, e1, e2, w0, w1, w2, s0, s1 = masks
    zero = jnp.zeros_like(up)
    east = jnp.where(e0, up, zero) + jnp.where(e1, mid, zero) + jnp.where(e2, down, zero)
    west = jnp.where(w0, up, zero) + jnp.where(w1, mid, zero) + jnp.where(w2, down, zero)
    same = jnp.where(s0, up, zero) + jnp.where(s1, down, zero)
    return pltpu.roll(east, 1, 1) + pltpu.roll(west, W - 1, 1) + same


def outflow(h, liquid, orate, kind, lrate, ice, inv_por):
    q = orate * h * h / (h + 2.0)
    zero = jnp.zeros_like(q)
    moving = [jnp.where(kind == 0.0, q, zero)]
    for k in range(LAYERS):
        sat = jnp.minimum((liquid[k] + ice[k]) * inv_por, 1.0)
        moving.append((lrate * layer_speed[k]) * liquid[k] * (sat * sat))
    rest = [h - q] + [liquid[k] - moving[1 + k] for k in range(LAYERS)]
    return moving, rest, jnp.where(kind == 1.0, q, zero)


def settle(rest, arriving, ice_less_por):
    h = rest[0] + arriving[0]
    liquid = []
    for k in range(LAYERS):
        u = rest[1 + k] + arriving[1 + k]
        spill = jnp.maximum(u + ice_less_por[k], 0.0)
        h = h + (1000.0 * thickness[k]) * spill
        liquid.append(u - spill)
    return h, liquid


def kernel(
    nr,
    nc,
    rain_h,
    infil_h,
    por_h,
    liq_h,
    ice_h,
    dir_h,
    kind_h,
    orate_h,
    lrate_h,
    weight_h,
    out_liq,
    out_h,
    out_c,
    rain,
    infil,
    por,
    liq,
    ice,
    dir_v,
    kind_v,
    orate_v,
    lrate_v,
    weight_v,
    nat,
    stat,
    tstat,
    dirs,
    tdirs,
    coarse,
    tcoarse,
    moving,
    tmoving,
    rest,
    trest,
    zsend,
    zrecv,
    vsend,
    vrecv,
    csend,
    crecv,
    hsend,
    hrecv,
    bsend,
    brecv,
    in_sem,
    zs_sem,
    zh_sem,
    zr_sem,
    vs_sem,
    vr_sem,
    cs_sem,
    cr_sem,
    hs_sem,
    hr_sem,
    bs_sem,
    br_sem,
):
    mi = lax.axis_index("rows")
    mj = lax.axis_index("cols")
    has_up, has_down = mi > 0, mi < nr - 1
    has_left, has_right = mj > 0, mj < nc - 1

    copies = [
        pltpu.make_async_copy(src, dst, in_sem.at[n])
        for n, (src, dst) in enumerate(
            (
                (rain_h, rain),
                (infil_h, infil),
                (por_h, por),
                (liq_h, liq),
                (ice_h, ice),
                (weight_h, weight_v),
                (dir_h, dir_v),
                (kind_h, kind_v),
                (orate_h, orate_v),
                (lrate_h, lrate_v),
            )
        )
    ]
    for copy in copies:
        copy.start()

    barrier = pltpu.get_barrier_semaphore()

    def tell(i, j):
        pl.semaphore_signal(barrier, inc=1, device_id=(i, j), device_id_type=MESH)

    @pl.loop(1, nc)
    def _(d):
        tell(mi, lax.rem(mj + d, nc))

    sides = (
        (has_up, mi - 1, has_left, has_right, nc - 1),
        (has_down, mi + 1, has_left, has_right, 0),
    )
    for has, i, left, right, end in sides:

        @pl.when(has)
        def _(i=i, end=end):
            tell(i, mj)
            tell(i, end)

        @pl.when(has & left)
        def _(i=i):
            tell(i, mj - 1)

        @pl.when(has & right)
        def _(i=i):
            tell(i, mj + 1)

    for copy in copies[:5]:
        copy.wait()
    rain_x, por_x = rain[...], por[...]
    top_sat = (liq[0] + ice[0]) / por_x
    capacity = infil[...] * jnp.maximum(1.0 - top_sat, 0.1)
    excess = rain_x * rain_x / (rain_x + capacity)
    top = liq[0] + (rain_x - excess) / (1000.0 * thickness[0])
    strip = [excess, por_x, top] + [liq[k] for k in range(1, LAYERS)] + [ice[k] for k in range(LAYERS)]

    lane = iota((8, 128), 1)
    slot = tenth(lane * 10) * 0 + lax.shift_right_logical(lane * 2731, 16)
    t = lane - slot * 24
    for half in range(2):
        base = (iota((8, 128), 0) + 8 * half) * 16 - 1 + t
        inside = jnp.clip(base, 0, W - 1)
        index = inside & 127
        low = inside < 128
        for group in range(2):
            packed = jnp.zeros((8, 128), jnp.float32)
            for n in range(5):
                x = strip[group * 5 + n]
                a = jnp.broadcast_to(x[:, :128], (8, 128))
                b = jnp.broadcast_to(x[:, 128:], (8, 128))
                packed = jnp.where(slot == n, jnp.where(low, take(a, index), take(b, index)), packed)
            for s in range(8):
                zsend[8 * half + s, :, 128 * group : 128 * group + 128] = packed[s : s + 1]

    zrecv[mj] = zsend[mj]

    @pl.when(jnp.logical_not(has_down))
    def _():
        zrecv[CR] = zsend[mj]

    @pl.when(jnp.logical_not(has_up))
    def _():
        zrecv[CR + 1] = zsend[mj]

    incoming = nc - 1
    for has, i, left, right, end in sides:
        incoming += has.astype(jnp.int32) + (has & left).astype(jnp.int32) + (has & right).astype(jnp.int32)
    incoming += nc * ((has_up & (mj == 0)).astype(jnp.int32) + (has_down & (mj == nc - 1)).astype(jnp.int32))
    pl.semaphore_wait(barrier, incoming)

    def piece(k, i, s, sems):
        return pltpu.make_async_remote_copy(
            src_ref=zsend.at[k],
            dst_ref=zrecv.at[s],
            send_sem=sems.at[k],
            recv_sem=zr_sem.at[s],
            device_id=(i, k),
            device_id_type=MESH,
        )

    @pl.loop(1, nc)
    def _(d):
        piece(lax.rem(mj + d, nc), mi, mj, zs_sem).start()

    first_up = has_up & (mj == 0)
    last_down = has_down & (mj == nc - 1)

    @pl.when(first_up)
    def _():
        @pl.loop(0, nc)
        def _(k):
            piece(k, mi - 1, CR, zh_sem).start()

    @pl.when(last_down)
    def _():
        @pl.loop(0, nc)
        def _(k):
            piece(k, mi + 1, CR + 1, zh_sem).start()

    for copy in copies[5:]:
        copy.wait()
    lane160 = jnp.zeros((TILE, 96), jnp.float32)
    kind_x = kind_v[...].astype(jnp.float32)
    orate_x = jnp.where(kind_x == 2.0, 0.0, orate_v[...].astype(jnp.float32))
    natural = (
        dir_v[...].astype(jnp.float32),
        orate_x,
        kind_x,
        lrate_v[...].astype(jnp.float32),
        weight_v[...].astype(jnp.float32),
    )
    for f in range(FIELDS):
        nat[2 * f] = natural[f][:, :128]
        nat[2 * f + 1] = jnp.concatenate([natural[f][:, 128:], lane160], 1)

    def rows_of(f, rr):
        return jnp.concatenate(
            [nat.at[2 * f + half][pl.ds(rr, CR, stride=REFINE), :] for half in range(2)], 1
        )

    weights = [rows_of(SHARE, rr) for rr in range(REFINE)]
    total = functools.reduce(lambda a, b: a + b, weights)
    row_c, col_c = iota((W, W), 0), iota((W, W), 1)
    same_block = (tenth(row_c) == tenth(col_c)) & (row_c < TILE) & (col_c < TILE)
    mean_of = dot3(total, jnp.where(same_block, 1.0, 0.0).astype(jnp.bfloat16))
    wide = iota((CR, W), 1)
    per_mean = 100.0 / jnp.where(wide < TILE, mean_of, 1.0)
    for rr in range(REFINE):
        stat[SHARE, rr * CR : (rr + 1) * CR] = weights[rr] * per_mean
        for f in (ORATE, KIND, LRATE):
            stat[f, rr * CR : (rr + 1) * CR] = rows_of(f, rr)
        dirs[(rr + 1) * CR : (rr + 2) * CR] = rows_of(DIR, rr)

    def tile_rows(f, rr):
        if f == DIR:
            return dirs[(rr + 1) * CR : (rr + 2) * CR]
        return stat[f, rr * CR : (rr + 1) * CR]

    zero_row = jnp.zeros((1, W), jnp.float32)
    for f in range(FIELDS):
        off = CR if f == DIR else 0
        ref = dirs if f == DIR else stat.at[f]
        for p in range(HALO):
            vsend[0, HALO * f + p : HALO * f + p + 1] = ref[off + p * CR : off + p * CR + 1]
            r = off + (REFINE - HALO + p) * CR + CR - 1
            vsend[1, HALO * f + p : HALO * f + p + 1] = ref[r : r + 1]
    for v in range(2):
        vsend[v, 15:16] = zero_row
        csend[v, 0] = pltpu.roll(vsend[v, :, :128], 32, 1)
        csend[v, 1] = pltpu.roll(vsend[v, :, 128:], 96, 1)

    def vertical(v, i):
        return pltpu.make_async_remote_copy(
            src_ref=vsend.at[v],
            dst_ref=vrecv.at[v],
            send_sem=vs_sem.at[v],
            recv_sem=vr_sem.at[v],
            device_id=(i, mj),
            device_id_type=MESH,
        )

    def corner(v, s, i, j):
        return pltpu.make_async_remote_copy(
            src_ref=csend.at[v, s],
            dst_ref=crecv.at[v, s],
            send_sem=cs_sem.at[v, s],
            recv_sem=cr_sem.at[v, s],
            device_id=(i, j),
            device_id_type=MESH,
        )

    for v, (has, i, left, right, end) in enumerate(sides):

        @pl.when(has)
        def _(v=v, i=i):
            vertical(v, i).start()

        @pl.when(has & left)
        def _(v=v, i=i):
            corner(v, 0, i, mj - 1).start()

        @pl.when(has & right)
        def _(v=v, i=i):
            corner(v, 1, i, mj + 1).start()

    lane16 = iota((CR, 128), 1)
    for s in range(3):
        slab = jnp.zeros((CR, 128), jnp.float32)
        for u in range(4):
            rr = 4 * s + u
            if rr >= REFINE:
                break
            for f in range(FIELDS):
                x = tile_rows(f, rr)
                at = HALO * (FIELDS * u + f)
                a = pltpu.roll(x[:, :128], at, 1) if at else x[:, :128]
                b = pltpu.roll(x[:, 128:], (64 + at - 29) % 128, 1)
                slab = jnp.where((lane16 >= at) & (lane16 < at + HALO), a, slab)
                slab = jnp.where((lane16 >= 64 + at) & (lane16 < 64 + at + HALO), b, slab)
        hsend[s] = slab

    def sideways(n, j):
        return pltpu.make_async_remote_copy(
            src_ref=hsend,
            dst_ref=hrecv.at[n],
            send_sem=hs_sem.at[n],
            recv_sem=hr_sem.at[n],
            device_id=(mi, j),
            device_id_type=MESH,
        )

    @pl.when(has_left)
    def _():
        sideways(0, mj - 1).start()

    @pl.when(has_right)
    def _():
        sideways(1, mj + 1).start()

    for v, (has, i, left, right, end) in enumerate(sides):

        @pl.when(jnp.logical_not(has))
        def _(v=v):
            vrecv[1 - v] = jnp.zeros(vrecv.shape[1:], jnp.float32)

        @pl.when(jnp.logical_not(has & left))
        def _(v=v):
            crecv[1 - v, 1] = jnp.zeros((CR, 128), jnp.float32)

        @pl.when(jnp.logical_not(has & right))
        def _(v=v):
            crecv[1 - v, 0] = jnp.zeros((CR, 128), jnp.float32)

    @pl.when(jnp.logical_not(has_right))
    def _():
        hrecv[0] = jnp.zeros(hrecv.shape[1:], jnp.float32)

    @pl.when(jnp.logical_not(has_left))
    def _():
        hrecv[1] = jnp.zeros(hrecv.shape[1:], jnp.float32)

    @pl.loop(1, nc)
    def _(d):
        k = lax.rem(mj + d, nc)
        piece(k, mi, k, zs_sem).wait_recv()

    @pl.when(has_down)
    def _():
        piece(0, mi, CR, zh_sem).wait_recv()

    @pl.when(has_up)
    def _():
        piece(0, mi, CR + 1, zh_sem).wait_recv()

    sub8 = iota((8, W), 0)
    under = jnp.broadcast_to(zrecv[CR], (8, W))
    over = jnp.broadcast_to(zrecv[CR + 1], (8, W))
    rows = [jnp.concatenate([zrecv[8 * n + s] for s in range(8)], 0) for n in range(2)]
    rows = jnp.concatenate(rows + [jnp.where(sub8 < 4, under, over)], 0)
    wide24 = iota((24, 128), 1)
    column = (
        1 + tenth(wide24),
        jnp.where(wide24 >= 125, 0, jnp.minimum(1 + tenth(wide24 + 128), 17)),
    )
    wide_fields = []
    for f in range(COARSE):
        g = rows[:, 128 * (f // 5) : 128 * (f // 5) + 128]
        at = 24 * (f % 5)
        wide_fields.append(jnp.concatenate([take(g, column[0] + at), take(g, column[1] + at)], 1))
    excess_w, por_w = wide_fields[0], wide_fields[1]
    ice_w = wide_fields[2 + LAYERS :]
    kept = [1.0 / por_w] + ice_w + [x - por_w for x in ice_w]
    for n, x in enumerate(kept):
        coarse[n] = x[:CR]
        tcoarse[n] = x[CR:]

    for v, (has, i, left, right, end) in enumerate(sides):

        @pl.when(has)
        def _(v=v):
            vertical(1 - v, mi).wait_recv()

        @pl.when(has & left)
        def _(v=v):
            corner(1 - v, 1, mi, mj).wait_recv()

        @pl.when(has & right)
        def _(v=v):
            corner(1 - v, 0, mi, mj).wait_recv()

    @pl.when(has_right)
    def _():
        sideways(0, mj).wait_recv()

    @pl.when(has_left)
    def _():
        sideways(1, mj).wait_recv()

    right_halo = (lane16 >= 32) & (lane16 < 32 + HALO)
    left_halo = lane16 >= 128 - HALO

    for v in range(2):
        far = jnp.where(right_halo, crecv[v, 0], jnp.where(left_halo, crecv[v, 1], 0.0))
        far = jnp.where(lane16 < 32, vrecv[v, :, 128:], far)
        vrecv[v, :, 128:] = far
    zero3 = jnp.zeros((2, W), jnp.float32)
    for f in range(FIELDS):
        x = jnp.concatenate(
            [vrecv[0, HALO * f : HALO * f + HALO], zero3, vrecv[1, HALO * f : HALO * f + HALO]], 0
        )
        tstat[f] = x

    for s in range(3):
        slab = jnp.where(lane16 < 64, hrecv[0, s], hrecv[1, s])
        for u in range(4):
            rr = 4 * s + u
            if rr >= REFINE:
                break
            for f in range(FIELDS):
                at = HALO * (FIELDS * u + f)
                from_right = pltpu.roll(slab, (32 - at) % 128, 1)
                from_left = pltpu.roll(slab, (125 - 64 - at) % 128, 1)
                ref = dirs if f == DIR else stat.at[f]
                r = rr * CR + (CR if f == DIR else 0)
                x = ref[r : r + CR, 128:]
                x = jnp.where(right_halo, from_right, jnp.where(left_halo, from_left, x))
                ref[r : r + CR, 128:] = x

    def wrap(first, last, tail):
        up = pltpu.roll(jnp.concatenate([last, tail], 0), 1, 0)
        down = pltpu.roll(jnp.concatenate([first, tail], 0), CR + 7, 0)
        return up, down

    up, down = wrap(dirs[CR : 2 * CR], dirs[TILE : TILE + CR], tstat[DIR])
    dirs[:CR], tdirs[0] = up[:CR], up[CR:]
    dirs[TILE + CR :], tdirs[1] = down[:CR], down[CR:]

    def finish_wrap(b):
        for f in range(FIELDS):
            up, down = wrap(moving[b, f, CR : 2 * CR], moving[b, f, TILE : TILE + CR], tmoving[b, f])
            moving[b, f, :CR], tmoving[2 + b, f] = up[:CR], up[CR:]
            moving[b, f, TILE + CR :], tmoving[4 + b, f] = down[:CR], down[CR:]

    def main_in(b, r):
        d = [dirs[pl.ds(r + n * CR, CR), :] for n in range(3)]
        masks = inflow_masks(*d)
        arriving = [
            inflow(masks, *[moving[b, f, pl.ds(r + n * CR, CR), :] for n in range(3)])
            for f in range(FIELDS)
        ]
        left = [rest[f, pl.ds(r, CR), :] for f in range(FIELDS)]
        return settle(left, arriving, [coarse[1 + LAYERS + k] for k in range(LAYERS)])

    def main_out(b, r, h, liquid):
        move, left, chan = outflow(
            h,
            liquid,
            stat[ORATE, pl.ds(r, CR), :],
            stat[KIND, pl.ds(r, CR), :],
            stat[LRATE, pl.ds(r, CR), :],
            [coarse[1 + k] for k in range(LAYERS)],
            coarse[0],
        )
        for f in range(FIELDS):
            moving[b, f, pl.ds(r + CR, CR), :] = move[f]
            rest[f, pl.ds(r, CR), :] = left[f]
        return chan

    def tail_in(b):
        masks = inflow_masks(tdirs[0], tstat[DIR], tdirs[1])
        arriving = [
            inflow(masks, tmoving[2 + b, f], tmoving[b, f], tmoving[4 + b, f]) for f in range(FIELDS)
        ]
        return settle(
            [trest[f] for f in range(FIELDS)], arriving, [tcoarse[1 + LAYERS + k] for k in range(LAYERS)]
        )

    def tail_out(b, h, liquid):
        move, left, _ = outflow(
            h,
            liquid,
            tstat[ORATE],
            tstat[KIND],
            tstat[LRATE],
            [tcoarse[1 + k] for k in range(LAYERS)],
            tcoarse[0],
        )
        for f in range(FIELDS):
            tmoving[b, f] = move[f]
            trest[f] = left[f]

    def row_at(rr):
        return pl.multiple_of(rr * CR, CR)

    zero16 = jnp.zeros((CR, W), jnp.float32)
    excess_m = excess_w[:CR]
    liquid_m = [x[:CR] for x in wide_fields[2 : 2 + LAYERS]]

    def first(rr, chan):
        r = row_at(rr)
        return chan + main_out(0, r, excess_m * stat[SHARE, pl.ds(r, CR), :], liquid_m)

    chan = lax.fori_loop(0, REFINE, first, zero16)
    tail_out(0, excess_w[CR:] * tstat[SHARE], [x[CR:] for x in wide_fields[2 : 2 + LAYERS]])
    finish_wrap(0)

    for b in range(2):

        def middle(rr, chan, b=b):
            r = row_at(rr)
            return chan + main_out(1 - b, r, *main_in(b, r))

        chan = lax.fori_loop(0, REFINE, middle, chan)
        tail_out(1 - b, *tail_in(b))
        finish_wrap(1 - b)

    def last(rr, sums):
        h, liquid = main_in(0, row_at(rr))
        return tuple(a + x for a, x in zip(sums, liquid + [h]))

    sums = lax.fori_loop(0, REFINE, last, (zero16,) * (LAYERS + 1))

    row_p, col_p = iota((W, 128), 0), iota((W, 128), 1)
    to_block = (tenth(row_p) == col_p) & (row_p < TILE)
    means = dot3(jnp.concatenate(sums + (chan,), 0), jnp.where(to_block, 1.0, 0.0).astype(jnp.bfloat16)) * 0.01
    back = means[:CR]
    for n in range(1, LAYERS + 2):
        back = back + pltpu.roll(means[n * CR : (n + 1) * CR], 16 * n, 1)
    for s in range(CR):
        bsend[s] = back[s : s + 1]
    brecv[mj] = bsend[mj]

    def answer(k, s):
        return pltpu.make_async_remote_copy(
            src_ref=bsend.at[k],
            dst_ref=brecv.at[s],
            send_sem=bs_sem.at[k],
            recv_sem=br_sem.at[s],
            device_id=(mi, k),
            device_id_type=MESH,
        )

    @pl.loop(1, nc)
    def _(d):
        answer(lax.rem(mj + d, nc), mj).start()

    @pl.loop(1, nc)
    def _(d):
        piece(lax.rem(mj + d, nc), mi, mj, zs_sem).wait_send()

    @pl.when(first_up | last_down)
    def _():
        @pl.loop(0, nc)
        def _(k):
            piece(k, mi, CR, zh_sem).wait_send()

    for v, (has, i, left, right, end) in enumerate(sides):

        @pl.when(has)
        def _(v=v, i=i):
            vertical(v, i).wait_send()

        @pl.when(has & left)
        def _(v=v, i=i):
            corner(v, 0, i, mj - 1).wait_send()

        @pl.when(has & right)
        def _(v=v, i=i):
            corner(v, 1, i, mj + 1).wait_send()

    @pl.when(has_left)
    def _():
        sideways(0, mj - 1).wait_send()

    @pl.when(has_right)
    def _():
        sideways(1, mj + 1).wait_send()

    @pl.loop(1, nc)
    def _(d):
        k = lax.rem(mj + d, nc)
        answer(k, k).wait_recv()

    gather = iota((8, 128), 0) * 16 + (lane & 15)
    gather = jnp.minimum(gather, 127)
    owner = lax.shift_right_logical(lane, 4)
    for half in range(2):
        out = jnp.zeros((8, 128), jnp.float32)
        for s in range(8):
            x = jnp.broadcast_to(brecv[8 * half + s], (8, 128))
            out = jnp.where(owner == s, take(x, gather), out)
        lanes = slice(128 * half, 128 * half + 128)
        for k in range(LAYERS):
            out_liq[k, :, lanes] = out[k : k + 1]
        out_h[:, lanes] = out[LAYERS : LAYERS + 1]
        out_c[:, lanes] = out[LAYERS + 1 : LAYERS + 2]

    @pl.loop(1, nc)
    def _(d):
        k = lax.rem(mj + d, nc)
        answer(k, k).wait_send()


def solution(mesh):
    nr, nc = mesh.shape["rows"], mesh.shape["cols"]
    f32, bf16 = jnp.float32, jnp.bfloat16

    def step(*args):
        v = pltpu.VMEM
        dma = pltpu.SemaphoreType.DMA
        return pl.pallas_call(
            functools.partial(kernel, nr, nc),
            out_shape=(
                jax.ShapeDtypeStruct((LAYERS, 1, W), f32),
                jax.ShapeDtypeStruct((1, W), f32),
                jax.ShapeDtypeStruct((1, W), f32),
            ),
            in_specs=[pl.BlockSpec(memory_space=pl.ANY)] * 10,
            out_specs=[pl.BlockSpec(memory_space=pltpu.VMEM)] * 3,
            scratch_shapes=[
                v((1, W), f32),
                v((1, W), f32),
                v((1, W), f32),
                v((LAYERS, 1, W), f32),
                v((LAYERS, 1, W), f32),
                v((TILE, TILE), jnp.int32),
                v((TILE, TILE), jnp.int32),
                v((TILE, TILE), bf16),
                v((TILE, TILE), bf16),
                v((TILE, TILE), bf16),
                v((2 * FIELDS, TILE, 128), f32),
                v((FIELDS, TILE, W), f32),
                v((FIELDS, 8, W), f32),
                v((TILE + 2 * CR, W), f32),
                v((2, 8, W), f32),
                v((1 + 2 * LAYERS, CR, W), f32),
                v((1 + 2 * LAYERS, 8, W), f32),
                v((2, FIELDS, TILE + 2 * CR, W), f32),
                v((6, FIELDS, 8, W), f32),
                v((FIELDS, TILE, W), f32),
                v((FIELDS, 8, W), f32),
                v((CR, 1, W), f32),
                v((CR + 2, 1, W), f32),
                v((2, CR, W), f32),
                v((2, CR, W), f32),
                v((2, 2, CR, 128), f32),
                v((2, 2, CR, 128), f32),
                v((3, CR, 128), f32),
                v((2, 3, CR, 128), f32),
                v((CR, 1, 128), f32),
                v((CR, 1, 128), f32),
                dma((10,)),
                dma((CR,)),
                dma((CR,)),
                dma((CR + 2,)),
                dma((2,)),
                dma((2,)),
                dma((2, 2)),
                dma((2, 2)),
                dma((2,)),
                dma((2,)),
                dma((CR,)),
                dma((CR,)),
            ],
            compiler_params=pltpu.CompilerParams(
                collective_id=0, has_side_effects=True, vmem_limit_bytes=32 * 1024 * 1024
            ),
        )(*args)

    return jax.shard_map(
        step,
        mesh=mesh,
        in_specs=(
            P(("rows", "cols"), None),
            P(("rows", "cols"), None),
            P(("rows", "cols"), None),
            P(None, ("rows", "cols"), None),
            P(None, ("rows", "cols"), None),
            P("rows", "cols"),
            P("rows", "cols"),
            P("rows", "cols"),
            P("rows", "cols"),
            P("rows", "cols"),
        ),
        out_specs=(
            P(None, ("rows", "cols"), None),
            P(("rows", "cols"), None),
            P(("rows", "cols"), None),
        ),
        check_vma=False,
    )
```

```python
import functools
import math

import jax
import jax.numpy as jnp
from jax import lax
from jax.experimental import pallas as pl
from jax.experimental.pallas import tpu as pltpu
from jax.sharding import PartitionSpec as P

MESH = pl.DeviceIdType.MESH
REFINE = 10
LAYERS = 4
TILE = 160
CR = 16
W = 256
HALO = 3
ROWS = 2 * CR

thickness = (0.1, 0.3, 0.6, 1.0)
layer_speed = (1.0, 0.8, 0.6, 0.4)

DIR, ORATE, KIND, LRATE, SHARE = range(5)
FIELDS = 5
COARSE = 10


FAR_FIRST = sorted(
    ((z, y, c) for z in range(2) for y in range(4) for c in range(2) if z + y + c),
    key=lambda p: -(p[0] + min(p[1], 4 - p[1])),
)


def others(j):
    z, y, c = j // 8, (j // 2) % 4, j % 2
    return [((z + dz) % 2) * 8 + ((y + dy) % 4) * 2 + (c + dc) % 2 for dz, dy, dc in FAR_FIRST]


def iota(shape, dim):
    return lax.broadcasted_iota(jnp.int32, shape, dim)


def take(x, index):
    return jnp.take_along_axis(x, index, axis=1, mode="promise_in_bounds")


def tenth(x):
    return lax.shift_right_logical(x * 6554, 16)


def split3(x):
    hi = x.astype(jnp.bfloat16)
    r = x - hi.astype(jnp.float32)
    mid = r.astype(jnp.bfloat16)
    lo = (r - mid.astype(jnp.float32)).astype(jnp.bfloat16)
    return jnp.concatenate([hi, mid, lo], 0)


def split2(x):
    hi = x.astype(jnp.bfloat16)
    lo = (x - hi.astype(jnp.float32)).astype(jnp.bfloat16)
    return jnp.concatenate([hi, lo], 0)


def dot3(x, ones):
    n = x.shape[0]
    y = jnp.dot(split3(x), ones, preferred_element_type=jnp.float32)
    return y[:n] + y[n : 2 * n] + y[2 * n :]


def dot2(x, ones):
    n = x.shape[0]
    y = jnp.dot(split2(x), ones, preferred_element_type=jnp.float32)
    return y[:n] + y[n:]


def inflow_masks(d_up, d_mid, d_down):
    return (
        d_up == 1.0,
        d_mid == 0.0,
        d_down == 7.0,
        d_up == 3.0,
        d_mid == 4.0,
        d_down == 5.0,
        d_up == 2.0,
        d_down == 6.0,
    )


def inflow(masks, up, mid, down):
    e0, e1, e2, w0, w1, w2, s0, s1 = masks
    zero = jnp.zeros_like(up)
    east = jnp.where(e0, up, zero) + jnp.where(e1, mid, zero) + jnp.where(e2, down, zero)
    west = jnp.where(w0, up, zero) + jnp.where(w1, mid, zero) + jnp.where(w2, down, zero)
    same = jnp.where(s0, up, zero) + jnp.where(s1, down, zero)
    return same + pltpu.roll(east, 1, 1) + pltpu.roll(west, 127, 1)


def outflow(h, liquid, orate, kind, lrate, ice, per_pore):
    q = orate * h * (h / (h + 2.0))
    zero = jnp.zeros_like(q)
    moving = [jnp.where(kind == 0.0, q, zero)]
    rest = [h - q]
    for k in range(LAYERS):
        sat = jnp.minimum((liquid[k] + ice[k]) * per_pore[k], math.sqrt(layer_speed[k]))
        lateral = (lrate * liquid[k]) * (sat * sat)
        moving.append(lateral)
        rest.append(liquid[k] - lateral)
    return moving, rest, jnp.where(kind == 1.0, q, zero)


def settle(rest, arriving, room):
    h = rest[0] + arriving[0]
    liquid = []
    for k in range(LAYERS):
        u = rest[1 + k] + arriving[1 + k]
        h = h + jnp.maximum(u - room[k], 0.0)
        liquid.append(jnp.minimum(u, room[k]))
    return h, liquid


def kernel(
    nr,
    nc,
    rain_h,
    infil_h,
    por_h,
    liq_h,
    ice_h,
    dir_h,
    kind_h,
    orate_h,
    lrate_h,
    weight_h,
    out_liq,
    out_h,
    out_c,
    rain,
    infil,
    por,
    liq,
    ice,
    dir_v,
    kind_v,
    orate_v,
    lrate_v,
    weight_v,
    nat,
    stat,
    dirs,
    coarse,
    moving,
    rest,
    sstat,
    scoarse,
    zsend,
    zrecv,
    vsend,
    vrecv,
    csend,
    crecv,
    hsend,
    hrecv,
    bsend,
    brecv,
    in_sem,
    zs_sem,
    zh_sem,
    zr_sem,
    vs_sem,
    vr_sem,
    cs_sem,
    cr_sem,
    hs_sem,
    hr_sem,
    bs_sem,
    br_sem,
    row_sem,
    relay_sem,
):
    mi = lax.axis_index("rows")
    mj = lax.axis_index("cols")
    has_up, has_down = mi > 0, mi < nr - 1
    has_left, has_right = mj > 0, mj < nc - 1

    copies = [
        pltpu.make_async_copy(src, dst, in_sem.at[n])
        for n, (src, dst) in enumerate(
            (
                (rain_h, rain),
                (infil_h, infil),
                (por_h, por),
                (liq_h, liq),
                (ice_h, ice),
                (weight_h, weight_v),
                (dir_h, dir_v),
                (kind_h, kind_v),
                (orate_h, orate_v),
                (lrate_h, lrate_v),
            )
        )
    ]
    for copy in copies:
        copy.start()

    barrier = pltpu.get_barrier_semaphore()
    lead = nc - 2
    is_lead = mj == lead

    def tell(i, j):
        pl.semaphore_signal(barrier, inc=1, device_id=(i, j), device_id_type=MESH)

    @pl.when(jnp.logical_not(is_lead))
    def _():
        tell(mi, lead)

    sides = (
        (has_up, mi - 1, has_left, has_right, nc - 1),
        (has_down, mi + 1, has_left, has_right, 0),
    )
    for has, i, left, right, end in sides:

        @pl.when(has)
        def _(i=i, end=end):
            tell(i, end)

        @pl.when(has & jnp.logical_not(is_lead))
        def _(i=i):
            tell(i, mj)

        @pl.when(has & left & (mj - 1 != lead))
        def _(i=i):
            tell(i, mj - 1)

        @pl.when(has & right & (mj + 1 != lead))
        def _(i=i):
            tell(i, mj + 1)

    for copy in copies[:5]:
        copy.wait()
    rain_x, por_x = rain[...], por[...]
    top_sat = (liq[0] + ice[0]) / por_x
    capacity = infil[...] * jnp.maximum(1.0 - top_sat, 0.1)
    excess = rain_x * rain_x / (rain_x + capacity)
    top = liq[0] + (rain_x - excess) / (1000.0 * thickness[0])
    strip = [excess, por_x, top] + [liq[k] for k in range(1, LAYERS)] + [ice[k] for k in range(LAYERS)]

    lane = iota((8, 128), 1)
    slot = tenth(lane * 10) * 0 + lax.shift_right_logical(lane * 2731, 16)
    t = lane - slot * 24
    for half in range(2):
        base = (iota((8, 128), 0) + 8 * half) * 16 - 1 + t
        inside = jnp.clip(base, 0, W - 1)
        index = inside & 127
        low = inside < 128
        for group in range(2):
            packed = jnp.zeros((8, 128), jnp.float32)
            for n in range(5):
                x = strip[group * 5 + n]
                a = jnp.broadcast_to(x[:, :128], (8, 128))
                b = jnp.broadcast_to(x[:, 128:], (8, 128))
                packed = jnp.where(slot == n, jnp.where(low, take(a, index), take(b, index)), packed)
            for s in range(8):
                zsend[8 * half + s, :, 128 * group : 128 * group + 128] = packed[s : s + 1]

    zrecv[mj] = zsend[mj]

    @pl.when(jnp.logical_not(has_down))
    def _():
        zrecv[CR] = zsend[mj]

    @pl.when(jnp.logical_not(has_up))
    def _():
        zrecv[CR + 1] = zsend[mj]

    @pl.when(is_lead)
    def _():
        pl.semaphore_wait(barrier, nc - 1)
        for k in range(nc):
            if k != lead:
                pl.semaphore_signal(row_sem, inc=1, device_id=(mi, k), device_id_type=MESH)

    @pl.when(jnp.logical_not(is_lead))
    def _():
        pl.semaphore_wait(row_sem, 1)

    def piece(k, i, s, send, arrive):
        return pltpu.make_async_remote_copy(
            src_ref=zsend.at[k],
            dst_ref=zrecv.at[s],
            send_sem=send,
            recv_sem=arrive,
            device_id=(i, k),
            device_id_type=MESH,
        )

    def row_pieces():
        return pltpu.make_async_remote_copy(
            src_ref=zsend.at[: nc - 1],
            dst_ref=zrecv.at[: nc - 1],
            send_sem=zs_sem,
            recv_sem=zr_sem.at[0],
            device_id=(mi, mj),
            device_id_type=MESH,
        )

    for k in others(mj):
        piece(k, mi, mj, zs_sem, zr_sem.at[0]).start()

    first_up = has_up & (mj == 0)
    last_down = has_down & (mj == nc - 1)

    for copy in copies[5:]:
        copy.wait()
    kind_x = kind_v[...].astype(jnp.float32)
    natural = (
        dir_v[...].astype(jnp.float32),
        jnp.where(kind_x == 2.0, 0.0, orate_v[...].astype(jnp.float32)),
        kind_x,
        lrate_v[...].astype(jnp.float32),
        weight_v[...].astype(jnp.float32),
    )
    no_lanes = jnp.zeros((TILE, 96), jnp.float32)
    for f in range(FIELDS):
        nat[2 * f] = natural[f][:, :128]
        nat[2 * f + 1] = jnp.concatenate([natural[f][:, 128:], no_lanes], 1)

    lane16 = iota((CR, 128), 1)

    def halves(a, b):
        right = jnp.where(lane16 < 51, pltpu.roll(a, 51, 1), pltpu.roll(b, 51, 1))
        return jnp.concatenate([pltpu.roll(a, HALO, 1), right], 0)

    def rows_of(f, rr):
        return [nat.at[2 * f + half][pl.ds(rr, CR, stride=REFINE), :] for half in range(2)]

    def field(f):
        return (dirs, ROWS) if f == DIR else (stat.at[f], 0)

    def put(f, rr, x):
        ref, off = field(f)
        ref[off + rr * ROWS : off + (rr + 1) * ROWS] = x

    def get(f, rr):
        ref, off = field(f)
        return ref[off + rr * ROWS : off + (rr + 1) * ROWS]

    weights = [rows_of(SHARE, rr) for rr in range(REFINE)]
    total = [functools.reduce(lambda a, b: a + b, [w[half] for w in weights]) for half in range(2)]
    row_c, col_c = iota((W, W), 0), iota((W, W), 1)
    same_block = (tenth(row_c) == tenth(col_c)) & (row_c < TILE) & (col_c < TILE)
    sums = dot3(jnp.concatenate(total, 1), jnp.where(same_block, 1.0, 0.0).astype(jnp.bfloat16))
    per_mean = 100.0 / jnp.where(iota((CR, W), 1) < TILE, sums, 1.0)
    shares = [[w[half] * per_mean[:, 128 * half : 128 * half + 128] for half in range(2)] for w in weights]

    for v in range(2):
        r = v * (TILE - HALO)
        for half in range(2):
            for f in range(SHARE):
                vsend[v, half, HALO * f : HALO * f + HALO] = nat[2 * f + half, r : r + HALO]
            for p in range(HALO):
                x = shares[p + v * (REFINE - HALO)][half][v * (CR - 1) : v * (CR - 1) + 1]
                vsend[v, half, HALO * SHARE + p : HALO * SHARE + p + 1] = x
            vsend[v, half, HALO * FIELDS :] = jnp.zeros((1, 128), jnp.float32)
        x = halves(vsend[v, 0], vsend[v, 1])
        vsend[v, 0], vsend[v, 1] = x[:CR], x[CR:]
        for half, at in ((0, HALO), (1, 80)):
            place = lane16 - HALO * iota((CR, 128), 0)
            end = take(x[half * CR : half * CR + CR], jnp.clip(place + at, 0, 127))
            end = jnp.where((place >= 0) & (place < HALO), end, 0.0)
            csend[v, half] = jnp.sum(end, 0, keepdims=True)

    def slab_place(rr, f):
        n = rr * FIELDS + f
        return n // 18, HALO * (n % 9) + 64 * (n % 18 // 9)

    slabs = [jnp.zeros((CR, 128), jnp.float32)] * 3
    for rr in range(REFINE):
        for f in range(FIELDS):
            a, b = shares[rr] if f == SHARE else rows_of(f, rr)
            x = jnp.where(lane16 < HALO, a, jnp.where((lane16 >= 29) & (lane16 < 32), b, 0.0))
            n, at = slab_place(rr, f)
            slabs[n] = slabs[n] + (pltpu.roll(x, at, 1) if at else x)
    for n in range(3):
        hsend[n] = slabs[n]

    def sideways(n, j):
        return pltpu.make_async_remote_copy(
            src_ref=hsend,
            dst_ref=hrecv.at[n],
            send_sem=hs_sem.at[n],
            recv_sem=hr_sem.at[n],
            device_id=(mi, j),
            device_id_type=MESH,
        )

    @pl.when(has_left)
    def _():
        sideways(0, mj - 1).start()

    @pl.when(has_right)
    def _():
        sideways(1, mj + 1).start()

    for rr in range(REFINE):
        for f in range(SHARE):
            put(f, rr, halves(*rows_of(f, rr)))
        put(SHARE, rr, halves(*shares[rr]))

    def vertical(v, i):
        return pltpu.make_async_remote_copy(
            src_ref=vsend.at[v],
            dst_ref=vrecv.at[v],
            send_sem=vs_sem.at[v],
            recv_sem=vr_sem.at[v],
            device_id=(i, mj),
            device_id_type=MESH,
        )

    def corner(v, s, i, j):
        return pltpu.make_async_remote_copy(
            src_ref=csend.at[v, s],
            dst_ref=crecv.at[v, s],
            send_sem=cs_sem.at[v, s],
            recv_sem=cr_sem.at[v, s],
            device_id=(i, j),
            device_id_type=MESH,
        )

    incoming = 0
    for has, i, left, right, end in sides:
        incoming += has.astype(jnp.int32) + (has & left).astype(jnp.int32) + (has & right).astype(jnp.int32)
    incoming += nc * ((has_up & (mj == 0)).astype(jnp.int32) + (has_down & (mj == nc - 1)).astype(jnp.int32))

    @pl.when(jnp.logical_not(is_lead))
    def _():
        pl.semaphore_wait(barrier, incoming)

    @pl.when((mj == lead - 1) | (mj == lead + 1))
    def _():
        pl.semaphore_signal(relay_sem, inc=1, device_id=(mi, lead), device_id_type=MESH)

    @pl.when(is_lead)
    def _():
        pl.semaphore_wait(relay_sem, 2)

    @pl.when(first_up)
    def _():
        @pl.loop(0, nc)
        def _(k):
            piece(k, mi - 1, CR, zh_sem, zr_sem.at[1]).start()

    @pl.when(last_down)
    def _():
        @pl.loop(0, nc)
        def _(k):
            piece(k, mi + 1, CR + 1, zh_sem, zr_sem.at[2]).start()

    for v, (has, i, left, right, end) in enumerate(sides):

        @pl.when(has)
        def _(v=v, i=i):
            vertical(v, i).start()

        @pl.when(has & left)
        def _(v=v, i=i):
            corner(v, 0, i, mj - 1).start()

        @pl.when(has & right)
        def _(v=v, i=i):
            corner(v, 1, i, mj + 1).start()

    for v, (has, i, left, right, end) in enumerate(sides):

        @pl.when(jnp.logical_not(has))
        def _(v=v):
            vrecv[1 - v] = jnp.zeros(vrecv.shape[1:], jnp.float32)

        @pl.when(jnp.logical_not(has & left))
        def _(v=v):
            crecv[1 - v, 1] = jnp.zeros((1, 128), jnp.float32)

        @pl.when(jnp.logical_not(has & right))
        def _(v=v):
            crecv[1 - v, 0] = jnp.zeros((1, 128), jnp.float32)

    @pl.when(jnp.logical_not(has_right))
    def _():
        hrecv[0] = jnp.zeros(hrecv.shape[1:], jnp.float32)

    @pl.when(jnp.logical_not(has_left))
    def _():
        hrecv[1] = jnp.zeros(hrecv.shape[1:], jnp.float32)

    def widen(groups):
        n = groups[0].shape[0]
        column = jnp.minimum(tenth(iota((n, 128), 1) + 7), 9)
        wide = []
        for f in range(COARSE):
            at = 24 * (f % 5)
            wide.append([take(groups[f // 5], column + (at + 8 * half)) for half in range(2)])
        return wide

    def layers_of(wide):
        por_w = wide[1]
        liquid, ice_w, room, per_pore = [], [], [], []
        for k in range(LAYERS):
            depth = 1000.0 * thickness[k]
            liquid.append(wide[2 + k] * depth)
            ice_w.append(wide[2 + LAYERS + k] * depth)
            room.append((por_w - wide[2 + LAYERS + k]) * depth)
            per_pore.append((math.sqrt(layer_speed[k]) / depth) / por_w)
        return liquid, ice_w, room, per_pore

    row_pieces().wait_recv()

    def rows_at(group, slots):
        return jnp.concatenate([zrecv[n, :, 128 * group : 128 * group + 128] for n in slots], 0)

    wide = [jnp.concatenate(x, 0) for x in widen([rows_at(g, range(CR)) for g in range(2)])]
    excess_w = wide[0]
    liquid_w, ice_w, room, per_pore = layers_of(wide)
    for n, x in enumerate(ice_w + room + per_pore):
        coarse[n] = x

    @pl.when(has_right)
    def _():
        sideways(0, mj).wait_recv()

    @pl.when(has_left)
    def _():
        sideways(1, mj).wait_recv()

    in_left = lane16 < HALO
    in_right = (lane16 >= 83) & (lane16 < 83 + HALO)
    for rr in range(REFINE):
        for f in range(FIELDS):
            n, at = slab_place(rr, f)
            from_left = pltpu.roll(hrecv[1, n], (-29 - at) % 128, 1)
            from_right = pltpu.roll(hrecv[0, n], (83 - at) % 128, 1)
            ref, off = field(f)
            r = off + rr * ROWS
            ref[r : r + CR] = jnp.where(in_left, from_left, ref[r : r + CR])
            ref[r + CR : r + ROWS] = jnp.where(in_right, from_right, ref[r + CR : r + ROWS])

    END = ROWS * (REFINE + 1)
    up_of = functools.partial(pltpu.roll, shift=1, axis=0)
    down_of = functools.partial(pltpu.roll, shift=ROWS - 1, axis=0)
    dirs[:ROWS] = up_of(dirs[END - ROWS : END])
    dirs[END:] = down_of(dirs[ROWS : 2 * ROWS])

    def finish_wrap(b):
        for f in range(FIELDS):
            moving[b, f, :ROWS] = up_of(moving[b, f, END - ROWS : END])
            moving[b, f, END:] = down_of(moving[b, f, ROWS : 2 * ROWS])

    def main_in(b, r, c):
        masks = inflow_masks(*[dirs[pl.ds(r + n * ROWS, CR), :] for n in range(3)])
        arriving = [
            inflow(masks, *[moving[b, f, pl.ds(r + n * ROWS, CR), :] for n in range(3)])
            for f in range(FIELDS)
        ]
        left = [rest[f, pl.ds(r, CR), :] for f in range(FIELDS)]
        return settle(left, arriving, [coarse[LAYERS + k, c : c + CR] for k in range(LAYERS)])

    def main_out(b, r, c, h, liquid):
        move, left, chan = outflow(
            h,
            liquid,
            stat[ORATE, pl.ds(r, CR), :],
            stat[KIND, pl.ds(r, CR), :],
            stat[LRATE, pl.ds(r, CR), :],
            [coarse[k, c : c + CR] for k in range(LAYERS)],
            [coarse[2 * LAYERS + k, c : c + CR] for k in range(LAYERS)],
        )
        for f in range(FIELDS):
            moving[b, f, pl.ds(r + ROWS, CR), :] = move[f]
            rest[f, pl.ds(r, CR), :] = left[f]
        return chan

    def row_at(rr, c):
        return pl.multiple_of(rr * ROWS + c, CR)

    zero16 = jnp.zeros((CR, 128), jnp.float32)

    def first(rr, chan):
        out = []
        for n, c in enumerate((0, CR)):
            r = row_at(rr, c)
            h = excess_w[c : c + CR] * stat[SHARE, pl.ds(r, CR), :]
            out.append(chan[n] + main_out(0, r, c, h, [x[c : c + CR] for x in liquid_w]))
        return tuple(out)

    chan = lax.fori_loop(0, REFINE, first, (zero16, zero16), unroll=2)
    finish_wrap(0)

    for b in range(2):

        def middle(rr, chan, b=b):
            out = []
            for n, c in enumerate((0, CR)):
                r = row_at(rr, c)
                out.append(chan[n] + main_out(1 - b, r, c, *main_in(b, r, c)))
            return tuple(out)

        chan = lax.fori_loop(0, REFINE, middle, chan, unroll=2)
        finish_wrap(1 - b)

    def last(rr, sums):
        out = []
        for n, c in enumerate((0, CR)):
            h, liquid = main_in(0, row_at(rr, c), c)
            out.append(tuple(a + x for a, x in zip(sums[n], liquid + [h])))
        return tuple(out)

    sums = lax.fori_loop(0, REFINE, last, ((zero16,) * (LAYERS + 1),) * 2, unroll=2)

    row_p, col_p = iota((128, 128), 0), iota((128, 128), 1)
    inside = (row_p >= HALO) & (row_p < HALO + 80)
    to_block = jnp.where((tenth(row_p + 7) == col_p + 1) & inside, 1.0, 0.0).astype(jnp.bfloat16)
    scales = [0.01 / (1000.0 * x) for x in thickness] + [0.01, 0.01]
    blocks = [x * scales[n] for half in range(2) for n, x in enumerate(sums[half] + (chan[half],))]
    means = dot2(jnp.concatenate(blocks, 0), to_block)
    back = jnp.zeros((CR, 128), jnp.float32)
    for half in range(2):
        for n in range(LAYERS + 2):
            r = (half * (LAYERS + 2) + n) * CR
            at = 16 * n + 8 * half
            back = back + (pltpu.roll(means[r : r + CR], at, 1) if at else means[r : r + CR])
    for s in range(1, CR - 1):
        bsend[s] = back[s : s + 1]

    def answer(k, s):
        return pltpu.make_async_remote_copy(
            src_ref=bsend.at[k],
            dst_ref=brecv.at[s],
            send_sem=bs_sem,
            recv_sem=br_sem,
            device_id=(mi, k),
            device_id_type=MESH,
        )

    def answers():
        return pltpu.make_async_remote_copy(
            src_ref=bsend.at[: nc - 1],
            dst_ref=brecv.at[: nc - 1],
            send_sem=bs_sem,
            recv_sem=br_sem,
            device_id=(mi, mj),
            device_id_type=MESH,
        )

    for k in others(mj):

        @pl.when((k != 0) & (k != nc - 1))
        def _(k=k):
            answer(k, mj).start()

    for v, (has, i, left, right, end) in enumerate(sides):

        @pl.when(has)
        def _(v=v):
            vertical(1 - v, mi).wait_recv()

        @pl.when(has & left)
        def _(v=v):
            corner(1 - v, 1, mi, mj).wait_recv()

        @pl.when(has & right)
        def _(v=v):
            corner(1 - v, 0, mi, mj).wait_recv()

    @pl.when(has_down)
    def _():
        piece(0, mi, CR, zh_sem, zr_sem.at[1]).wait_recv()

    @pl.when(has_up)
    def _():
        piece(0, mi, CR + 1, zh_sem, zr_sem.at[2]).wait_recv()

    for v in range(2):
        for half, mine in enumerate((in_left, in_right)):
            index = jnp.clip(HALO * iota((CR, 128), 0) + lane16 - 83 * half, 0, 127)
            side = take(jnp.broadcast_to(crecv[v, 1 - half], (CR, 128)), index)
            vrecv[v, half] = jnp.where(mine, side, vrecv[v, half])
    for f in range(FIELDS):
        ref, off = field(f)
        for half in range(2):
            for v in range(2):
                r = (2 * v + half) * CR
                own = off + half * CR
                if v == 0:
                    own_rows = ref[pl.ds(own, REFINE, stride=ROWS), :]
                    next_rows = ref[pl.ds(own + 1, HALO, stride=ROWS), :]
                    at, near = r, r + HALO + REFINE
                else:
                    own_rows = ref[pl.ds(own + CR - 1, REFINE, stride=ROWS), :]
                    next_rows = ref[pl.ds(own + (REFINE - HALO) * ROWS + CR - 2, HALO, stride=ROWS), :]
                    at, near = r + HALO + REFINE, r
                sstat[f, r + HALO : r + HALO + REFINE] = own_rows
                sstat[f, near : near + HALO] = next_rows
                sstat[f, at : at + HALO] = vrecv[1 - v, half, HALO * f : HALO * f + HALO]
    sub8 = iota((8, 128), 0)

    def strip_rows(group):
        def row(n):
            return jnp.broadcast_to(zrecv[n, :, 128 * group : 128 * group + 128], (8, 128))

        return [
            jnp.where(sub8 < 3, row(CR + 1), row(0)),
            jnp.where(sub8 < 5, row(0), row(1)),
            jnp.where(sub8 < 3, row(CR - 2), row(CR - 1)),
            jnp.where(sub8 < 5, row(CR - 1), row(CR)),
        ]

    groups = [jnp.concatenate(strip_rows(g), 0) for g in range(2)]
    wide = [jnp.concatenate([a[:CR], b[:CR], a[CR:], b[CR:]], 0) for a, b in widen(groups)]
    excess_w = wide[0]
    liquid, ice_w, room, per_pore = layers_of(wide)
    for n, x in enumerate(ice_w + room + per_pore):
        scoarse[n] = x
    sdir = sstat[DIR]
    sub_up = functools.partial(pltpu.roll, shift=1, axis=0)
    sub_down = functools.partial(pltpu.roll, shift=4 * CR - 1, axis=0)
    masks = inflow_masks(sub_up(sdir), sdir, sub_down(sdir))
    h = excess_w * sstat[SHARE]
    chan = jnp.zeros((4 * CR, 128), jnp.float32)
    for step in range(3):
        move, left, taken = outflow(
            h,
            liquid,
            sstat[ORATE],
            sstat[KIND],
            sstat[LRATE],
            [scoarse[k] for k in range(LAYERS)],
            [scoarse[2 * LAYERS + k] for k in range(LAYERS)],
        )
        chan = chan + taken
        arriving = [inflow(masks, sub_up(m), m, sub_down(m)) for m in move]
        h, liquid = settle(left, arriving, [scoarse[LAYERS + k] for k in range(LAYERS)])

    sub16 = iota((CR, 128), 0)
    of_row = (sub16 >= HALO) & (sub16 < HALO + REFINE)
    sums = []
    for v in range(2):
        for n, x in enumerate(liquid + [h, chan]):
            for half in range(2):
                r = (2 * v + half) * CR
                sums.append(jnp.sum(jnp.where(of_row, x[r : r + CR], 0.0), 0, keepdims=True) * scales[n])
        sums.append(jnp.zeros((4, 128), jnp.float32))
    means = dot2(jnp.concatenate(sums, 0), to_block)
    for v in range(2):
        x = pltpu.roll(means[v * CR : (v + 1) * CR], 0, 1, stride=8, stride_axis=0)
        bsend[v * (CR - 1)] = jnp.sum(x, 0, keepdims=True)

    for k in (0, nc - 1):

        @pl.when(mj != k)
        def _(k=k):
            answer(k, mj).start()

    brecv[mj] = bsend[mj]

    row_pieces().wait_send()

    @pl.when(first_up | last_down)
    def _():
        pltpu.make_async_remote_copy(
            src_ref=zsend,
            dst_ref=zrecv.at[:nc],
            send_sem=zh_sem,
            recv_sem=zr_sem.at[1],
            device_id=(mi, mj),
            device_id_type=MESH,
        ).wait_send()

    for v, (has, i, left, right, end) in enumerate(sides):

        @pl.when(has)
        def _(v=v, i=i):
            vertical(v, i).wait_send()

        @pl.when(has & left)
        def _(v=v, i=i):
            corner(v, 0, i, mj - 1).wait_send()

        @pl.when(has & right)
        def _(v=v, i=i):
            corner(v, 1, i, mj + 1).wait_send()

    @pl.when(has_left)
    def _():
        sideways(0, mj - 1).wait_send()

    @pl.when(has_right)
    def _():
        sideways(1, mj + 1).wait_send()

    answers().wait_recv()

    gather = jnp.minimum(iota((8, 128), 0) * 16 + (lane & 15), 127)
    owner = lax.shift_right_logical(lane, 4)
    for half in range(2):
        out = jnp.zeros((8, 128), jnp.float32)
        for s in range(8):
            x = jnp.broadcast_to(brecv[8 * half + s], (8, 128))
            out = jnp.where(owner == s, take(x, gather), out)
        lanes = slice(128 * half, 128 * half + 128)
        for k in range(LAYERS):
            out_liq[k, :, lanes] = out[k : k + 1]
        out_h[:, lanes] = out[LAYERS : LAYERS + 1]
        out_c[:, lanes] = out[LAYERS + 1 : LAYERS + 2]

    answers().wait_send()


def store(a, b, c, out_a, out_b, out_c, sem):
    copies = [
        pltpu.make_async_copy(src, dst, sem.at[n])
        for n, (src, dst) in enumerate(((a, out_a), (b, out_b), (c, out_c)))
    ]
    for copy in copies:
        copy.start()
    for copy in copies:
        copy.wait()


def solution(mesh):
    nr, nc = mesh.shape["rows"], mesh.shape["cols"]
    f32, bf16 = jnp.float32, jnp.bfloat16

    def step(*args):
        v = pltpu.VMEM
        dma = pltpu.SemaphoreType.DMA
        args = [pltpu.with_memory_space_constraint(x, pltpu.HBM) for x in args]
        results = pl.pallas_call(
            functools.partial(kernel, nr, nc),
            out_shape=(v((LAYERS, 1, W), f32), v((1, W), f32), v((1, W), f32)),
            in_specs=[pl.BlockSpec(memory_space=pltpu.HBM)] * 10,
            out_specs=[pl.BlockSpec(memory_space=pltpu.VMEM)] * 3,
            scratch_shapes=[
                v((1, W), f32),
                v((1, W), f32),
                v((1, W), f32),
                v((LAYERS, 1, W), f32),
                v((LAYERS, 1, W), f32),
                v((TILE, TILE), jnp.int32),
                v((TILE, TILE), jnp.int32),
                v((TILE, TILE), bf16),
                v((TILE, TILE), bf16),
                v((TILE, TILE), bf16),
                v((2 * FIELDS, TILE, 128), f32),
                v((FIELDS, 2 * TILE, 128), f32),
                v((2 * TILE + 2 * ROWS, 128), f32),
                v((3 * LAYERS, ROWS, 128), f32),
                v((2, FIELDS, 2 * TILE + 2 * ROWS, 128), f32),
                v((FIELDS, 2 * TILE, 128), f32),
                v((FIELDS, 4 * CR, 128), f32),
                v((3 * LAYERS, 4 * CR, 128), f32),
                v((CR, 1, W), f32),
                v((CR + 2, 1, W), f32),
                v((2, 2, CR, 128), f32),
                v((2, 2, CR, 128), f32),
                v((2, 2, 1, 128), f32),
                v((2, 2, 1, 128), f32),
                v((3, CR, 128), f32),
                v((2, 3, CR, 128), f32),
                v((CR, 1, 128), f32),
                v((CR, 1, 128), f32),
                dma((10,)),
                dma(()),
                dma(()),
                dma((3,)),
                dma((2,)),
                dma((2,)),
                dma((2, 2)),
                dma((2, 2)),
                dma((2,)),
                dma((2,)),
                dma(()),
                dma(()),
                pltpu.SemaphoreType.REGULAR,
                pltpu.SemaphoreType.REGULAR,
            ],
            compiler_params=pltpu.CompilerParams(
                collective_id=0, has_side_effects=True, vmem_limit_bytes=62 * 1024 * 1024
            ),
        )(*args)
        return pl.pallas_call(
            store,
            out_shape=(
                jax.ShapeDtypeStruct((LAYERS, 1, W), f32),
                jax.ShapeDtypeStruct((1, W), f32),
                jax.ShapeDtypeStruct((1, W), f32),
            ),
            in_specs=[pl.BlockSpec(memory_space=pltpu.VMEM)] * 3,
            out_specs=[pl.BlockSpec(memory_space=pltpu.HBM)] * 3,
            scratch_shapes=[dma((3,))],
        )(*[pltpu.with_memory_space_constraint(x, pltpu.VMEM) for x in results])

    return jax.shard_map(
        step,
        mesh=mesh,
        in_specs=(
            P(("rows", "cols"), None),
            P(("rows", "cols"), None),
            P(("rows", "cols"), None),
            P(None, ("rows", "cols"), None),
            P(None, ("rows", "cols"), None),
            P("rows", "cols"),
            P("rows", "cols"),
            P("rows", "cols"),
            P("rows", "cols"),
            P("rows", "cols"),
        ),
        out_specs=(
            P(None, ("rows", "cols"), None),
            P(("rows", "cols"), None),
            P(("rows", "cols"), None),
        ),
        check_vma=False,
    )
```

```python
import functools
import math

import jax
import jax.numpy as jnp
from jax import lax
from jax.experimental import pallas as pl
from jax.experimental.pallas import tpu as pltpu
from jax.sharding import PartitionSpec as P

MESH = pl.DeviceIdType.MESH
REFINE = 10
LAYERS = 4
TILE = 160
CR = 16
W = 256
HALO = 3
PAIRS = REFINE // 2
ROWS = 3 * CR
SPLIT = 56

thickness = (0.1, 0.3, 0.6, 1.0)
layer_speed = (1.0, 0.8, 0.6, 0.4)

DIR, ORATE, LAND, LRATE, SHARE, CHANNEL = range(6)
FIELDS = 5
COARSE = 10


FAR_FIRST = sorted(
    ((z, y, c) for z in range(2) for y in range(4) for c in range(2) if z + y + c),
    key=lambda p: -(p[0] + min(p[1], 4 - p[1])),
)


def others(j):
    z, y, c = j // 8, (j // 2) % 4, j % 2
    return [((z + dz) % 2) * 8 + ((y + dy) % 4) * 2 + (c + dc) % 2 for dz, dy, dc in FAR_FIRST]


def iota(shape, dim):
    return lax.broadcasted_iota(jnp.int32, shape, dim)


def take(x, index):
    return jnp.take_along_axis(x, index, axis=1, mode="promise_in_bounds")


def tenth(x):
    return lax.shift_right_logical(x * 6554, 16)


def split3(x):
    hi = x.astype(jnp.bfloat16)
    r = x - hi.astype(jnp.float32)
    mid = r.astype(jnp.bfloat16)
    lo = (r - mid.astype(jnp.float32)).astype(jnp.bfloat16)
    return jnp.concatenate([hi, mid, lo], 0)


def split2(x):
    hi = x.astype(jnp.bfloat16)
    lo = (x - hi.astype(jnp.float32)).astype(jnp.bfloat16)
    return jnp.concatenate([hi, lo], 0)


def dot3(x, ones):
    n = x.shape[0]
    y = jnp.dot(split3(x), ones, preferred_element_type=jnp.float32)
    return y[:n] + y[n : 2 * n] + y[2 * n :]


def dot2(x, ones):
    n = x.shape[0]
    y = jnp.dot(split2(x), ones, preferred_element_type=jnp.float32)
    return y[:n] + y[n:]


def inflow_masks(d_up, d_mid, d_down):
    return (
        d_up == 1.0,
        d_mid == 0.0,
        d_down == 7.0,
        d_up == 3.0,
        d_mid == 4.0,
        d_down == 5.0,
        d_up == 2.0,
        d_down == 6.0,
    )


def inflow(masks, up, mid, down):
    e0, e1, e2, w0, w1, w2, s0, s1 = masks
    zero = jnp.zeros_like(up)
    east = jnp.where(e0, up, zero) + jnp.where(e1, mid, zero) + jnp.where(e2, down, zero)
    west = jnp.where(w0, up, zero) + jnp.where(w1, mid, zero) + jnp.where(w2, down, zero)
    same = jnp.where(s0, up, zero) + jnp.where(s1, down, zero)
    return same + pltpu.roll(east, 1, 1) + pltpu.roll(west, 127, 1)


def outflow(h, liquid, orate, land, channel, lrate, ice, per_pore):
    q = orate * h * (h / (h + 2.0))
    moving = [q * land]
    rest = [h - q]
    for k in range(LAYERS):
        sat = jnp.minimum((liquid[k] + ice[k]) * per_pore[k], math.sqrt(layer_speed[k]))
        lateral = (lrate * liquid[k]) * (sat * sat)
        moving.append(lateral)
        rest.append(liquid[k] - lateral)
    return moving, rest, q * channel


def settle(rest, arriving, room):
    h = rest[0] + arriving[0]
    liquid = []
    for k in range(LAYERS):
        u = rest[1 + k] + arriving[1 + k]
        h = h + jnp.maximum(u - room[k], 0.0)
        liquid.append(jnp.minimum(u, room[k]))
    return h, liquid


def kernel(
    nr,
    nc,
    rain_h,
    infil_h,
    por_h,
    liq_h,
    ice_h,
    dir_h,
    kind_h,
    orate_h,
    lrate_h,
    weight_h,
    out_liq,
    out_h,
    out_c,
    rain,
    infil,
    por,
    liq,
    ice,
    dir_v,
    kind_v,
    orate_v,
    lrate_v,
    weight_v,
    nat,
    share_v,
    stat,
    dirs,
    coarse,
    moving,
    rest,
    sums,
    sstat,
    schannel,
    enter,
    zsend,
    zrecv,
    vsend,
    vrecv,
    csend,
    crecv,
    hsend,
    hrecv,
    bsend,
    brecv,
    in_sem,
    zs_sem,
    zh_sem,
    zr_sem,
    vs_sem,
    vr_sem,
    cs_sem,
    cr_sem,
    hs_sem,
    hr_sem,
    bs_sem,
    br_sem,
    row_sem,
    relay_sem,
):
    mi = lax.axis_index("rows")
    mj = lax.axis_index("cols")
    has_up, has_down = mi > 0, mi < nr - 1
    has_left, has_right = mj > 0, mj < nc - 1

    barrier = pltpu.get_barrier_semaphore()
    lead = nc - 2
    is_lead = mj == lead

    def tell(i, j):
        pl.semaphore_signal(barrier, inc=1, device_id=(i, j), device_id_type=MESH)

    @pl.when(jnp.logical_not(is_lead))
    def _():
        tell(mi, lead)

    copies = [
        pltpu.make_async_copy(src, dst, in_sem.at[n])
        for n, (src, dst) in enumerate(
            (
                (rain_h, rain),
                (infil_h, infil),
                (por_h, por),
                (liq_h, liq),
                (ice_h, ice),
                (weight_h, weight_v),
                (dir_h, dir_v),
                (kind_h, kind_v),
                (orate_h, orate_v),
                (lrate_h, lrate_v),
            )
        )
    ]
    for copy in copies:
        copy.start()

    sides = (
        (has_up, mi - 1, has_left, has_right, nc - 1),
        (has_down, mi + 1, has_left, has_right, 0),
    )
    for has, i, left, right, end in sides:

        @pl.when(has)
        def _(i=i, end=end):
            tell(i, end)

        @pl.when(has & jnp.logical_not(is_lead))
        def _(i=i):
            tell(i, mj)

        @pl.when(has & left & (mj - 1 != lead))
        def _(i=i):
            tell(i, mj - 1)

        @pl.when(has & right & (mj + 1 != lead))
        def _(i=i):
            tell(i, mj + 1)

    @pl.when(is_lead)
    def _():
        pl.semaphore_wait(barrier, nc - 1)
        for k in range(nc):
            if k != lead:
                pl.semaphore_signal(row_sem, inc=1, device_id=(mi, k), device_id_type=MESH)

    lane = iota((8, 128), 1)
    lane16 = iota((CR, 128), 1)
    sub16 = iota((CR, 128), 0)

    def piece(k, i, s, send, arrive):
        return pltpu.make_async_remote_copy(
            src_ref=zsend.at[k],
            dst_ref=zrecv.at[s],
            send_sem=send,
            recv_sem=arrive,
            device_id=(i, k),
            device_id_type=MESH,
        )

    def row_pieces():
        return pltpu.make_async_remote_copy(
            src_ref=zsend.at[: nc - 1],
            dst_ref=zrecv.at[: nc - 1],
            send_sem=zs_sem,
            recv_sem=zr_sem.at[0],
            device_id=(mi, mj),
            device_id_type=MESH,
        )

    first_up = has_up & (mj == 0)
    last_down = has_down & (mj == nc - 1)

    def first_run(a):
        return pltpu.roll(a, HALO, 1)

    def second_run(a, b):
        return jnp.where(lane16 < 21, pltpu.roll(a, 21, 1), pltpu.roll(b, 21, 1))

    def third_run(a):
        return pltpu.roll(a, 59, 1)

    def fourth_run(a, b):
        return jnp.where(lane16 < 81, pltpu.roll(a, 81, 1), pltpu.roll(b, 81, 1))

    def rows_of(f, rr):
        return [nat.at[2 * f + half][pl.ds(rr, CR, stride=REFINE), :] for half in range(2)]

    def field(f):
        return (dirs, ROWS) if f == DIR else (stat.at[f], 0)

    def vertical(v, i):
        return pltpu.make_async_remote_copy(
            src_ref=vsend.at[v],
            dst_ref=vrecv.at[v],
            send_sem=vs_sem.at[v],
            recv_sem=vr_sem.at[v],
            device_id=(i, mj),
            device_id_type=MESH,
        )

    def corner(v, s, i, j):
        return pltpu.make_async_remote_copy(
            src_ref=csend.at[v, s],
            dst_ref=crecv.at[v, s],
            send_sem=cs_sem.at[v, s],
            recv_sem=cr_sem.at[v, s],
            device_id=(i, j),
            device_id_type=MESH,
        )

    incoming = 0
    for has, i, left, right, end in sides:
        incoming += has.astype(jnp.int32) + (has & left).astype(jnp.int32) + (has & right).astype(jnp.int32)
    incoming += nc * ((has_up & (mj == 0)).astype(jnp.int32) + (has_down & (mj == nc - 1)).astype(jnp.int32))

    def rows_ready():
        @pl.when(jnp.logical_not(is_lead))
        def _():
            pl.semaphore_wait(barrier, incoming)

        @pl.when((mj == lead - 1) | (mj == lead + 1))
        def _():
            pl.semaphore_signal(relay_sem, inc=1, device_id=(mi, lead), device_id_type=MESH)

        @pl.when(is_lead)
        def _():
            pl.semaphore_wait(relay_sem, 2)

    def send_ends():
        @pl.when(first_up)
        def _():
            @pl.loop(0, nc)
            def _(k):
                piece(k, mi - 1, CR, zh_sem, zr_sem.at[1]).start()

        @pl.when(last_down)
        def _():
            @pl.loop(0, nc)
            def _(k):
                piece(k, mi + 1, CR + 1, zh_sem, zr_sem.at[2]).start()

    def send_rows():
        for v, (has, i, left, right, end) in enumerate(sides):

            @pl.when(has)
            def _(v=v, i=i):
                vertical(v, i).start()

            @pl.when(has & left)
            def _(v=v, i=i):
                corner(v, 0, i, mj - 1).start()

            @pl.when(has & right)
            def _(v=v, i=i):
                corner(v, 1, i, mj + 1).start()

    def coarse_part():
        for copy in copies[:5]:
            copy.wait()
        rain_x, por_x = rain[...], por[...]
        top_sat = (liq[0] + ice[0]) / por_x
        capacity = infil[...] * jnp.maximum(1.0 - top_sat, 0.1)
        excess = rain_x * rain_x / (rain_x + capacity)
        top = liq[0] + (rain_x - excess) / (1000.0 * thickness[0])
        strip = [excess, por_x, top] + [liq[k] for k in range(1, LAYERS)] + [ice[k] for k in range(LAYERS)]

        slot = lax.shift_right_logical(lane * 2731, 16)
        t = lane - slot * 24
        for half in range(2):
            base = (iota((8, 128), 0) + 8 * half) * 16 - 1 + t
            inside = jnp.clip(base, 0, W - 1)
            index = inside & 127
            low = inside < 128
            for group in range(2):
                packed = jnp.zeros((8, 128), jnp.float32)
                for n in range(5):
                    x = strip[group * 5 + n]
                    a = jnp.broadcast_to(x[:, :128], (8, 128))
                    b = jnp.broadcast_to(x[:, 128:], (8, 128))
                    packed = jnp.where(slot == n, jnp.where(low, take(a, index), take(b, index)), packed)
                for s in range(8):
                    zsend[8 * half + s, :, 128 * group : 128 * group + 128] = packed[s : s + 1]

        zrecv[mj] = zsend[mj]

        @pl.when(jnp.logical_not(has_down))
        def _():
            zrecv[CR] = zsend[mj]

        @pl.when(jnp.logical_not(has_up))
        def _():
            zrecv[CR + 1] = zsend[mj]

    def tile_part():
        for copy in copies[5:]:
            copy.wait()
        kind_x = kind_v[...]
        natural = (
            dir_v[...].astype(jnp.float32),
            jnp.where(kind_x == 2, 0.0, orate_v[...].astype(jnp.float32)),
            jnp.where(kind_x == 0, 1.0, 0.0),
            lrate_v[...].astype(jnp.float32),
            weight_v[...].astype(jnp.float32),
            jnp.where(kind_x == 1, 1.0, 0.0),
        )
        no_lanes = jnp.zeros((TILE, 96), jnp.float32)
        for f in range(FIELDS + 1):
            nat[2 * f] = natural[f][:, :128]
            nat[2 * f + 1] = jnp.concatenate([natural[f][:, 128:], no_lanes], 1)

        weights = [rows_of(SHARE, rr) for rr in range(REFINE)]
        total = [functools.reduce(lambda a, b: a + b, [w[half] for w in weights]) for half in range(2)]
        row_c, col_c = iota((W, W), 0), iota((W, W), 1)
        same_block = (tenth(row_c) == tenth(col_c)) & (row_c < TILE) & (col_c < TILE)
        block_sum = dot3(jnp.concatenate(total, 1), jnp.where(same_block, 1.0, 0.0).astype(jnp.bfloat16))
        per_mean = 100.0 / jnp.where(iota((CR, W), 1) < TILE, block_sum, 1.0)
        shares = [[w[half] * per_mean[:, 128 * half : 128 * half + 128] for half in range(2)] for w in weights]
        for rr in range(REFINE):
            for half in range(2):
                share_v[2 * rr + half] = shares[rr][half]

        place = lane16 - HALO * sub16
        for v in range(2):
            r = v * (TILE - HALO)
            for half in range(2):
                for f in range(SHARE):
                    vsend[v, half, HALO * f : HALO * f + HALO] = nat[2 * f + half, r : r + HALO]
                for p in range(HALO):
                    x = shares[p + v * (REFINE - HALO)][half][v * (CR - 1) : v * (CR - 1) + 1]
                    vsend[v, half, HALO * SHARE + p : HALO * SHARE + p + 1] = x
                vsend[v, half, HALO * FIELDS :] = jnp.zeros((1, 128), jnp.float32)
            a, b = vsend[v, 0], vsend[v, 1]
            if v == 0:
                vsend[v, 0], vsend[v, 1] = third_run(a), fourth_run(a, b)
            else:
                vsend[v, 0], vsend[v, 1] = first_run(a), second_run(a, b)
            for n, (x, at) in enumerate(((a, 0), (b, 29))):
                end = jnp.where((place >= 0) & (place < HALO), take(x, jnp.clip(place + at, 0, 127)), 0.0)
                csend[v, n] = jnp.sum(end, 0, keepdims=True)

    late = (lax.rem(mi, 4) == 3) & has_down
    late_first = late.astype(jnp.int32)

    @pl.loop(0, 2)
    def _(phase):
        part = lax.rem(phase + late_first, 2)

        @pl.when(part == 0)
        def _():
            coarse_part()

        @pl.when(part == 1)
        def _():
            tile_part()

        @pl.when((phase == 0) & jnp.logical_not(is_lead))
        def _():
            pl.semaphore_wait(row_sem, 1)

        @pl.when(part == 0)
        def _():
            for k in others(mj):
                piece(k, mi, mj, zs_sem, zr_sem.at[0]).start()

        @pl.when((part == 1) & late)
        def _():
            rows_ready()
            send_rows()

    @pl.when(late)
    def _():
        send_ends()

    shares = [[share_v[2 * rr + half] for half in range(2)] for rr in range(REFINE)]

    def slab_place(rr, f):
        n = rr * FIELDS + f
        return n // 18, HALO * (n % 9) + 64 * (n % 18 // 9)

    slabs = [jnp.zeros((CR, 128), jnp.float32)] * 3
    for rr in range(REFINE):
        for f in range(FIELDS):
            a, b = shares[rr] if f == SHARE else rows_of(f, rr)
            x = jnp.where(lane16 < HALO, a, jnp.where((lane16 >= 29) & (lane16 < 32), b, 0.0))
            n, at = slab_place(rr, f)
            slabs[n] = slabs[n] + (pltpu.roll(x, at, 1) if at else x)
    for n in range(3):
        hsend[n] = slabs[n]

    def sideways(n, j):
        return pltpu.make_async_remote_copy(
            src_ref=hsend,
            dst_ref=hrecv.at[n],
            send_sem=hs_sem.at[n],
            recv_sem=hr_sem.at[n],
            device_id=(mi, j),
            device_id_type=MESH,
        )

    @pl.when(has_left)
    def _():
        sideways(0, mj - 1).start()

    @pl.when(has_right)
    def _():
        sideways(1, mj + 1).start()

    for p in range(PAIRS):
        for f in range(FIELDS + 1):
            if f == SHARE:
                (a, b), (c, d) = shares[p], shares[p + PAIRS]
            else:
                (a, b), (c, d) = rows_of(f, p), rows_of(f, p + PAIRS)
            ref, off = field(f)
            r = off + p * ROWS
            ref[r : r + CR] = first_run(a)
            ref[r + CR : r + 2 * CR] = jnp.where(lane16 < SPLIT, second_run(a, b), third_run(c))
            ref[r + 2 * CR : r + ROWS] = fourth_run(c, d)

    def strip_own(f, v, out):
        ref, off = field(f)
        for half in range(2):
            at = 8 * half + (0 if v else HALO)
            r = off + (v + half) * CR + v * (CR - 1)
            out[at : at + PAIRS] = ref[pl.ds(r, PAIRS, stride=ROWS), :]

    lane8, sub8 = iota((8, 128), 1), iota((8, 128), 0)
    schannel[...] = jnp.zeros(schannel.shape, jnp.float32)
    for v in range(2):
        strip_own(CHANNEL, v, schannel.at[v])

    row48, lane48 = iota((ROWS, 128), 0), iota((ROWS, 128), 1)
    in_first = (row48 == 0) | ((row48 == CR) & (lane48 < SPLIT))
    in_last = (row48 == ROWS - 1) | ((row48 == 2 * CR - 1) & (lane48 >= SPLIT))
    for p in range(PAIRS):
        out = in_first if p < 2 else in_last if p > 2 else in_first | in_last
        r = p * ROWS
        stat[CHANNEL, r : r + ROWS] = jnp.where(out, 0.0, stat[CHANNEL, r : r + ROWS])

    @pl.when(jnp.logical_not(late))
    def _():
        rows_ready()
        send_ends()
        send_rows()

    for v, (has, i, left, right, end) in enumerate(sides):

        @pl.when(jnp.logical_not(has))
        def _(v=v):
            vrecv[1 - v] = jnp.zeros(vrecv.shape[1:], jnp.float32)

        @pl.when(jnp.logical_not(has & left))
        def _(v=v):
            crecv[1 - v, 1] = jnp.zeros((1, 128), jnp.float32)

        @pl.when(jnp.logical_not(has & right))
        def _(v=v):
            crecv[1 - v, 0] = jnp.zeros((1, 128), jnp.float32)

    @pl.when(jnp.logical_not(has_right))
    def _():
        hrecv[0] = jnp.zeros(hrecv.shape[1:], jnp.float32)

    @pl.when(jnp.logical_not(has_left))
    def _():
        hrecv[1] = jnp.zeros(hrecv.shape[1:], jnp.float32)

    def columns(n):
        lanes = iota((n, 128), 1)
        return (
            tenth(lanes + 7),
            tenth(jnp.where(lanes < SPLIT, lanes + 117, lanes - 49)),
            jnp.minimum(tenth(lanes + 57), 17),
        )

    def layers_of(wide):
        por_w = wide[1]
        liquid, ice_w, room, per_pore = [], [], [], []
        for k in range(LAYERS):
            depth = 1000.0 * thickness[k]
            liquid.append(wide[2 + k] * depth)
            ice_w.append(wide[2 + LAYERS + k] * depth)
            room.append((por_w - wide[2 + LAYERS + k]) * depth)
            per_pore.append((math.sqrt(layer_speed[k]) / depth) / por_w)
        return liquid, ice_w, room, per_pore

    row_pieces().wait_recv()

    def rows_at(group, slots):
        return jnp.concatenate([zrecv[n, :, 128 * group : 128 * group + 128] for n in slots], 0)

    packed_rows = [rows_at(g, range(CR)) for g in range(2)]
    wide = [
        jnp.concatenate([take(packed_rows[f // 5], c + 24 * (f % 5)) for c in columns(CR)], 0) for f in range(COARSE)
    ]
    liquid_w, ice_w, room, per_pore = layers_of(wide)
    for n, x in enumerate(ice_w + room + per_pore + liquid_w + wide[:1]):
        coarse[n] = x

    @pl.when(has_right)
    def _():
        sideways(0, mj).wait_recv()

    @pl.when(has_left)
    def _():
        sideways(1, mj).wait_recv()

    def span(at):
        return (lane16 >= at) & (lane16 < at + HALO)

    for p in range(PAIRS):
        for f in range(FIELDS):
            ref, off = field(f)
            r = off + p * ROWS
            for rr, (left_row, left_at), (right_row, right_at) in (
                (p, (r, 0), (r + CR, SPLIT - HALO)),
                (p + PAIRS, (r + CR, SPLIT), (r + 2 * CR, 113)),
            ):
                n, at = slab_place(rr, f)
                from_left = pltpu.roll(hrecv[1, n], (left_at - 29 - at) % 128, 1)
                from_right = pltpu.roll(hrecv[0, n], (right_at - at) % 128, 1)
                ref[left_row : left_row + CR] = jnp.where(
                    span(left_at), from_left, ref[left_row : left_row + CR]
                )
                ref[right_row : right_row + CR] = jnp.where(
                    span(right_at), from_right, ref[right_row : right_row + CR]
                )

    END = ROWS * (PAIRS + 1)
    sub_up = functools.partial(pltpu.roll, shift=1, axis=0)

    def sub_down(x):
        return pltpu.roll(x, x.shape[0] - 1, 0)

    def across(x):
        x0, x1, x2 = x[:CR], x[CR : 2 * CR], x[2 * CR :]
        return (
            jnp.where(lane16 < 53, pltpu.roll(x1, 72, 1), pltpu.roll(x2, 50, 1)),
            pltpu.roll(x2, 68, 1),
            pltpu.roll(x0, SPLIT, 1),
            jnp.where(lane16 < 63, pltpu.roll(x0, 78, 1), pltpu.roll(x1, 60, 1)),
        )

    def wrap(ref):
        a, b, c, d = across(ref[END - ROWS : END])
        ref[:CR] = sub_up(a)
        ref[CR : 2 * CR] = jnp.where(lane16 < SPLIT, sub_up(b), c)
        ref[2 * CR : ROWS] = d
        a, b, c, d = across(ref[ROWS : 2 * ROWS])
        ref[END : END + CR] = a
        ref[END + CR : END + 2 * CR] = jnp.where(lane16 < SPLIT, b, sub_down(c))
        ref[END + 2 * CR :] = sub_down(d)

    wrap(dirs)

    def finish(b, step):
        top, bottom = ROWS + HALO * ROWS, ROWS + ROWS + CR - 1
        for f in range(FIELDS):
            wrap(moving.at[b, f])
            enter[step, 0, f, 6:7] = moving[b, f, top : top + 1]
            enter[step, 0, f, 14:15] = moving[b, f, top + CR : top + CR + 1]
            enter[step, 1, f, 1:2] = moving[b, f, bottom + CR : bottom + CR + 1]
            enter[step, 1, f, 9:10] = moving[b, f, bottom + 2 * CR : bottom + 2 * CR + 1]

    def main_in(b, r, c):
        masks = inflow_masks(*[dirs[pl.ds(r + n * ROWS, CR), :] for n in range(3)])
        arriving = [
            inflow(masks, *[moving[b, f, pl.ds(r + n * ROWS, CR), :] for n in range(3)])
            for f in range(FIELDS)
        ]
        left = [rest[f, pl.ds(r, CR), :] for f in range(FIELDS)]
        return settle(left, arriving, [coarse[LAYERS + k, c : c + CR] for k in range(LAYERS)])

    def main_out(b, r, c, h, liquid):
        move, left, taken = outflow(
            h,
            liquid,
            stat[ORATE, pl.ds(r, CR), :],
            stat[LAND, pl.ds(r, CR), :],
            stat[CHANNEL, pl.ds(r, CR), :],
            stat[LRATE, pl.ds(r, CR), :],
            [coarse[k, c : c + CR] for k in range(LAYERS)],
            [coarse[2 * LAYERS + k, c : c + CR] for k in range(LAYERS)],
        )
        for f in range(FIELDS):
            moving[b, f, pl.ds(r + ROWS, CR), :] = move[f]
            rest[f, pl.ds(r, CR), :] = left[f]
        sums[LAYERS + 1, c : c + CR] += taken

    def row_at(p, c):
        return pl.multiple_of(p * ROWS + c, CR)

    sums[...] = jnp.zeros(sums.shape, jnp.float32)

    @pl.loop(0, PAIRS, unroll=True)
    def _(p):
        for c in range(0, ROWS, CR):
            r = row_at(p, c)
            h = coarse[4 * LAYERS, c : c + CR] * stat[SHARE, pl.ds(r, CR), :]
            main_out(0, r, c, h, [coarse[3 * LAYERS + k, c : c + CR] for k in range(LAYERS)])

    finish(0, 0)

    for b in range(2):

        @pl.loop(0, PAIRS, unroll=True)
        def _(p, b=b):
            for c in range(0, ROWS, CR):
                r = row_at(p, c)
                main_out(1 - b, r, c, *main_in(b, r, c))

        finish(1 - b, 1 + b)

    since = jnp.where(in_first, HALO, 0)
    until = jnp.where(in_last, PAIRS - HALO, PAIRS)

    @pl.loop(0, PAIRS, unroll=True)
    def _(p):
        for c in range(0, ROWS, CR):
            h, liquid = main_in(0, row_at(p, c), c)
            keep = (since[c : c + CR] <= p) & (until[c : c + CR] > p)
            for n, x in enumerate(liquid + [h]):
                sums[n, c : c + CR] += jnp.where(keep, x, 0.0)

    row_p, col_p = iota((128, 128), 0), iota((128, 128), 1)
    to_block = []
    for at, end, shift in ((3, 113, 0), (3, 53, 11), (3, 113, 5)):
        mine = (row_p >= at) & (row_p < end) & (tenth(row_p + 7) == col_p + 1 - shift)
        if shift == 11:
            mine = mine | ((row_p >= 59) & (row_p < 109) & (tenth(row_p - 49) == col_p + 1))
        to_block.append(jnp.where(mine, 1.0, 0.0).astype(jnp.bfloat16))
    to_block = jnp.concatenate(to_block, 0)
    scales = [0.01 / (1000.0 * x) for x in thickness] + [0.01, 0.01]

    def three(n):
        return jnp.concatenate([sums[n, c : c + CR] for c in range(0, ROWS, CR)], 1) * scales[n]

    means = dot2(jnp.concatenate([three(n) for n in range(LAYERS + 2)], 0), to_block)
    back = means[:CR]
    for n in range(1, LAYERS + 2):
        back = back + pltpu.roll(means[n * CR : (n + 1) * CR], 16 * n, 1)
    for s in range(1, CR - 1):
        bsend[s] = back[s : s + 1]

    def answer(k, s):
        return pltpu.make_async_remote_copy(
            src_ref=bsend.at[k],
            dst_ref=brecv.at[s],
            send_sem=bs_sem,
            recv_sem=br_sem,
            device_id=(mi, k),
            device_id_type=MESH,
        )

    def answers():
        return pltpu.make_async_remote_copy(
            src_ref=bsend.at[: nc - 1],
            dst_ref=brecv.at[: nc - 1],
            send_sem=bs_sem,
            recv_sem=br_sem,
            device_id=(mi, mj),
            device_id_type=MESH,
        )

    for k in others(mj):

        @pl.when((k != 0) & (k != nc - 1))
        def _(k=k):
            answer(k, mj).start()

    def strip(v):
        has, _, left, right, _ = sides[v]

        @pl.when(has)
        def _():
            vertical(1 - v, mi).wait_recv()
            piece(0, mi, CR + 1 - v, zh_sem, zr_sem.at[2 - v]).wait_recv()

        @pl.when(has & left)
        def _():
            corner(1 - v, 1, mi, mj).wait_recv()

        @pl.when(has & right)
        def _():
            corner(1 - v, 0, mi, mj).wait_recv()

        halo, far = vrecv.at[1 - v], (PAIRS if v else 0)
        for half, at in enumerate((SPLIT, 113) if v else (0, SPLIT - HALO)):
            index = jnp.clip(HALO * sub16 + lane16 - at, 0, 127)
            side = take(jnp.broadcast_to(crecv[1 - v, 1 - half], (CR, 128)), index)
            halo[half] = jnp.where(span(at), side, halo[half])
        for f in range(FIELDS):
            strip_own(f, v, sstat.at[f])
            for half in range(2):
                at = 8 * half + far
                sstat[f, at : at + HALO] = halo[half, HALO * f : HALO * f + HALO]

        sub = sub8 >= PAIRS if v else sub8 < HALO
        groups = [
            jnp.where(sub, zrecv[CR + 1 - v, :, at : at + 128], zrecv[v * (CR - 1), :, at : at + 128])
            for at in (0, 128)
        ]
        tables = columns(8)[v : v + 2]
        wide = [jnp.concatenate([take(groups[f // 5], c + 24 * (f % 5)) for c in tables], 0) for f in range(COARSE)]
        liquid, ice_w, room, per_pore = layers_of(wide)
        sdir = sstat[DIR]
        masks = inflow_masks(sub_up(sdir), sdir, sub_down(sdir))
        entering = (sub16 & 7) == (1 if v else 6)
        h = wide[0] * sstat[SHARE]
        channel = jnp.zeros((CR, 128), jnp.float32)
        for step in range(3):
            move, rest_s, taken = outflow(
                h, liquid, sstat[ORATE], sstat[LAND], schannel[v], sstat[LRATE], ice_w, per_pore
            )
            channel = channel + taken
            move = [jnp.where(entering, enter[step, v, f], m) for f, m in enumerate(move)]
            arriving = [inflow(masks, sub_up(m), m, sub_down(m)) for m in move]
            h, liquid = settle(rest_s, arriving, room)

        first_row = 2 if v else HALO
        mine = ((sub16 & 7) >= first_row) & ((sub16 & 7) < first_row + HALO)
        mine = mine & ((sub16 >= 8) | (lane16 >= SPLIT)) if v else mine & ((sub16 < 8) | (lane16 < SPLIT))
        rows = []
        for n, x in enumerate(liquid + [h, channel]):
            x = jnp.where(mine, x, 0.0) * scales[n]
            rows.append(jnp.concatenate([jnp.sum(x[at : at + 8], 0, keepdims=True) for at in (0, 8)], 1))
        rows.append(jnp.zeros((2, 2 * 128), jnp.float32))
        part = dot2(jnp.concatenate(rows, 0), to_block[128 * v : 128 * v + 256])
        part = pltpu.roll(part, 0, 1, stride=16, stride_axis=0)
        s = v * (CR - 1)
        bsend[s] = back[s : s + 1] + jnp.sum(part, 0, keepdims=True)

        @pl.when(mj != s)
        def _():
            answer(s, mj).start()

    lower_first = lax.rem(mi, 4) == 0

    @pl.when(lower_first)
    def _():
        strip(1)

    strip(0)

    @pl.when(jnp.logical_not(lower_first))
    def _():
        strip(1)

    brecv[mj] = bsend[mj]

    row_pieces().wait_send()

    @pl.when(first_up | last_down)
    def _():
        pltpu.make_async_remote_copy(
            src_ref=zsend,
            dst_ref=zrecv.at[:nc],
            send_sem=zh_sem,
            recv_sem=zr_sem.at[1],
            device_id=(mi, mj),
            device_id_type=MESH,
        ).wait_send()

    for v, (has, i, left, right, end) in enumerate(sides):

        @pl.when(has)
        def _(v=v, i=i):
            vertical(v, i).wait_send()

        @pl.when(has & left)
        def _(v=v, i=i):
            corner(v, 0, i, mj - 1).wait_send()

        @pl.when(has & right)
        def _(v=v, i=i):
            corner(v, 1, i, mj + 1).wait_send()

    @pl.when(has_left)
    def _():
        sideways(0, mj - 1).wait_send()

    @pl.when(has_right)
    def _():
        sideways(1, mj + 1).wait_send()

    answers().wait_recv()

    gather = jnp.minimum(iota((8, 128), 0) * 16 + (lane & 15), 127)
    owner = lax.shift_right_logical(lane, 4)
    for half in range(2):
        out = jnp.zeros((8, 128), jnp.float32)
        for s in range(8):
            x = jnp.broadcast_to(brecv[8 * half + s], (8, 128))
            out = jnp.where(owner == s, take(x, gather), out)
        lanes = slice(128 * half, 128 * half + 128)
        for k in range(LAYERS):
            out_liq[k, :, lanes] = out[k : k + 1]
        out_h[:, lanes] = out[LAYERS : LAYERS + 1]
        out_c[:, lanes] = out[LAYERS + 1 : LAYERS + 2]

    answers().wait_send()


def store(a, b, c, out_a, out_b, out_c, sem):
    copies = [
        pltpu.make_async_copy(src, dst, sem.at[n])
        for n, (src, dst) in enumerate(((a, out_a), (b, out_b), (c, out_c)))
    ]
    for copy in copies:
        copy.start()
    for copy in copies:
        copy.wait()


def solution(mesh):
    nr, nc = mesh.shape["rows"], mesh.shape["cols"]
    f32, bf16 = jnp.float32, jnp.bfloat16

    def step(*args):
        v = pltpu.VMEM
        dma = pltpu.SemaphoreType.DMA
        args = [pltpu.with_memory_space_constraint(x, pltpu.HBM) for x in args]
        results = pl.pallas_call(
            functools.partial(kernel, nr, nc),
            out_shape=(v((LAYERS, 1, W), f32), v((1, W), f32), v((1, W), f32)),
            in_specs=[pl.BlockSpec(memory_space=pltpu.HBM)] * 10,
            out_specs=[pl.BlockSpec(memory_space=pltpu.VMEM)] * 3,
            scratch_shapes=[
                v((1, W), f32),
                v((1, W), f32),
                v((1, W), f32),
                v((LAYERS, 1, W), f32),
                v((LAYERS, 1, W), f32),
                v((TILE, TILE), jnp.int32),
                v((TILE, TILE), jnp.int32),
                v((TILE, TILE), bf16),
                v((TILE, TILE), bf16),
                v((TILE, TILE), bf16),
                v((2 * FIELDS + 2, TILE, 128), f32),
                v((2 * REFINE, CR, 128), f32),
                v((FIELDS + 1, PAIRS * ROWS, 128), f32),
                v(((PAIRS + 2) * ROWS, 128), f32),
                v((4 * LAYERS + 1, ROWS, 128), f32),
                v((2, FIELDS, (PAIRS + 2) * ROWS, 128), f32),
                v((FIELDS, PAIRS * ROWS, 128), f32),
                v((LAYERS + 2, ROWS, 128), f32),
                v((FIELDS, CR, 128), f32),
                v((2, CR, 128), f32),
                v((3, 2, FIELDS, CR, 128), f32),
                v((CR, 1, W), f32),
                v((CR + 2, 1, W), f32),
                v((2, 2, CR, 128), f32),
                v((2, 2, CR, 128), f32),
                v((2, 2, 1, 128), f32),
                v((2, 2, 1, 128), f32),
                v((3, CR, 128), f32),
                v((2, 3, CR, 128), f32),
                v((CR, 1, 128), f32),
                v((CR, 1, 128), f32),
                dma((10,)),
                dma(()),
                dma(()),
                dma((3,)),
                dma((2,)),
                dma((2,)),
                dma((2, 2)),
                dma((2, 2)),
                dma((2,)),
                dma((2,)),
                dma(()),
                dma(()),
                pltpu.SemaphoreType.REGULAR,
                pltpu.SemaphoreType.REGULAR,
            ],
            compiler_params=pltpu.CompilerParams(
                collective_id=0, has_side_effects=True, vmem_limit_bytes=62 * 1024 * 1024
            ),
        )(*args)
        return pl.pallas_call(
            store,
            out_shape=(
                jax.ShapeDtypeStruct((LAYERS, 1, W), f32),
                jax.ShapeDtypeStruct((1, W), f32),
                jax.ShapeDtypeStruct((1, W), f32),
            ),
            in_specs=[pl.BlockSpec(memory_space=pltpu.VMEM)] * 3,
            out_specs=[pl.BlockSpec(memory_space=pltpu.HBM)] * 3,
            scratch_shapes=[dma((3,))],
        )(*[pltpu.with_memory_space_constraint(x, pltpu.VMEM) for x in results])

    return jax.shard_map(
        step,
        mesh=mesh,
        in_specs=(
            P(("rows", "cols"), None),
            P(("rows", "cols"), None),
            P(("rows", "cols"), None),
            P(None, ("rows", "cols"), None),
            P(None, ("rows", "cols"), None),
            P("rows", "cols"),
            P("rows", "cols"),
            P("rows", "cols"),
            P("rows", "cols"),
            P("rows", "cols"),
        ),
        out_specs=(
            P(None, ("rows", "cols"), None),
            P(("rows", "cols"), None),
            P(("rows", "cols"), None),
        ),
        check_vma=False,
    )
```

```python
import functools
import math

import jax
import jax.numpy as jnp
from jax import lax
from jax.experimental import pallas as pl
from jax.experimental.pallas import tpu as pltpu
from jax.sharding import PartitionSpec as P

MESH = pl.DeviceIdType.MESH
REFINE = 10
LAYERS = 4
TILE = 160
CR = 16
W = 256
HALO = 3
PAIRS = REFINE // 2
ROWS = 3 * CR
SPLIT = 56

thickness = (0.1, 0.3, 0.6, 1.0)
layer_speed = (1.0, 0.8, 0.6, 0.4)

DIR, ORATE, LAND, LRATE, SHARE, CHANNEL = range(6)
FIELDS = 5
COARSE = 10


FAR_FIRST = sorted(
    ((z, y, c) for z in range(2) for y in range(4) for c in range(2) if z + y + c),
    key=lambda p: -(p[0] + min(p[1], 4 - p[1])),
)


def others(j):
    z, y, c = j // 8, (j // 2) % 4, j % 2
    return [((z + dz) % 2) * 8 + ((y + dy) % 4) * 2 + (c + dc) % 2 for dz, dy, dc in FAR_FIRST]


def iota(shape, dim):
    return lax.broadcasted_iota(jnp.int32, shape, dim)


def take(x, index):
    return jnp.take_along_axis(x, index, axis=1, mode="promise_in_bounds")


def tenth(x):
    return lax.shift_right_logical(x * 6554, 16)


def split3(x):
    hi = x.astype(jnp.bfloat16)
    r = x - hi.astype(jnp.float32)
    mid = r.astype(jnp.bfloat16)
    lo = (r - mid.astype(jnp.float32)).astype(jnp.bfloat16)
    return jnp.concatenate([hi, mid, lo], 0)


def split2(x):
    hi = x.astype(jnp.bfloat16)
    lo = (x - hi.astype(jnp.float32)).astype(jnp.bfloat16)
    return jnp.concatenate([hi, lo], 0)


def dot3(x, ones):
    n = x.shape[0]
    y = jnp.dot(split3(x), ones, preferred_element_type=jnp.float32)
    return y[:n] + y[n : 2 * n] + y[2 * n :]


def dot2(x, ones):
    n = x.shape[0]
    y = jnp.dot(split2(x), ones, preferred_element_type=jnp.float32)
    return y[:n] + y[n:]


def inflow_masks(d_up, d_mid, d_down):
    return (
        d_up == 1.0,
        d_mid == 0.0,
        d_down == 7.0,
        d_up == 3.0,
        d_mid == 4.0,
        d_down == 5.0,
        d_up == 2.0,
        d_down == 6.0,
    )


def inflow(masks, up, mid, down):
    e0, e1, e2, w0, w1, w2, s0, s1 = masks
    zero = jnp.zeros_like(up)
    east = jnp.where(e0, up, zero) + jnp.where(e1, mid, zero) + jnp.where(e2, down, zero)
    west = jnp.where(w0, up, zero) + jnp.where(w1, mid, zero) + jnp.where(w2, down, zero)
    same = jnp.where(s0, up, zero) + jnp.where(s1, down, zero)
    return same + pltpu.roll(east, 1, 1) + pltpu.roll(west, 127, 1)


def outflow(h, liquid, orate, land, channel, lrate, ice, per_pore):
    q = orate * h * (h / (h + 2.0))
    moving = [q * land]
    rest = [h - q]
    for k in range(LAYERS):
        sat = jnp.minimum((liquid[k] + ice[k]) * per_pore[k], math.sqrt(layer_speed[k]))
        lateral = (lrate * liquid[k]) * (sat * sat)
        moving.append(lateral)
        rest.append(liquid[k] - lateral)
    return moving, rest, q * channel


def settle(rest, arriving, room):
    h = rest[0] + arriving[0]
    liquid = []
    for k in range(LAYERS):
        u = rest[1 + k] + arriving[1 + k]
        h = h + jnp.maximum(u - room[k], 0.0)
        liquid.append(jnp.minimum(u, room[k]))
    return h, liquid


def kernel(
    nr,
    nc,
    rain_h,
    infil_h,
    por_h,
    liq_h,
    ice_h,
    dir_h,
    kind_h,
    orate_h,
    lrate_h,
    weight_h,
    out_liq,
    out_h,
    out_c,
    rain,
    infil,
    por,
    liq,
    ice,
    dir_v,
    kind_v,
    orate_v,
    lrate_v,
    weight_v,
    same_block_v,
    to_block_v,
    nat,
    share_v,
    stat,
    dirs,
    coarse,
    moving,
    rest,
    sums,
    sstat,
    schannel,
    enter,
    zsend,
    zrecv,
    vsend,
    vrecv,
    csend,
    crecv,
    hsend,
    hrecv,
    bsend,
    brecv,
    in_sem,
    zs_sem,
    zh_sem,
    zr_sem,
    vs_sem,
    vr_sem,
    cs_sem,
    cr_sem,
    hs_sem,
    hr_sem,
    bs_sem,
    br_sem,
    row_sem,
    relay_sem,
    late_sem,
):
    mi = lax.axis_index("rows")
    mj = lax.axis_index("cols")
    has_up, has_down = mi > 0, mi < nr - 1
    has_left, has_right = mj > 0, mj < nc - 1

    barrier = pltpu.get_barrier_semaphore()
    lead = nc - 2
    is_lead = mj == lead

    def tell(i, j):
        pl.semaphore_signal(barrier, inc=1, device_id=(i, j), device_id_type=MESH)

    @pl.when(jnp.logical_not(is_lead))
    def _():
        tell(mi, lead)

    copies = [
        pltpu.make_async_copy(src, dst, in_sem.at[n])
        for n, (src, dst) in enumerate(
            (
                (rain_h, rain),
                (infil_h, infil),
                (por_h, por),
                (liq_h, liq),
                (ice_h, ice),
                (weight_h, weight_v),
                (dir_h, dir_v),
                (kind_h, kind_v),
                (orate_h, orate_v),
                (lrate_h, lrate_v),
            )
        )
    ]
    for copy in copies:
        copy.start()

    sides = (
        (has_up, mi - 1, has_left, has_right, nc - 1),
        (has_down, mi + 1, has_left, has_right, 0),
    )
    late = (lax.rem(mi, 4) == 3) & has_down
    late_side = (has_up & (lax.rem(mi, 4) != 0), late)
    early_side = (has_up & (lax.rem(mi, 4) == 0), has_down & (lax.rem(mi, 4) != 3))
    own_end = (0, nc - 1)

    def partners(v, signal):
        has, i, left, right, end = sides[v]
        signal(i, end)
        signal(i, mj)

        @pl.when(left)
        def _():
            signal(i, mj - 1)

        @pl.when(right)
        def _():
            signal(i, mj + 1)

        @pl.when(mj == own_end[v])
        def _():
            @pl.loop(0, nc)
            def _(k):
                signal(i, k)

    def count(v):
        one = 2 + has_left.astype(jnp.int32) + has_right.astype(jnp.int32)
        return one + nc * (mj == own_end[v]).astype(jnp.int32)

    def tell_late_one(i, j):
        @pl.when(j != lead)
        def _():
            tell(i, j)

    for v in range(2):

        @pl.when(early_side[v])
        def _(v=v):
            partners(v, tell_late_one)

    @pl.when(is_lead)
    def _():
        pl.semaphore_wait(barrier, nc - 1)
        near = [lead - 1, lead + 1]
        for k in near + [k for k in others(lead) if k not in near]:
            pl.semaphore_signal(row_sem, inc=1, device_id=(mi, k), device_id_type=MESH)

    row_c, col_c = iota((W, W), 0), iota((W, W), 1)
    same_block = (tenth(row_c) == tenth(col_c)) & (row_c < TILE) & (col_c < TILE)
    same_block_v[...] = jnp.where(same_block, 1.0, 0.0).astype(jnp.bfloat16)
    row_p, col_p = iota((128, 128), 0), iota((128, 128), 1)
    to_block = []
    for at, end, shift in ((3, 113, 0), (3, 53, 11), (3, 113, 5)):
        mine = (row_p >= at) & (row_p < end) & (tenth(row_p + 7) == col_p + 1 - shift)
        if shift == 11:
            mine = mine | ((row_p >= 59) & (row_p < 109) & (tenth(row_p - 49) == col_p + 1))
        to_block.append(jnp.where(mine, 1.0, 0.0).astype(jnp.bfloat16))
    to_block_v[...] = jnp.concatenate(to_block, 0)

    lane = iota((8, 128), 1)
    lane16 = iota((CR, 128), 1)
    sub16 = iota((CR, 128), 0)

    def piece(k, i, s, send, arrive):
        return pltpu.make_async_remote_copy(
            src_ref=zsend.at[k],
            dst_ref=zrecv.at[s],
            send_sem=send,
            recv_sem=arrive,
            device_id=(i, k),
            device_id_type=MESH,
        )

    def row_pieces():
        return pltpu.make_async_remote_copy(
            src_ref=zsend.at[: nc - 1],
            dst_ref=zrecv.at[: nc - 1],
            send_sem=zs_sem,
            recv_sem=zr_sem.at[0],
            device_id=(mi, mj),
            device_id_type=MESH,
        )

    first_up = has_up & (mj == 0)
    last_down = has_down & (mj == nc - 1)

    def first_run(a):
        return pltpu.roll(a, HALO, 1)

    def second_run(a, b):
        return jnp.where(lane16 < 21, pltpu.roll(a, 21, 1), pltpu.roll(b, 21, 1))

    def third_run(a):
        return pltpu.roll(a, 59, 1)

    def fourth_run(a, b):
        return jnp.where(lane16 < 81, pltpu.roll(a, 81, 1), pltpu.roll(b, 81, 1))

    def rows_of(f, rr):
        return [nat.at[2 * f + half][pl.ds(rr, CR, stride=REFINE), :] for half in range(2)]

    def field(f):
        return (dirs, ROWS) if f == DIR else (stat.at[f], 0)

    def vertical(v, i):
        return pltpu.make_async_remote_copy(
            src_ref=vsend.at[v],
            dst_ref=vrecv.at[v],
            send_sem=vs_sem.at[v],
            recv_sem=vr_sem.at[v],
            device_id=(i, mj),
            device_id_type=MESH,
        )

    def corner(v, s, i, j):
        return pltpu.make_async_remote_copy(
            src_ref=csend.at[v, s],
            dst_ref=crecv.at[v, s],
            send_sem=cs_sem.at[v, s],
            recv_sem=cr_sem.at[v, s],
            device_id=(i, j),
            device_id_type=MESH,
        )

    incoming = sum(late_side[v].astype(jnp.int32) * count(v) for v in range(2))

    any_late = late_side[0] | late_side[1]
    passes_on = (mj == lead - 1) | (mj == lead + 1)

    def rows_ready():
        pl.semaphore_wait(barrier, incoming)

    def pass_on():
        pl.semaphore_signal(relay_sem, inc=1, device_id=(mi, lead), device_id_type=MESH)

    def send_ends(v):
        @pl.when(mj == own_end[v])
        def _():
            @pl.loop(0, nc)
            def _(k):
                piece(k, sides[v][1], CR + v, zh_sem, zr_sem.at[1 + v]).start()

    def send_rows(v):
        _, i, left, right, _ = sides[v]
        vertical(v, i).start()

        @pl.when(left)
        def _():
            corner(v, 0, i, mj - 1).start()

        @pl.when(right)
        def _():
            corner(v, 1, i, mj + 1).start()

    def tell_early(v):
        def signal(i, j):
            pl.semaphore_signal(late_sem.at[1 - v], inc=1, device_id=(i, j), device_id_type=MESH)

        partners(v, signal)

    def coarse_part():
        for copy in copies[:5]:
            copy.wait()
        rain_x, por_x = rain[...], por[...]
        top_sat = (liq[0] + ice[0]) / por_x
        capacity = infil[...] * jnp.maximum(1.0 - top_sat, 0.1)
        excess = rain_x * rain_x / (rain_x + capacity)
        top = liq[0] + (rain_x - excess) / (1000.0 * thickness[0])
        strip = [excess, por_x, top] + [liq[k] for k in range(1, LAYERS)] + [ice[k] for k in range(LAYERS)]

        slot = lax.shift_right_logical(lane * 2731, 16)
        t = lane - slot * 24
        for half in range(2):
            base = (iota((8, 128), 0) + 8 * half) * 16 - 1 + t
            inside = jnp.clip(base, 0, W - 1)
            index = inside & 127
            low = inside < 128
            for group in range(2):
                packed = jnp.zeros((8, 128), jnp.float32)
                for n in range(5):
                    x = strip[group * 5 + n]
                    a = jnp.broadcast_to(x[:, :128], (8, 128))
                    b = jnp.broadcast_to(x[:, 128:], (8, 128))
                    packed = jnp.where(slot == n, jnp.where(low, take(a, index), take(b, index)), packed)
                for s in range(8):
                    zsend[8 * half + s, :, 128 * group : 128 * group + 128] = packed[s : s + 1]

        zrecv[mj] = zsend[mj]

        @pl.when(jnp.logical_not(has_down))
        def _():
            zrecv[CR] = zsend[mj]

        @pl.when(jnp.logical_not(has_up))
        def _():
            zrecv[CR + 1] = zsend[mj]

    def tile_arrived():
        for copy in copies[5:]:
            copy.wait()

    def vertical_part():
        no_lanes = jnp.zeros((CR, 96), jnp.float32)

        def in_halves(x):
            return x[:, :128], jnp.concatenate([x[:, 128:], no_lanes[: x.shape[0]]], 1)

        edges, totals = [], []
        for v in range(2):
            r = v * (TILE - CR)
            kind_x = kind_v[r : r + CR]
            edge = [
                dir_v[r : r + CR].astype(jnp.float32),
                jnp.where(kind_x == 2, 0.0, orate_v[r : r + CR].astype(jnp.float32)),
                jnp.where(kind_x == 0, 1.0, 0.0),
                lrate_v[r : r + CR].astype(jnp.float32),
                weight_v[r : r + CR].astype(jnp.float32),
            ]
            edge = [in_halves(x) for x in edge]
            mine = sub16 >= CR - REFINE if v else sub16 < REFINE
            total = [jnp.sum(jnp.where(mine, x, 0.0), 0, keepdims=True) for x in edge[SHARE]]
            edges.append(edge)
            totals.append(jnp.concatenate(total, 1))
        totals.append(jnp.zeros((6, W), jnp.float32))
        per_mean = 100.0 / jnp.where(iota((8, W), 1) < TILE, dot3(jnp.concatenate(totals, 0), same_block_v[...]), 1.0)
        place = lane16 - HALO * sub16
        for v in (1, 0):
            r = v * (CR - HALO)
            for half in range(2):
                scale = per_mean[v : v + 1, 128 * half : 128 * half + 128]
                for f in range(FIELDS):
                    x = edges[v][f][half][r : r + HALO]
                    vsend[v, half, HALO * f : HALO * f + HALO] = x * scale if f == SHARE else x
                vsend[v, half, HALO * FIELDS :] = jnp.zeros((1, 128), jnp.float32)
            a, b = vsend[v, 0], vsend[v, 1]
            if v == 0:
                vsend[v, 0], vsend[v, 1] = third_run(a), fourth_run(a, b)
            else:
                vsend[v, 0], vsend[v, 1] = first_run(a), second_run(a, b)
            for n, (x, at) in enumerate(((a, 0), (b, 29))):
                end = jnp.where((place >= 0) & (place < HALO), take(x, jnp.clip(place + at, 0, 127)), 0.0)
                csend[v, n] = jnp.sum(end, 0, keepdims=True)

    def tile_part():
        kind_x = kind_v[...]
        natural = (
            dir_v[...].astype(jnp.float32),
            jnp.where(kind_x == 2, 0.0, orate_v[...].astype(jnp.float32)),
            jnp.where(kind_x == 0, 1.0, 0.0),
            lrate_v[...].astype(jnp.float32),
            weight_v[...].astype(jnp.float32),
            jnp.where(kind_x == 1, 1.0, 0.0),
        )
        no_lanes = jnp.zeros((TILE, 96), jnp.float32)
        for f in range(FIELDS + 1):
            nat[2 * f] = natural[f][:, :128]
            nat[2 * f + 1] = jnp.concatenate([natural[f][:, 128:], no_lanes], 1)

        weights = [rows_of(SHARE, rr) for rr in range(REFINE)]
        total = [functools.reduce(lambda a, b: a + b, [w[half] for w in weights]) for half in range(2)]
        block_sum = dot3(jnp.concatenate(total, 1), same_block_v[...])
        per_mean = 100.0 / jnp.where(iota((CR, W), 1) < TILE, block_sum, 1.0)
        shares = [[w[half] * per_mean[:, 128 * half : 128 * half + 128] for half in range(2)] for w in weights]
        for rr in range(REFINE):
            for half in range(2):
                share_v[2 * rr + half] = shares[rr][half]

    def send_pieces():
        for k in others(mj):
            piece(k, mi, mj, zs_sem, zr_sem.at[0]).start()

    def meet_early():
        @pl.when(passes_on)
        def _():
            pl.semaphore_wait(row_sem, 1)

        @pl.when(jnp.logical_not(is_lead))
        def _():
            rows_ready()

        @pl.when(passes_on)
        def _():
            pass_on()

        @pl.when(is_lead)
        def _():
            pl.semaphore_wait(relay_sem, 2)

        for v in (1, 0):

            @pl.when(late_side[v])
            def _(v=v):
                tell_early(v)

    def send_late():
        for v in (1, 0):

            @pl.when(late_side[v])
            def _(v=v):
                send_rows(v)

    @pl.when(late)
    def _():
        tile_arrived()
        vertical_part()
        meet_early()
        send_late()

    coarse_part()

    @pl.when(late)
    def _():
        send_ends(1)
        send_ends(0)

    @pl.when(is_lead)
    def _():
        send_pieces()

    @pl.when(jnp.logical_not(late))
    def _():
        tile_arrived()

    tile_part()

    @pl.when(any_late & jnp.logical_not(late))
    def _():
        meet_early()
        send_ends(0)

    shares = [[share_v[2 * rr + half] for half in range(2)] for rr in range(REFINE)]

    def slab_place(rr, f):
        n = rr * FIELDS + f
        return n // 18, HALO * (n % 9) + 64 * (n % 18 // 9)

    slabs = [jnp.zeros((CR, 128), jnp.float32)] * 3
    for rr in range(REFINE):
        for f in range(FIELDS):
            a, b = shares[rr] if f == SHARE else rows_of(f, rr)
            x = jnp.where(lane16 < HALO, a, jnp.where((lane16 >= 29) & (lane16 < 32), b, 0.0))
            n, at = slab_place(rr, f)
            slabs[n] = slabs[n] + (pltpu.roll(x, at, 1) if at else x)
    for n in range(3):
        hsend[n] = slabs[n]

    def sideways(n, j):
        return pltpu.make_async_remote_copy(
            src_ref=hsend,
            dst_ref=hrecv.at[n],
            send_sem=hs_sem.at[n],
            recv_sem=hr_sem.at[n],
            device_id=(mi, j),
            device_id_type=MESH,
        )

    @pl.when(jnp.logical_not(is_lead))
    def _():
        @pl.when(jnp.logical_not(any_late & passes_on))
        def _():
            pl.semaphore_wait(row_sem, 1)

        send_pieces()

    @pl.when(has_left)
    def _():
        sideways(0, mj - 1).start()

    @pl.when(has_right)
    def _():
        sideways(1, mj + 1).start()

    @pl.when(jnp.logical_not(late))
    def _():
        vertical_part()
        send_late()

    for p in range(PAIRS):
        for f in range(FIELDS + 1):
            if f == SHARE:
                (a, b), (c, d) = shares[p], shares[p + PAIRS]
            else:
                (a, b), (c, d) = rows_of(f, p), rows_of(f, p + PAIRS)
            ref, off = field(f)
            r = off + p * ROWS
            ref[r : r + CR] = first_run(a)
            ref[r + CR : r + 2 * CR] = jnp.where(lane16 < SPLIT, second_run(a, b), third_run(c))
            ref[r + 2 * CR : r + ROWS] = fourth_run(c, d)

    def strip_own(f, v, out):
        ref, off = field(f)
        for half in range(2):
            at = 8 * half + (0 if v else HALO)
            r = off + (v + half) * CR + v * (CR - 1)
            out[at : at + PAIRS] = ref[pl.ds(r, PAIRS, stride=ROWS), :]

    lane8, sub8 = iota((8, 128), 1), iota((8, 128), 0)
    schannel[...] = jnp.zeros(schannel.shape, jnp.float32)
    for v in range(2):
        strip_own(CHANNEL, v, schannel.at[v])

    row48, lane48 = iota((ROWS, 128), 0), iota((ROWS, 128), 1)
    in_first = (row48 == 0) | ((row48 == CR) & (lane48 < SPLIT))
    in_last = (row48 == ROWS - 1) | ((row48 == 2 * CR - 1) & (lane48 >= SPLIT))
    for p in range(PAIRS):
        out = in_first if p < 2 else in_last if p > 2 else in_first | in_last
        r = p * ROWS
        stat[CHANNEL, r : r + ROWS] = jnp.where(out, 0.0, stat[CHANNEL, r : r + ROWS])

    def send_early(v):
        @pl.when(early_side[v])
        def _():
            pl.semaphore_wait(late_sem.at[v], count(v))
            send_rows(v)
            send_ends(v)

    send_early(1)

    for v, (has, i, left, right, end) in enumerate(sides):

        @pl.when(jnp.logical_not(has))
        def _(v=v):
            vrecv[1 - v] = jnp.zeros(vrecv.shape[1:], jnp.float32)

        @pl.when(jnp.logical_not(has & left))
        def _(v=v):
            crecv[1 - v, 1] = jnp.zeros((1, 128), jnp.float32)

        @pl.when(jnp.logical_not(has & right))
        def _(v=v):
            crecv[1 - v, 0] = jnp.zeros((1, 128), jnp.float32)

    @pl.when(jnp.logical_not(has_right))
    def _():
        hrecv[0] = jnp.zeros(hrecv.shape[1:], jnp.float32)

    @pl.when(jnp.logical_not(has_left))
    def _():
        hrecv[1] = jnp.zeros(hrecv.shape[1:], jnp.float32)

    def columns(n):
        lanes = iota((n, 128), 1)
        return (
            tenth(lanes + 7),
            tenth(jnp.where(lanes < SPLIT, lanes + 117, lanes - 49)),
            jnp.minimum(tenth(lanes + 57), 17),
        )

    def layers_of(wide):
        por_w = wide[1]
        liquid, ice_w, room, per_pore = [], [], [], []
        for k in range(LAYERS):
            depth = 1000.0 * thickness[k]
            liquid.append(wide[2 + k] * depth)
            ice_w.append(wide[2 + LAYERS + k] * depth)
            room.append((por_w - wide[2 + LAYERS + k]) * depth)
            per_pore.append((math.sqrt(layer_speed[k]) / depth) / por_w)
        return liquid, ice_w, room, per_pore

    @pl.when(has_right)
    def _():
        sideways(0, mj).wait_recv()

    @pl.when(has_left)
    def _():
        sideways(1, mj).wait_recv()

    def span(at):
        return (lane16 >= at) & (lane16 < at + HALO)

    for p in range(PAIRS):
        for f in range(FIELDS):
            ref, off = field(f)
            r = off + p * ROWS
            for rr, (left_row, left_at), (right_row, right_at) in (
                (p, (r, 0), (r + CR, SPLIT - HALO)),
                (p + PAIRS, (r + CR, SPLIT), (r + 2 * CR, 113)),
            ):
                n, at = slab_place(rr, f)
                from_left = pltpu.roll(hrecv[1, n], (left_at - 29 - at) % 128, 1)
                from_right = pltpu.roll(hrecv[0, n], (right_at - at) % 128, 1)
                ref[left_row : left_row + CR] = jnp.where(
                    span(left_at), from_left, ref[left_row : left_row + CR]
                )
                ref[right_row : right_row + CR] = jnp.where(
                    span(right_at), from_right, ref[right_row : right_row + CR]
                )

    END = ROWS * (PAIRS + 1)
    sub_up = functools.partial(pltpu.roll, shift=1, axis=0)

    def sub_down(x):
        return pltpu.roll(x, x.shape[0] - 1, 0)

    def across(x):
        x0, x1, x2 = x[:CR], x[CR : 2 * CR], x[2 * CR :]
        return (
            jnp.where(lane16 < 53, pltpu.roll(x1, 72, 1), pltpu.roll(x2, 50, 1)),
            pltpu.roll(x2, 68, 1),
            pltpu.roll(x0, SPLIT, 1),
            jnp.where(lane16 < 63, pltpu.roll(x0, 78, 1), pltpu.roll(x1, 60, 1)),
        )

    def wrap(ref):
        a, b, c, d = across(ref[END - ROWS : END])
        ref[:CR] = sub_up(a)
        ref[CR : 2 * CR] = jnp.where(lane16 < SPLIT, sub_up(b), c)
        ref[2 * CR : ROWS] = d
        a, b, c, d = across(ref[ROWS : 2 * ROWS])
        ref[END : END + CR] = a
        ref[END + CR : END + 2 * CR] = jnp.where(lane16 < SPLIT, b, sub_down(c))
        ref[END + 2 * CR :] = sub_down(d)

    wrap(dirs)
    sums[...] = jnp.zeros(sums.shape, jnp.float32)

    row_pieces().wait_recv()

    def rows_at(group, slots):
        return jnp.concatenate([zrecv[n, :, 128 * group : 128 * group + 128] for n in slots], 0)

    packed_rows = [rows_at(g, range(CR)) for g in range(2)]
    wide = [
        jnp.concatenate([take(packed_rows[f // 5], c + 24 * (f % 5)) for c in columns(CR)], 0) for f in range(COARSE)
    ]
    liquid_w, ice_w, room, per_pore = layers_of(wide)
    for n, x in enumerate(ice_w + room + per_pore + liquid_w + wide[:1]):
        coarse[n] = x

    def finish(b, step):
        top, bottom = ROWS + HALO * ROWS, ROWS + ROWS + CR - 1
        for f in range(FIELDS):
            wrap(moving.at[b, f])
            enter[step, 0, f, 6:7] = moving[b, f, top : top + 1]
            enter[step, 0, f, 14:15] = moving[b, f, top + CR : top + CR + 1]
            enter[step, 1, f, 1:2] = moving[b, f, bottom + CR : bottom + CR + 1]
            enter[step, 1, f, 9:10] = moving[b, f, bottom + 2 * CR : bottom + 2 * CR + 1]

    def main_in(b, r, c):
        masks = inflow_masks(*[dirs[pl.ds(r + n * ROWS, CR), :] for n in range(3)])
        arriving = [
            inflow(masks, *[moving[b, f, pl.ds(r + n * ROWS, CR), :] for n in range(3)])
            for f in range(FIELDS)
        ]
        left = [rest[f, pl.ds(r, CR), :] for f in range(FIELDS)]
        return settle(left, arriving, [coarse[LAYERS + k, c : c + CR] for k in range(LAYERS)])

    def main_out(b, r, c, h, liquid):
        move, left, taken = outflow(
            h,
            liquid,
            stat[ORATE, pl.ds(r, CR), :],
            stat[LAND, pl.ds(r, CR), :],
            stat[CHANNEL, pl.ds(r, CR), :],
            stat[LRATE, pl.ds(r, CR), :],
            [coarse[k, c : c + CR] for k in range(LAYERS)],
            [coarse[2 * LAYERS + k, c : c + CR] for k in range(LAYERS)],
        )
        for f in range(FIELDS):
            moving[b, f, pl.ds(r + ROWS, CR), :] = move[f]
            rest[f, pl.ds(r, CR), :] = left[f]
        sums[LAYERS + 1, c : c + CR] += taken

    def row_at(p, c):
        return pl.multiple_of(p * ROWS + c, CR)

    @pl.loop(0, PAIRS, unroll=True)
    def _(p):
        for c in range(0, ROWS, CR):
            r = row_at(p, c)
            h = coarse[4 * LAYERS, c : c + CR] * stat[SHARE, pl.ds(r, CR), :]
            main_out(0, r, c, h, [coarse[3 * LAYERS + k, c : c + CR] for k in range(LAYERS)])

    finish(0, 0)

    for b in range(2):

        @pl.loop(0, PAIRS, unroll=True)
        def _(p, b=b):
            for c in range(0, ROWS, CR):
                r = row_at(p, c)
                main_out(1 - b, r, c, *main_in(b, r, c))

        finish(1 - b, 1 + b)

    since = jnp.where(in_first, HALO, 0)
    until = jnp.where(in_last, PAIRS - HALO, PAIRS)

    @pl.loop(0, PAIRS, unroll=True)
    def _(p):
        for c in range(0, ROWS, CR):
            h, liquid = main_in(0, row_at(p, c), c)
            keep = (since[c : c + CR] <= p) & (until[c : c + CR] > p)
            for n, x in enumerate(liquid + [h]):
                sums[n, c : c + CR] += jnp.where(keep, x, 0.0)

    scales = [0.01 / (1000.0 * x) for x in thickness] + [0.01, 0.01]

    def three(n):
        return jnp.concatenate([sums[n, c : c + CR] for c in range(0, ROWS, CR)], 1) * scales[n]

    means = dot2(jnp.concatenate([three(n) for n in range(LAYERS + 2)], 0), to_block_v[...])
    back = means[:CR]
    for n in range(1, LAYERS + 2):
        back = back + pltpu.roll(means[n * CR : (n + 1) * CR], 16 * n, 1)
    for s in range(1, CR - 1):
        bsend[s] = back[s : s + 1]

    def answer(k, s):
        return pltpu.make_async_remote_copy(
            src_ref=bsend.at[k],
            dst_ref=brecv.at[s],
            send_sem=bs_sem,
            recv_sem=br_sem,
            device_id=(mi, k),
            device_id_type=MESH,
        )

    def answers():
        return pltpu.make_async_remote_copy(
            src_ref=bsend.at[: nc - 1],
            dst_ref=brecv.at[: nc - 1],
            send_sem=bs_sem,
            recv_sem=br_sem,
            device_id=(mi, mj),
            device_id_type=MESH,
        )

    for k in others(mj):

        @pl.when((k != 0) & (k != nc - 1))
        def _(k=k):
            answer(k, mj).start()

    def strip(v):
        has, _, left, right, _ = sides[v]

        @pl.when(has)
        def _():
            vertical(1 - v, mi).wait_recv()
            piece(0, mi, CR + 1 - v, zh_sem, zr_sem.at[2 - v]).wait_recv()

        @pl.when(has & left)
        def _():
            corner(1 - v, 1, mi, mj).wait_recv()

        @pl.when(has & right)
        def _():
            corner(1 - v, 0, mi, mj).wait_recv()

        halo, far = vrecv.at[1 - v], (PAIRS if v else 0)
        for half, at in enumerate((SPLIT, 113) if v else (0, SPLIT - HALO)):
            index = jnp.clip(HALO * sub16 + lane16 - at, 0, 127)
            side = take(jnp.broadcast_to(crecv[1 - v, 1 - half], (CR, 128)), index)
            halo[half] = jnp.where(span(at), side, halo[half])
        for f in range(FIELDS):
            strip_own(f, v, sstat.at[f])
            for half in range(2):
                at = 8 * half + far
                sstat[f, at : at + HALO] = halo[half, HALO * f : HALO * f + HALO]

        sub = sub8 >= PAIRS if v else sub8 < HALO
        groups = [
            jnp.where(sub, zrecv[CR + 1 - v, :, at : at + 128], zrecv[v * (CR - 1), :, at : at + 128])
            for at in (0, 128)
        ]
        tables = columns(8)[v : v + 2]
        wide = [jnp.concatenate([take(groups[f // 5], c + 24 * (f % 5)) for c in tables], 0) for f in range(COARSE)]
        liquid, ice_w, room, per_pore = layers_of(wide)
        sdir = sstat[DIR]
        masks = inflow_masks(sub_up(sdir), sdir, sub_down(sdir))
        entering = (sub16 & 7) == (1 if v else 6)
        h = wide[0] * sstat[SHARE]
        channel = jnp.zeros((CR, 128), jnp.float32)
        for step in range(3):
            move, rest_s, taken = outflow(
                h, liquid, sstat[ORATE], sstat[LAND], schannel[v], sstat[LRATE], ice_w, per_pore
            )
            channel = channel + taken
            move = [jnp.where(entering, enter[step, v, f], m) for f, m in enumerate(move)]
            arriving = [inflow(masks, sub_up(m), m, sub_down(m)) for m in move]
            h, liquid = settle(rest_s, arriving, room)

        first_row = 2 if v else HALO
        mine = ((sub16 & 7) >= first_row) & ((sub16 & 7) < first_row + HALO)
        mine = mine & ((sub16 >= 8) | (lane16 >= SPLIT)) if v else mine & ((sub16 < 8) | (lane16 < SPLIT))
        rows = []
        for n, x in enumerate(liquid + [h, channel]):
            x = jnp.where(mine, x, 0.0) * scales[n]
            rows.append(jnp.concatenate([jnp.sum(x[at : at + 8], 0, keepdims=True) for at in (0, 8)], 1))
        rows.append(jnp.zeros((2, 2 * 128), jnp.float32))
        part = dot2(jnp.concatenate(rows, 0), to_block_v[128 * v : 128 * v + 256])
        part = pltpu.roll(part, 0, 1, stride=16, stride_axis=0)
        s = v * (CR - 1)
        bsend[s] = back[s : s + 1] + jnp.sum(part, 0, keepdims=True)

        @pl.when(mj != s)
        def _():
            answer(s, mj).start()

    lower_first = lax.rem(mi, 4) == 0
    send_early(0)

    @pl.when(lower_first)
    def _():
        strip(1)

    strip(0)

    @pl.when(jnp.logical_not(lower_first))
    def _():
        strip(1)

    brecv[mj] = bsend[mj]

    row_pieces().wait_send()

    @pl.when(first_up | last_down)
    def _():
        pltpu.make_async_remote_copy(
            src_ref=zsend,
            dst_ref=zrecv.at[:nc],
            send_sem=zh_sem,
            recv_sem=zr_sem.at[1],
            device_id=(mi, mj),
            device_id_type=MESH,
        ).wait_send()

    for v, (has, i, left, right, end) in enumerate(sides):

        @pl.when(has)
        def _(v=v, i=i):
            vertical(v, i).wait_send()

        @pl.when(has & left)
        def _(v=v, i=i):
            corner(v, 0, i, mj - 1).wait_send()

        @pl.when(has & right)
        def _(v=v, i=i):
            corner(v, 1, i, mj + 1).wait_send()

    @pl.when(has_left)
    def _():
        sideways(0, mj - 1).wait_send()

    @pl.when(has_right)
    def _():
        sideways(1, mj + 1).wait_send()

    answers().wait_recv()

    gather = jnp.minimum(iota((8, 128), 0) * 16 + (lane & 15), 127)
    owner = lax.shift_right_logical(lane, 4)
    for half in range(2):
        out = jnp.zeros((8, 128), jnp.float32)
        for s in range(8):
            x = jnp.broadcast_to(brecv[8 * half + s], (8, 128))
            out = jnp.where(owner == s, take(x, gather), out)
        lanes = slice(128 * half, 128 * half + 128)
        for k in range(LAYERS):
            out_liq[k, :, lanes] = out[k : k + 1]
        out_h[:, lanes] = out[LAYERS : LAYERS + 1]
        out_c[:, lanes] = out[LAYERS + 1 : LAYERS + 2]

    answers().wait_send()


def store(a, b, c, out_a, out_b, out_c, sem):
    copies = [
        pltpu.make_async_copy(src, dst, sem.at[n])
        for n, (src, dst) in enumerate(((a, out_a), (b, out_b), (c, out_c)))
    ]
    for copy in copies:
        copy.start()
    for copy in copies:
        copy.wait()


def solution(mesh):
    nr, nc = mesh.shape["rows"], mesh.shape["cols"]
    f32, bf16 = jnp.float32, jnp.bfloat16

    def step(*args):
        v = pltpu.VMEM
        dma = pltpu.SemaphoreType.DMA
        args = [pltpu.with_memory_space_constraint(x, pltpu.HBM) for x in args]
        results = pl.pallas_call(
            functools.partial(kernel, nr, nc),
            out_shape=(v((LAYERS, 1, W), f32), v((1, W), f32), v((1, W), f32)),
            in_specs=[pl.BlockSpec(memory_space=pltpu.HBM)] * 10,
            out_specs=[pl.BlockSpec(memory_space=pltpu.VMEM)] * 3,
            scratch_shapes=[
                v((1, W), f32),
                v((1, W), f32),
                v((1, W), f32),
                v((LAYERS, 1, W), f32),
                v((LAYERS, 1, W), f32),
                v((TILE, TILE), jnp.int32),
                v((TILE, TILE), jnp.int32),
                v((TILE, TILE), bf16),
                v((TILE, TILE), bf16),
                v((TILE, TILE), bf16),
                v((W, W), bf16),
                v((3 * 128, 128), bf16),
                v((2 * FIELDS + 2, TILE, 128), f32),
                v((2 * REFINE, CR, 128), f32),
                v((FIELDS + 1, PAIRS * ROWS, 128), f32),
                v(((PAIRS + 2) * ROWS, 128), f32),
                v((4 * LAYERS + 1, ROWS, 128), f32),
                v((2, FIELDS, (PAIRS + 2) * ROWS, 128), f32),
                v((FIELDS, PAIRS * ROWS, 128), f32),
                v((LAYERS + 2, ROWS, 128), f32),
                v((FIELDS, CR, 128), f32),
                v((2, CR, 128), f32),
                v((3, 2, FIELDS, CR, 128), f32),
                v((CR, 1, W), f32),
                v((CR + 2, 1, W), f32),
                v((2, 2, CR, 128), f32),
                v((2, 2, CR, 128), f32),
                v((2, 2, 1, 128), f32),
                v((2, 2, 1, 128), f32),
                v((3, CR, 128), f32),
                v((2, 3, CR, 128), f32),
                v((CR, 1, 128), f32),
                v((CR, 1, 128), f32),
                dma((10,)),
                dma(()),
                dma(()),
                dma((3,)),
                dma((2,)),
                dma((2,)),
                dma((2, 2)),
                dma((2, 2)),
                dma((2,)),
                dma((2,)),
                dma(()),
                dma(()),
                pltpu.SemaphoreType.REGULAR,
                pltpu.SemaphoreType.REGULAR,
                pltpu.SemaphoreType.REGULAR((2,)),
            ],
            compiler_params=pltpu.CompilerParams(
                collective_id=0, has_side_effects=True, vmem_limit_bytes=62 * 1024 * 1024
            ),
        )(*args)
        return pl.pallas_call(
            store,
            out_shape=(
                jax.ShapeDtypeStruct((LAYERS, 1, W), f32),
                jax.ShapeDtypeStruct((1, W), f32),
                jax.ShapeDtypeStruct((1, W), f32),
            ),
            in_specs=[pl.BlockSpec(memory_space=pltpu.VMEM)] * 3,
            out_specs=[pl.BlockSpec(memory_space=pltpu.HBM)] * 3,
            scratch_shapes=[dma((3,))],
        )(*[pltpu.with_memory_space_constraint(x, pltpu.VMEM) for x in results])

    return jax.shard_map(
        step,
        mesh=mesh,
        in_specs=(
            P(("rows", "cols"), None),
            P(("rows", "cols"), None),
            P(("rows", "cols"), None),
            P(None, ("rows", "cols"), None),
            P(None, ("rows", "cols"), None),
            P("rows", "cols"),
            P("rows", "cols"),
            P("rows", "cols"),
            P("rows", "cols"),
            P("rows", "cols"),
        ),
        out_specs=(
            P(None, ("rows", "cols"), None),
            P(("rows", "cols"), None),
            P(("rows", "cols"), None),
        ),
        check_vma=False,
    )
```

```python
import functools
import math

import jax
import jax.numpy as jnp
from jax import lax
from jax.experimental import pallas as pl
from jax.experimental.pallas import tpu as pltpu
from jax.sharding import PartitionSpec as P

MESH = pl.DeviceIdType.MESH
REFINE = 10
LAYERS = 4
TILE = 160
CR = 16
W = 256
HALO = 3
PAIRS = REFINE // 2
INNER_FIRST = tuple(range(1, PAIRS - 1)) + (0, PAIRS - 1)
OUTER_FIRST = (0, PAIRS - 1) + tuple(range(1, PAIRS - 1))
ROWS = 3 * CR
SPLIT = 56

thickness = (0.1, 0.3, 0.6, 1.0)
layer_speed = (1.0, 0.8, 0.6, 0.4)

DIR, ORATE, LAND, LRATE, SHARE, CHANNEL = range(6)
FIELDS = 5
COARSE = 10


FAR_FIRST = sorted(
    ((z, y, c) for z in range(2) for y in range(4) for c in range(2) if z + y + c),
    key=lambda p: -(p[0] + min(p[1], 4 - p[1])),
)


def others(j):
    z, y, c = j // 8, (j // 2) % 4, j % 2
    return [((z + dz) % 2) * 8 + ((y + dy) % 4) * 2 + (c + dc) % 2 for dz, dy, dc in FAR_FIRST]


def iota(shape, dim):
    return lax.broadcasted_iota(jnp.int32, shape, dim)


def take(x, index):
    return jnp.take_along_axis(x, index, axis=1, mode="promise_in_bounds")


def tenth(x):
    return lax.shift_right_logical(x * 6554, 16)


def split3(x):
    hi = x.astype(jnp.bfloat16)
    r = x - hi.astype(jnp.float32)
    mid = r.astype(jnp.bfloat16)
    lo = (r - mid.astype(jnp.float32)).astype(jnp.bfloat16)
    return jnp.concatenate([hi, mid, lo], 0)


def split2(x):
    hi = x.astype(jnp.bfloat16)
    lo = (x - hi.astype(jnp.float32)).astype(jnp.bfloat16)
    return jnp.concatenate([hi, lo], 0)


def dot3(x, ones):
    n = x.shape[0]
    y = jnp.dot(split3(x), ones, preferred_element_type=jnp.float32)
    return y[:n] + y[n : 2 * n] + y[2 * n :]


def dot2(x, ones):
    n = x.shape[0]
    y = jnp.dot(split2(x), ones, preferred_element_type=jnp.float32)
    return y[:n] + y[n:]


def inflow_masks(d_up, d_mid, d_down):
    return (
        d_up == 1.0,
        d_mid == 0.0,
        d_down == 7.0,
        d_up == 3.0,
        d_mid == 4.0,
        d_down == 5.0,
        d_up == 2.0,
        d_down == 6.0,
    )


def inflow(masks, up, mid, down):
    e0, e1, e2, w0, w1, w2, s0, s1 = masks
    zero = jnp.zeros_like(up)
    east = jnp.where(e0, up, zero) + jnp.where(e1, mid, zero) + jnp.where(e2, down, zero)
    west = jnp.where(w0, up, zero) + jnp.where(w1, mid, zero) + jnp.where(w2, down, zero)
    same = jnp.where(s0, up, zero) + jnp.where(s1, down, zero)
    return same + pltpu.roll(east, 1, 1) + pltpu.roll(west, 127, 1)


def outflow(h, liquid, orate, land, channel, lrate, ice, per_pore):
    q = orate * h * (h / (h + 2.0))
    moving = [q * land]
    rest = [h - q]
    for k in range(LAYERS):
        sat = jnp.minimum((liquid[k] + ice[k]) * per_pore[k], math.sqrt(layer_speed[k]))
        lateral = (lrate * liquid[k]) * (sat * sat)
        moving.append(lateral)
        rest.append(liquid[k] - lateral)
    return moving, rest, q * channel


def settle(rest, arriving, room):
    h = rest[0] + arriving[0]
    liquid = []
    for k in range(LAYERS):
        u = rest[1 + k] + arriving[1 + k]
        h = h + jnp.maximum(u - room[k], 0.0)
        liquid.append(jnp.minimum(u, room[k]))
    return h, liquid


def kernel(
    nr,
    nc,
    rain_h,
    infil_h,
    por_h,
    liq_h,
    ice_h,
    dir_h,
    kind_h,
    orate_h,
    lrate_h,
    weight_h,
    out_liq,
    out_h,
    out_c,
    rain,
    infil,
    por,
    liq,
    ice,
    dir_v,
    kind_v,
    orate_v,
    lrate_v,
    weight_v,
    same_block_v,
    to_block_v,
    nat,
    share_v,
    stat,
    dirs,
    coarse,
    moving,
    rest,
    sums,
    sstat,
    schannel,
    enter,
    zsend,
    zrecv,
    vsend,
    vrecv,
    csend,
    crecv,
    hsend,
    hrecv,
    bsend,
    brecv,
    in_sem,
    zs_sem,
    zh_sem,
    zr_sem,
    vs_sem,
    vr_sem,
    cs_sem,
    cr_sem,
    hs_sem,
    hr_sem,
    bs_sem,
    br_sem,
    row_sem,
    relay_sem,
    late_sem,
):
    mi = lax.axis_index("rows")
    mj = lax.axis_index("cols")
    has_up, has_down = mi > 0, mi < nr - 1
    has_left, has_right = mj > 0, mj < nc - 1

    barrier = pltpu.get_barrier_semaphore()
    lead = nc - 2
    is_lead = mj == lead

    def tell(i, j):
        pl.semaphore_signal(barrier, inc=1, device_id=(i, j), device_id_type=MESH)

    @pl.when(jnp.logical_not(is_lead))
    def _():
        tell(mi, lead)

    copies = [
        pltpu.make_async_copy(src, dst, in_sem.at[n])
        for n, (src, dst) in enumerate(
            (
                (rain_h, rain),
                (infil_h, infil),
                (por_h, por),
                (liq_h, liq),
                (ice_h, ice),
                (weight_h, weight_v),
                (dir_h, dir_v),
                (kind_h, kind_v),
                (orate_h, orate_v),
                (lrate_h, lrate_v),
            )
        )
    ]
    for copy in copies:
        copy.start()

    sides = (
        (has_up, mi - 1, has_left, has_right, nc - 1),
        (has_down, mi + 1, has_left, has_right, 0),
    )
    late = (lax.rem(mi, 4) == 3) & has_down
    late_side = (has_up & (lax.rem(mi, 4) != 0), late)
    early_side = (has_up & (lax.rem(mi, 4) == 0), has_down & (lax.rem(mi, 4) != 3))
    own_end = (0, nc - 1)

    def partners(v, signal):
        has, i, left, right, end = sides[v]
        signal(i, end)
        signal(i, mj)

        @pl.when(left)
        def _():
            signal(i, mj - 1)

        @pl.when(right)
        def _():
            signal(i, mj + 1)

        @pl.when(mj == own_end[v])
        def _():
            @pl.loop(0, nc)
            def _(k):
                signal(i, k)

    def count(v):
        one = 2 + has_left.astype(jnp.int32) + has_right.astype(jnp.int32)
        return one + nc * (mj == own_end[v]).astype(jnp.int32)

    def tell_late_one(i, j):
        @pl.when(j != lead)
        def _():
            tell(i, j)

    for v in range(2):

        @pl.when(early_side[v])
        def _(v=v):
            partners(v, tell_late_one)

    @pl.when(is_lead)
    def _():
        pl.semaphore_wait(barrier, nc - 1)
        near = [lead - 1, lead + 1]
        for k in near + [k for k in others(lead) if k not in near]:
            pl.semaphore_signal(row_sem, inc=1, device_id=(mi, k), device_id_type=MESH)

    row_c, col_c = iota((W, W), 0), iota((W, W), 1)
    same_block = (tenth(row_c) == tenth(col_c)) & (row_c < TILE) & (col_c < TILE)
    same_block_v[...] = jnp.where(same_block, 1.0, 0.0).astype(jnp.bfloat16)
    row_p, col_p = iota((128, 128), 0), iota((128, 128), 1)
    to_block = []
    for at, end, shift in ((3, 113, 0), (3, 53, 11), (3, 113, 5)):
        mine = (row_p >= at) & (row_p < end) & (tenth(row_p + 7) == col_p + 1 - shift)
        if shift == 11:
            mine = mine | ((row_p >= 59) & (row_p < 109) & (tenth(row_p - 49) == col_p + 1))
        to_block.append(jnp.where(mine, 1.0, 0.0).astype(jnp.bfloat16))
    to_block_v[...] = jnp.concatenate(to_block, 0)

    lane = iota((8, 128), 1)
    lane16 = iota((CR, 128), 1)
    sub16 = iota((CR, 128), 0)

    def piece(k, i, s, send, arrive):
        return pltpu.make_async_remote_copy(
            src_ref=zsend.at[k],
            dst_ref=zrecv.at[s],
            send_sem=send,
            recv_sem=arrive,
            device_id=(i, k),
            device_id_type=MESH,
        )

    def row_pieces():
        return pltpu.make_async_remote_copy(
            src_ref=zsend.at[: nc - 1],
            dst_ref=zrecv.at[: nc - 1],
            send_sem=zs_sem,
            recv_sem=zr_sem.at[0],
            device_id=(mi, mj),
            device_id_type=MESH,
        )

    first_up = has_up & (mj == 0)
    last_down = has_down & (mj == nc - 1)

    def first_run(a):
        return pltpu.roll(a, HALO, 1)

    def second_run(a, b):
        return jnp.where(lane16 < 21, pltpu.roll(a, 21, 1), pltpu.roll(b, 21, 1))

    def third_run(a):
        return pltpu.roll(a, 59, 1)

    def fourth_run(a, b):
        return jnp.where(lane16 < 81, pltpu.roll(a, 81, 1), pltpu.roll(b, 81, 1))

    def rows_of(f, rr):
        return [nat.at[2 * f + half][pl.ds(rr, CR, stride=REFINE), :] for half in range(2)]

    def field(f):
        return (dirs, ROWS) if f == DIR else (stat.at[f], 0)

    def vertical(v, i):
        return pltpu.make_async_remote_copy(
            src_ref=vsend.at[v],
            dst_ref=vrecv.at[v],
            send_sem=vs_sem.at[v],
            recv_sem=vr_sem.at[v],
            device_id=(i, mj),
            device_id_type=MESH,
        )

    def corner(v, s, i, j):
        return pltpu.make_async_remote_copy(
            src_ref=csend.at[v, s],
            dst_ref=crecv.at[v, s],
            send_sem=cs_sem.at[v, s],
            recv_sem=cr_sem.at[v, s],
            device_id=(i, j),
            device_id_type=MESH,
        )

    incoming = sum(late_side[v].astype(jnp.int32) * count(v) for v in range(2))

    any_late = late_side[0] | late_side[1]
    passes_on = (mj == lead - 1) | (mj == lead + 1)

    def rows_ready():
        pl.semaphore_wait(barrier, incoming)

    def pass_on():
        pl.semaphore_signal(relay_sem, inc=1, device_id=(mi, lead), device_id_type=MESH)

    def send_ends(v):
        @pl.when(mj == own_end[v])
        def _():
            @pl.loop(0, nc)
            def _(k):
                piece(k, sides[v][1], CR + v, zh_sem, zr_sem.at[1 + v]).start()

    def send_rows(v):
        _, i, left, right, _ = sides[v]
        vertical(v, i).start()

        @pl.when(left)
        def _():
            corner(v, 0, i, mj - 1).start()

        @pl.when(right)
        def _():
            corner(v, 1, i, mj + 1).start()

    def tell_early(v):
        def signal(i, j):
            pl.semaphore_signal(late_sem.at[1 - v], inc=1, device_id=(i, j), device_id_type=MESH)

        partners(v, signal)

    def coarse_part():
        for copy in copies[:5]:
            copy.wait()
        rain_x, por_x = rain[...], por[...]
        top_sat = (liq[0] + ice[0]) / por_x
        capacity = infil[...] * jnp.maximum(1.0 - top_sat, 0.1)
        excess = rain_x * rain_x / (rain_x + capacity)
        top = liq[0] + (rain_x - excess) / (1000.0 * thickness[0])
        strip = [excess, por_x, top] + [liq[k] for k in range(1, LAYERS)] + [ice[k] for k in range(LAYERS)]

        slot = lax.shift_right_logical(lane * 2731, 16)
        t = lane - slot * 24
        for half in range(2):
            base = (iota((8, 128), 0) + 8 * half) * 16 - 1 + t
            inside = jnp.clip(base, 0, W - 1)
            index = inside & 127
            low = inside < 128
            for group in range(2):
                packed = jnp.zeros((8, 128), jnp.float32)
                for n in range(5):
                    x = strip[group * 5 + n]
                    a = jnp.broadcast_to(x[:, :128], (8, 128))
                    b = jnp.broadcast_to(x[:, 128:], (8, 128))
                    packed = jnp.where(slot == n, jnp.where(low, take(a, index), take(b, index)), packed)
                for s in range(8):
                    zsend[8 * half + s, :, 128 * group : 128 * group + 128] = packed[s : s + 1]

        zrecv[mj] = zsend[mj]

        @pl.when(jnp.logical_not(has_down))
        def _():
            zrecv[CR] = zsend[mj]

        @pl.when(jnp.logical_not(has_up))
        def _():
            zrecv[CR + 1] = zsend[mj]

    def tile_arrived():
        for copy in copies[5:]:
            copy.wait()

    def vertical_part():
        no_lanes = jnp.zeros((CR, 96), jnp.float32)

        def in_halves(x):
            return x[:, :128], jnp.concatenate([x[:, 128:], no_lanes[: x.shape[0]]], 1)

        edges, totals = [], []
        for v in range(2):
            r = v * (TILE - CR)
            kind_x = kind_v[r : r + CR]
            edge = [
                dir_v[r : r + CR].astype(jnp.float32),
                jnp.where(kind_x == 2, 0.0, orate_v[r : r + CR].astype(jnp.float32)),
                jnp.where(kind_x == 0, 1.0, 0.0),
                lrate_v[r : r + CR].astype(jnp.float32),
                weight_v[r : r + CR].astype(jnp.float32),
            ]
            edge = [in_halves(x) for x in edge]
            mine = sub16 >= CR - REFINE if v else sub16 < REFINE
            total = [jnp.sum(jnp.where(mine, x, 0.0), 0, keepdims=True) for x in edge[SHARE]]
            edges.append(edge)
            totals.append(jnp.concatenate(total, 1))
        totals.append(jnp.zeros((6, W), jnp.float32))
        per_mean = 100.0 / jnp.where(iota((8, W), 1) < TILE, dot3(jnp.concatenate(totals, 0), same_block_v[...]), 1.0)
        place = lane16 - HALO * sub16
        for v in (1, 0):
            r = v * (CR - HALO)
            for half in range(2):
                scale = per_mean[v : v + 1, 128 * half : 128 * half + 128]
                for f in range(FIELDS):
                    x = edges[v][f][half][r : r + HALO]
                    vsend[v, half, HALO * f : HALO * f + HALO] = x * scale if f == SHARE else x
                vsend[v, half, HALO * FIELDS :] = jnp.zeros((1, 128), jnp.float32)
            a, b = vsend[v, 0], vsend[v, 1]
            if v == 0:
                vsend[v, 0], vsend[v, 1] = third_run(a), fourth_run(a, b)
            else:
                vsend[v, 0], vsend[v, 1] = first_run(a), second_run(a, b)
            for n, (x, at) in enumerate(((a, 0), (b, 29))):
                end = jnp.where((place >= 0) & (place < HALO), take(x, jnp.clip(place + at, 0, 127)), 0.0)
                csend[v, n] = jnp.sum(end, 0, keepdims=True)

    def tile_part():
        kind_x = kind_v[...]
        natural = (
            dir_v[...].astype(jnp.float32),
            jnp.where(kind_x == 2, 0.0, orate_v[...].astype(jnp.float32)),
            jnp.where(kind_x == 0, 1.0, 0.0),
            lrate_v[...].astype(jnp.float32),
            weight_v[...].astype(jnp.float32),
            jnp.where(kind_x == 1, 1.0, 0.0),
        )
        no_lanes = jnp.zeros((TILE, 96), jnp.float32)
        for f in range(FIELDS + 1):
            nat[2 * f] = natural[f][:, :128]
            nat[2 * f + 1] = jnp.concatenate([natural[f][:, 128:], no_lanes], 1)

        weights = [rows_of(SHARE, rr) for rr in range(REFINE)]
        total = [functools.reduce(lambda a, b: a + b, [w[half] for w in weights]) for half in range(2)]
        block_sum = dot3(jnp.concatenate(total, 1), same_block_v[...])
        per_mean = 100.0 / jnp.where(iota((CR, W), 1) < TILE, block_sum, 1.0)
        shares = [[w[half] * per_mean[:, 128 * half : 128 * half + 128] for half in range(2)] for w in weights]
        for rr in range(REFINE):
            for half in range(2):
                share_v[2 * rr + half] = shares[rr][half]

    def send_pieces():
        for k in others(mj):
            piece(k, mi, mj, zs_sem, zr_sem.at[0]).start()

    def meet_early():
        @pl.when(passes_on)
        def _():
            pl.semaphore_wait(row_sem, 1)

        @pl.when(jnp.logical_not(is_lead))
        def _():
            rows_ready()

        @pl.when(passes_on)
        def _():
            pass_on()

        @pl.when(is_lead)
        def _():
            pl.semaphore_wait(relay_sem, 2)

        for v in (1, 0):

            @pl.when(late_side[v])
            def _(v=v):
                tell_early(v)

    def send_late():
        for v in (1, 0):

            @pl.when(late_side[v])
            def _(v=v):
                send_rows(v)

    @pl.when(late)
    def _():
        tile_arrived()
        vertical_part()
        meet_early()
        send_late()

    coarse_part()

    @pl.when(late)
    def _():
        send_ends(1)
        send_ends(0)

    @pl.when(is_lead)
    def _():
        send_pieces()

    @pl.when(jnp.logical_not(late))
    def _():
        tile_arrived()

    tile_part()

    @pl.when(any_late & jnp.logical_not(late))
    def _():
        meet_early()
        send_ends(0)

    shares = [[share_v[2 * rr + half] for half in range(2)] for rr in range(REFINE)]

    def slab_place(rr, f):
        n = rr * FIELDS + f
        return n // 18, HALO * (n % 9) + 64 * (n % 18 // 9)

    slabs = [jnp.zeros((CR, 128), jnp.float32)] * 3
    for rr in range(REFINE):
        for f in range(FIELDS):
            a, b = shares[rr] if f == SHARE else rows_of(f, rr)
            x = jnp.where(lane16 < HALO, a, jnp.where((lane16 >= 29) & (lane16 < 32), b, 0.0))
            n, at = slab_place(rr, f)
            slabs[n] = slabs[n] + (pltpu.roll(x, at, 1) if at else x)
    for n in range(3):
        hsend[n] = slabs[n]

    def sideways(n, j):
        return pltpu.make_async_remote_copy(
            src_ref=hsend,
            dst_ref=hrecv.at[n],
            send_sem=hs_sem.at[n],
            recv_sem=hr_sem.at[n],
            device_id=(mi, j),
            device_id_type=MESH,
        )

    @pl.when(jnp.logical_not(is_lead))
    def _():
        @pl.when(jnp.logical_not(any_late & passes_on))
        def _():
            pl.semaphore_wait(row_sem, 1)

        send_pieces()

    @pl.when(has_left)
    def _():
        sideways(0, mj - 1).start()

    @pl.when(has_right)
    def _():
        sideways(1, mj + 1).start()

    @pl.when(jnp.logical_not(late))
    def _():
        vertical_part()
        send_late()

    for p in range(PAIRS):
        for f in range(FIELDS + 1):
            if f == SHARE:
                (a, b), (c, d) = shares[p], shares[p + PAIRS]
            else:
                (a, b), (c, d) = rows_of(f, p), rows_of(f, p + PAIRS)
            ref, off = field(f)
            r = off + p * ROWS
            ref[r : r + CR] = first_run(a)
            ref[r + CR : r + 2 * CR] = jnp.where(lane16 < SPLIT, second_run(a, b), third_run(c))
            ref[r + 2 * CR : r + ROWS] = fourth_run(c, d)

    def strip_own(f, v, out):
        ref, off = field(f)
        for half in range(2):
            at = 8 * half + (0 if v else HALO)
            r = off + (v + half) * CR + v * (CR - 1)
            out[at : at + PAIRS] = ref[pl.ds(r, PAIRS, stride=ROWS), :]

    lane8, sub8 = iota((8, 128), 1), iota((8, 128), 0)
    schannel[...] = jnp.zeros(schannel.shape, jnp.float32)
    for v in range(2):
        strip_own(CHANNEL, v, schannel.at[v])

    row48, lane48 = iota((ROWS, 128), 0), iota((ROWS, 128), 1)
    in_first = (row48 == 0) | ((row48 == CR) & (lane48 < SPLIT))
    in_last = (row48 == ROWS - 1) | ((row48 == 2 * CR - 1) & (lane48 >= SPLIT))
    for p in range(PAIRS):
        out = in_first if p < 2 else in_last if p > 2 else in_first | in_last
        r = p * ROWS
        stat[CHANNEL, r : r + ROWS] = jnp.where(out, 0.0, stat[CHANNEL, r : r + ROWS])

    def send_early(v):
        @pl.when(early_side[v])
        def _():
            pl.semaphore_wait(late_sem.at[v], count(v))
            send_rows(v)
            send_ends(v)

    send_early(1)

    for v, (has, i, left, right, end) in enumerate(sides):

        @pl.when(jnp.logical_not(has))
        def _(v=v):
            vrecv[1 - v] = jnp.zeros(vrecv.shape[1:], jnp.float32)

        @pl.when(jnp.logical_not(has & left))
        def _(v=v):
            crecv[1 - v, 1] = jnp.zeros((1, 128), jnp.float32)

        @pl.when(jnp.logical_not(has & right))
        def _(v=v):
            crecv[1 - v, 0] = jnp.zeros((1, 128), jnp.float32)

    @pl.when(jnp.logical_not(has_right))
    def _():
        hrecv[0] = jnp.zeros(hrecv.shape[1:], jnp.float32)

    @pl.when(jnp.logical_not(has_left))
    def _():
        hrecv[1] = jnp.zeros(hrecv.shape[1:], jnp.float32)

    def columns(n):
        lanes = iota((n, 128), 1)
        return (
            tenth(lanes + 7),
            tenth(jnp.where(lanes < SPLIT, lanes + 117, lanes - 49)),
            jnp.minimum(tenth(lanes + 57), 17),
        )

    def layers_of(wide):
        por_w = wide[1]
        liquid, ice_w, room, per_pore = [], [], [], []
        for k in range(LAYERS):
            depth = 1000.0 * thickness[k]
            liquid.append(wide[2 + k] * depth)
            ice_w.append(wide[2 + LAYERS + k] * depth)
            room.append((por_w - wide[2 + LAYERS + k]) * depth)
            per_pore.append((math.sqrt(layer_speed[k]) / depth) / por_w)
        return liquid, ice_w, room, per_pore

    @pl.when(has_right)
    def _():
        sideways(0, mj).wait_recv()

    @pl.when(has_left)
    def _():
        sideways(1, mj).wait_recv()

    def span(at):
        return (lane16 >= at) & (lane16 < at + HALO)

    for p in range(PAIRS):
        for f in range(FIELDS):
            ref, off = field(f)
            r = off + p * ROWS
            for rr, (left_row, left_at), (right_row, right_at) in (
                (p, (r, 0), (r + CR, SPLIT - HALO)),
                (p + PAIRS, (r + CR, SPLIT), (r + 2 * CR, 113)),
            ):
                n, at = slab_place(rr, f)
                from_left = pltpu.roll(hrecv[1, n], (left_at - 29 - at) % 128, 1)
                from_right = pltpu.roll(hrecv[0, n], (right_at - at) % 128, 1)
                ref[left_row : left_row + CR] = jnp.where(
                    span(left_at), from_left, ref[left_row : left_row + CR]
                )
                ref[right_row : right_row + CR] = jnp.where(
                    span(right_at), from_right, ref[right_row : right_row + CR]
                )

    END = ROWS * (PAIRS + 1)
    sub_up = functools.partial(pltpu.roll, shift=1, axis=0)

    def sub_down(x):
        return pltpu.roll(x, x.shape[0] - 1, 0)

    def across(x):
        x0, x1, x2 = x[:CR], x[CR : 2 * CR], x[2 * CR :]
        return (
            jnp.where(lane16 < 53, pltpu.roll(x1, 72, 1), pltpu.roll(x2, 50, 1)),
            pltpu.roll(x2, 68, 1),
            pltpu.roll(x0, SPLIT, 1),
            jnp.where(lane16 < 63, pltpu.roll(x0, 78, 1), pltpu.roll(x1, 60, 1)),
        )

    def wrap(ref):
        a, b, c, d = across(ref[END - ROWS : END])
        ref[:CR] = sub_up(a)
        ref[CR : 2 * CR] = jnp.where(lane16 < SPLIT, sub_up(b), c)
        ref[2 * CR : ROWS] = d
        a, b, c, d = across(ref[ROWS : 2 * ROWS])
        ref[END : END + CR] = a
        ref[END + CR : END + 2 * CR] = jnp.where(lane16 < SPLIT, b, sub_down(c))
        ref[END + 2 * CR :] = sub_down(d)

    wrap(dirs)
    sums[...] = jnp.zeros(sums.shape, jnp.float32)

    row_pieces().wait_recv()

    def rows_at(group, slots):
        return jnp.concatenate([zrecv[n, :, 128 * group : 128 * group + 128] for n in slots], 0)

    packed_rows = [rows_at(g, range(CR)) for g in range(2)]
    wide = [
        jnp.concatenate([take(packed_rows[f // 5], c + 24 * (f % 5)) for c in columns(CR)], 0) for f in range(COARSE)
    ]
    liquid_w, ice_w, room, per_pore = layers_of(wide)
    for n, x in enumerate(ice_w + room + per_pore + liquid_w + wide[:1]):
        coarse[n] = x

    def finish(b, step):
        top, bottom = ROWS + HALO * ROWS, ROWS + ROWS + CR - 1
        for f in range(FIELDS):
            wrap(moving.at[b, f])
            enter[step, 0, f, 6:7] = moving[b, f, top : top + 1]
            enter[step, 0, f, 14:15] = moving[b, f, top + CR : top + CR + 1]
            enter[step, 1, f, 1:2] = moving[b, f, bottom + CR : bottom + CR + 1]
            enter[step, 1, f, 9:10] = moving[b, f, bottom + 2 * CR : bottom + 2 * CR + 1]

    def main_in(b, r, c):
        masks = inflow_masks(*[dirs[pl.ds(r + n * ROWS, CR), :] for n in range(3)])
        arriving = [
            inflow(masks, *[moving[b, f, pl.ds(r + n * ROWS, CR), :] for n in range(3)])
            for f in range(FIELDS)
        ]
        left = [rest[f, pl.ds(r, CR), :] for f in range(FIELDS)]
        return settle(left, arriving, [coarse[LAYERS + k, c : c + CR] for k in range(LAYERS)])

    def main_out(b, r, c, h, liquid):
        move, left, taken = outflow(
            h,
            liquid,
            stat[ORATE, pl.ds(r, CR), :],
            stat[LAND, pl.ds(r, CR), :],
            stat[CHANNEL, pl.ds(r, CR), :],
            stat[LRATE, pl.ds(r, CR), :],
            [coarse[k, c : c + CR] for k in range(LAYERS)],
            [coarse[2 * LAYERS + k, c : c + CR] for k in range(LAYERS)],
        )
        for f in range(FIELDS):
            moving[b, f, pl.ds(r + ROWS, CR), :] = move[f]
            rest[f, pl.ds(r, CR), :] = left[f]
        sums[LAYERS + 1, c : c + CR] += taken

    def row_at(p, c):
        return p * ROWS + c

    for c in range(0, ROWS, CR):
        liquid = [coarse[3 * LAYERS + k, c : c + CR] for k in range(LAYERS)]
        drain = []
        for k in range(LAYERS):
            sat = (liquid[k] + coarse[k, c : c + CR]) * coarse[2 * LAYERS + k, c : c + CR]
            sat = jnp.minimum(sat, math.sqrt(layer_speed[k]))
            drain.append(liquid[k] * (sat * sat))
        taken_c = jnp.zeros((CR, 128), jnp.float32)
        for p in OUTER_FIRST:
            r = row_at(p, c)
            h = coarse[4 * LAYERS, c : c + CR] * stat[SHARE, r : r + CR]
            q = stat[ORATE, r : r + CR] * h * (h / (h + 2.0))
            moving[0, 0, r + ROWS : r + ROWS + CR] = q * stat[LAND, r : r + CR]
            rest[0, r : r + CR] = h - q
            taken_c = taken_c + q * stat[CHANNEL, r : r + CR]
            for k in range(LAYERS):
                lateral = stat[LRATE, r : r + CR] * drain[k]
                moving[0, 1 + k, r + ROWS : r + ROWS + CR] = lateral
                rest[1 + k, r : r + CR] = liquid[k] - lateral
        sums[LAYERS + 1, c : c + CR] = taken_c

    finish(0, 0)

    for b in range(2):

        for p in INNER_FIRST:
            for c in range(0, ROWS, CR):
                r = row_at(p, c)
                main_out(1 - b, r, c, *main_in(b, r, c))

        finish(1 - b, 1 + b)

    for p in INNER_FIRST:
        for c in range(0, ROWS, CR):
            h, liquid = main_in(0, row_at(p, c), c)
            out = [in_first[c : c + CR]] * (p < HALO and c < 2 * CR) + [in_last[c : c + CR]] * (p >= PAIRS - HALO and c > 0)
            for n, x in enumerate(liquid + [h]):
                for mine in out:
                    x = jnp.where(mine, 0.0, x)
                sums[n, c : c + CR] += x

    scales = [0.01 / (1000.0 * x) for x in thickness] + [0.01, 0.01]

    def three(n):
        return jnp.concatenate([sums[n, c : c + CR] for c in range(0, ROWS, CR)], 1) * scales[n]

    means = dot2(jnp.concatenate([three(n) for n in range(LAYERS + 2)], 0), to_block_v[...])
    back = means[:CR]
    for n in range(1, LAYERS + 2):
        back = back + pltpu.roll(means[n * CR : (n + 1) * CR], 16 * n, 1)
    for s in range(1, CR - 1):
        bsend[s] = back[s : s + 1]

    def answer(k, s):
        return pltpu.make_async_remote_copy(
            src_ref=bsend.at[k],
            dst_ref=brecv.at[s],
            send_sem=bs_sem,
            recv_sem=br_sem,
            device_id=(mi, k),
            device_id_type=MESH,
        )

    def answers():
        return pltpu.make_async_remote_copy(
            src_ref=bsend.at[: nc - 1],
            dst_ref=brecv.at[: nc - 1],
            send_sem=bs_sem,
            recv_sem=br_sem,
            device_id=(mi, mj),
            device_id_type=MESH,
        )

    for k in others(mj):

        @pl.when((k != 0) & (k != nc - 1))
        def _(k=k):
            answer(k, mj).start()

    def strip(v):
        has, _, left, right, _ = sides[v]
        for f in range(FIELDS):
            strip_own(f, v, sstat.at[f])

        @pl.when(has)
        def _():
            vertical(1 - v, mi).wait_recv()
            piece(0, mi, CR + 1 - v, zh_sem, zr_sem.at[2 - v]).wait_recv()

        @pl.when(has & left)
        def _():
            corner(1 - v, 1, mi, mj).wait_recv()

        @pl.when(has & right)
        def _():
            corner(1 - v, 0, mi, mj).wait_recv()

        halo, far = vrecv.at[1 - v], (PAIRS if v else 0)
        for half, at in enumerate((SPLIT, 113) if v else (0, SPLIT - HALO)):
            index = jnp.clip(HALO * sub16 + lane16 - at, 0, 127)
            side = take(jnp.broadcast_to(crecv[1 - v, 1 - half], (CR, 128)), index)
            halo[half] = jnp.where(span(at), side, halo[half])
        for f in range(FIELDS):
            for half in range(2):
                at = 8 * half + far
                sstat[f, at : at + HALO] = halo[half, HALO * f : HALO * f + HALO]

        sub = sub8 >= PAIRS if v else sub8 < HALO
        groups = [
            jnp.where(sub, zrecv[CR + 1 - v, :, at : at + 128], zrecv[v * (CR - 1), :, at : at + 128])
            for at in (0, 128)
        ]
        tables = columns(8)[v : v + 2]
        wide = [jnp.concatenate([take(groups[f // 5], c + 24 * (f % 5)) for c in tables], 0) for f in range(COARSE)]
        liquid, ice_w, room, per_pore = layers_of(wide)
        sdir = sstat[DIR]
        masks = inflow_masks(sub_up(sdir), sdir, sub_down(sdir))
        entering = (sub16 & 7) == (1 if v else 6)
        h = wide[0] * sstat[SHARE]
        channel = jnp.zeros((CR, 128), jnp.float32)
        for step in range(3):
            move, rest_s, taken = outflow(
                h, liquid, sstat[ORATE], sstat[LAND], schannel[v], sstat[LRATE], ice_w, per_pore
            )
            channel = channel + taken
            move = [jnp.where(entering, enter[step, v, f], m) for f, m in enumerate(move)]
            arriving = [inflow(masks, sub_up(m), m, sub_down(m)) for m in move]
            h, liquid = settle(rest_s, arriving, room)

        first_row = 2 if v else HALO
        mine = ((sub16 & 7) >= first_row) & ((sub16 & 7) < first_row + HALO)
        mine = mine & ((sub16 >= 8) | (lane16 >= SPLIT)) if v else mine & ((sub16 < 8) | (lane16 < SPLIT))
        rows = []
        for n, x in enumerate(liquid + [h, channel]):
            x = jnp.where(mine, x, 0.0) * scales[n]
            rows.append(jnp.concatenate([jnp.sum(x[at : at + 8], 0, keepdims=True) for at in (0, 8)], 1))
        rows.append(jnp.zeros((2, 2 * 128), jnp.float32))
        part = dot2(jnp.concatenate(rows, 0), to_block_v[128 * v : 128 * v + 256])
        part = pltpu.roll(part, 0, 1, stride=16, stride_axis=0)
        s = v * (CR - 1)
        bsend[s] = back[s : s + 1] + jnp.sum(part, 0, keepdims=True)

        @pl.when(mj != s)
        def _():
            answer(s, mj).start()

    send_early(0)
    strip(0)
    strip(1)

    brecv[mj] = bsend[mj]

    row_pieces().wait_send()

    @pl.when(first_up | last_down)
    def _():
        pltpu.make_async_remote_copy(
            src_ref=zsend,
            dst_ref=zrecv.at[:nc],
            send_sem=zh_sem,
            recv_sem=zr_sem.at[1],
            device_id=(mi, mj),
            device_id_type=MESH,
        ).wait_send()

    for v, (has, i, left, right, end) in enumerate(sides):

        @pl.when(has)
        def _(v=v, i=i):
            vertical(v, i).wait_send()

        @pl.when(has & left)
        def _(v=v, i=i):
            corner(v, 0, i, mj - 1).wait_send()

        @pl.when(has & right)
        def _(v=v, i=i):
            corner(v, 1, i, mj + 1).wait_send()

    @pl.when(has_left)
    def _():
        sideways(0, mj - 1).wait_send()

    @pl.when(has_right)
    def _():
        sideways(1, mj + 1).wait_send()

    answers().wait_recv()

    gather = jnp.minimum(iota((8, 128), 0) * 16 + (lane & 15), 127)
    owner = lax.shift_right_logical(lane, 4)
    for half in range(2):
        out = jnp.zeros((8, 128), jnp.float32)
        for s in range(8):
            x = jnp.broadcast_to(brecv[8 * half + s], (8, 128))
            out = jnp.where(owner == s, take(x, gather), out)
        lanes = slice(128 * half, 128 * half + 128)
        for k in range(LAYERS):
            out_liq[k, :, lanes] = out[k : k + 1]
        out_h[:, lanes] = out[LAYERS : LAYERS + 1]
        out_c[:, lanes] = out[LAYERS + 1 : LAYERS + 2]

    answers().wait_send()


def store(a, b, c, out_a, out_b, out_c, sem):
    copies = [
        pltpu.make_async_copy(src, dst, sem.at[n])
        for n, (src, dst) in enumerate(((a, out_a), (b, out_b), (c, out_c)))
    ]
    for copy in copies:
        copy.start()
    for copy in copies:
        copy.wait()


def solution(mesh):
    nr, nc = mesh.shape["rows"], mesh.shape["cols"]
    f32, bf16 = jnp.float32, jnp.bfloat16

    def step(*args):
        v = pltpu.VMEM
        dma = pltpu.SemaphoreType.DMA
        args = [pltpu.with_memory_space_constraint(x, pltpu.HBM) for x in args]
        results = pl.pallas_call(
            functools.partial(kernel, nr, nc),
            out_shape=(v((LAYERS, 1, W), f32), v((1, W), f32), v((1, W), f32)),
            in_specs=[pl.BlockSpec(memory_space=pltpu.HBM)] * 10,
            out_specs=[pl.BlockSpec(memory_space=pltpu.VMEM)] * 3,
            scratch_shapes=[
                v((1, W), f32),
                v((1, W), f32),
                v((1, W), f32),
                v((LAYERS, 1, W), f32),
                v((LAYERS, 1, W), f32),
                v((TILE, TILE), jnp.int32),
                v((TILE, TILE), jnp.int32),
                v((TILE, TILE), bf16),
                v((TILE, TILE), bf16),
                v((TILE, TILE), bf16),
                v((W, W), bf16),
                v((3 * 128, 128), bf16),
                v((2 * FIELDS + 2, TILE, 128), f32),
                v((2 * REFINE, CR, 128), f32),
                v((FIELDS + 1, PAIRS * ROWS, 128), f32),
                v(((PAIRS + 2) * ROWS, 128), f32),
                v((4 * LAYERS + 1, ROWS, 128), f32),
                v((2, FIELDS, (PAIRS + 2) * ROWS, 128), f32),
                v((FIELDS, PAIRS * ROWS, 128), f32),
                v((LAYERS + 2, ROWS, 128), f32),
                v((FIELDS, CR, 128), f32),
                v((2, CR, 128), f32),
                v((3, 2, FIELDS, CR, 128), f32),
                v((CR, 1, W), f32),
                v((CR + 2, 1, W), f32),
                v((2, 2, CR, 128), f32),
                v((2, 2, CR, 128), f32),
                v((2, 2, 1, 128), f32),
                v((2, 2, 1, 128), f32),
                v((3, CR, 128), f32),
                v((2, 3, CR, 128), f32),
                v((CR, 1, 128), f32),
                v((CR, 1, 128), f32),
                dma((10,)),
                dma(()),
                dma(()),
                dma((3,)),
                dma((2,)),
                dma((2,)),
                dma((2, 2)),
                dma((2, 2)),
                dma((2,)),
                dma((2,)),
                dma(()),
                dma(()),
                pltpu.SemaphoreType.REGULAR,
                pltpu.SemaphoreType.REGULAR,
                pltpu.SemaphoreType.REGULAR((2,)),
            ],
            compiler_params=pltpu.CompilerParams(
                collective_id=0, has_side_effects=True, vmem_limit_bytes=62 * 1024 * 1024
            ),
        )(*args)
        return pl.pallas_call(
            store,
            out_shape=(
                jax.ShapeDtypeStruct((LAYERS, 1, W), f32),
                jax.ShapeDtypeStruct((1, W), f32),
                jax.ShapeDtypeStruct((1, W), f32),
            ),
            in_specs=[pl.BlockSpec(memory_space=pltpu.VMEM)] * 3,
            out_specs=[pl.BlockSpec(memory_space=pltpu.HBM)] * 3,
            scratch_shapes=[dma((3,))],
        )(*[pltpu.with_memory_space_constraint(x, pltpu.VMEM) for x in results])

    return jax.shard_map(
        step,
        mesh=mesh,
        in_specs=(
            P(("rows", "cols"), None),
            P(("rows", "cols"), None),
            P(("rows", "cols"), None),
            P(None, ("rows", "cols"), None),
            P(None, ("rows", "cols"), None),
            P("rows", "cols"),
            P("rows", "cols"),
            P("rows", "cols"),
            P("rows", "cols"),
            P("rows", "cols"),
        ),
        out_specs=(
            P(None, ("rows", "cols"), None),
            P(("rows", "cols"), None),
            P(("rows", "cols"), None),
        ),
        check_vma=False,
    )
```

```python
import functools
import math

import jax
import jax.numpy as jnp
from jax import lax
from jax.experimental import pallas as pl
from jax.experimental.pallas import tpu as pltpu
from jax.sharding import PartitionSpec as P

MESH = pl.DeviceIdType.MESH
REFINE = 10
LAYERS = 4
TILE = 160
CR = 16
W = 256
HALO = 3
PAIRS = REFINE // 2
INNER_FIRST = tuple(range(1, PAIRS - 1)) + (0, PAIRS - 1)
OUTER_FIRST = (0, PAIRS - 1) + tuple(range(1, PAIRS - 1))
ROWS = 3 * CR
SPLIT = 56

thickness = (0.1, 0.3, 0.6, 1.0)
layer_speed = (1.0, 0.8, 0.6, 0.4)

DIR, ORATE, LAND, LRATE, SHARE, CHANNEL = range(6)
FIELDS = 5
COARSE = 10


FAR_FIRST = sorted(
    ((z, y, c) for z in range(2) for y in range(4) for c in range(2) if z + y + c),
    key=lambda p: -(p[0] + min(p[1], 4 - p[1])),
)


def others(j):
    z, y, c = j // 8, (j // 2) % 4, j % 2
    return [((z + dz) % 2) * 8 + ((y + dy) % 4) * 2 + (c + dc) % 2 for dz, dy, dc in FAR_FIRST]


def iota(shape, dim):
    return lax.broadcasted_iota(jnp.int32, shape, dim)


def take(x, index):
    return jnp.take_along_axis(x, index, axis=1, mode="promise_in_bounds")


def tenth(x):
    return lax.shift_right_logical(x * 6554, 16)


def split3(x):
    hi = x.astype(jnp.bfloat16)
    r = x - hi.astype(jnp.float32)
    mid = r.astype(jnp.bfloat16)
    lo = (r - mid.astype(jnp.float32)).astype(jnp.bfloat16)
    return jnp.concatenate([hi, mid, lo], 0)


def split2(x):
    hi = x.astype(jnp.bfloat16)
    lo = (x - hi.astype(jnp.float32)).astype(jnp.bfloat16)
    return jnp.concatenate([hi, lo], 0)


def dot3(x, ones):
    n = x.shape[0]
    y = jnp.dot(split3(x), ones, preferred_element_type=jnp.float32)
    return y[:n] + y[n : 2 * n] + y[2 * n :]


def dot2(x, ones):
    n = x.shape[0]
    y = jnp.dot(split2(x), ones, preferred_element_type=jnp.float32)
    return y[:n] + y[n:]


def inflow_masks(d_up, d_mid, d_down):
    return (
        d_up == 1.0,
        d_mid == 0.0,
        d_down == 7.0,
        d_up == 3.0,
        d_mid == 4.0,
        d_down == 5.0,
        d_up == 2.0,
        d_down == 6.0,
    )


def inflow(masks, up, mid, down):
    e0, e1, e2, w0, w1, w2, s0, s1 = masks
    zero = jnp.zeros_like(up)
    east = jnp.where(e0, up, zero) + jnp.where(e1, mid, zero) + jnp.where(e2, down, zero)
    west = jnp.where(w0, up, zero) + jnp.where(w1, mid, zero) + jnp.where(w2, down, zero)
    same = jnp.where(s0, up, zero) + jnp.where(s1, down, zero)
    return same + pltpu.roll(east, 1, 1) + pltpu.roll(west, 127, 1)


def outflow(h, liquid, orate, land, channel, lrate, ice, per_pore):
    q = orate * h * (h / (h + 2.0))
    moving = [q * land]
    rest = [h - q]
    for k in range(LAYERS):
        sat = jnp.minimum((liquid[k] + ice[k]) * per_pore[k], math.sqrt(layer_speed[k]))
        lateral = (lrate * liquid[k]) * (sat * sat)
        moving.append(lateral)
        rest.append(liquid[k] - lateral)
    return moving, rest, q * channel


def settle(rest, arriving, room):
    h = rest[0] + arriving[0]
    liquid = []
    for k in range(LAYERS):
        u = rest[1 + k] + arriving[1 + k]
        h = h + jnp.maximum(u - room[k], 0.0)
        liquid.append(jnp.minimum(u, room[k]))
    return h, liquid


def kernel(
    nr,
    nc,
    rain_h,
    infil_h,
    por_h,
    liq_h,
    ice_h,
    dir_h,
    kind_h,
    orate_h,
    lrate_h,
    weight_h,
    out_liq,
    out_h,
    out_c,
    rain,
    infil,
    por,
    liq,
    ice,
    dir_v,
    kind_v,
    orate_v,
    lrate_v,
    weight_v,
    same_block_v,
    to_block_v,
    nat,
    share_v,
    stat,
    dirs,
    coarse,
    moving,
    rest,
    sums,
    sstat,
    schannel,
    enter,
    zsend,
    zrecv,
    vsend,
    vrecv,
    csend,
    crecv,
    hsend,
    hrecv,
    bsend,
    brecv,
    in_sem,
    zs_sem,
    zh_sem,
    zr_sem,
    vs_sem,
    vr_sem,
    cs_sem,
    cr_sem,
    hs_sem,
    hr_sem,
    bs_sem,
    br_sem,
    row_sem,
    relay_sem,
    late_sem,
):
    mi = lax.axis_index("rows")
    mj = lax.axis_index("cols")
    has_up, has_down = mi > 0, mi < nr - 1
    has_left, has_right = mj > 0, mj < nc - 1

    barrier = pltpu.get_barrier_semaphore()
    lead = nc - 2
    is_lead = mj == lead

    def tell(i, j):
        pl.semaphore_signal(barrier, inc=1, device_id=(i, j), device_id_type=MESH)

    @pl.when(jnp.logical_not(is_lead))
    def _():
        tell(mi, lead)

    copies = [
        pltpu.make_async_copy(src, dst, in_sem.at[n])
        for n, (src, dst) in enumerate(
            (
                (rain_h, rain),
                (infil_h, infil),
                (por_h, por),
                (liq_h, liq),
                (ice_h, ice),
                (weight_h, weight_v),
                (dir_h, dir_v),
                (kind_h, kind_v),
                (orate_h, orate_v),
                (lrate_h, lrate_v),
            )
        )
    ]
    for copy in copies:
        copy.start()

    sides = (
        (has_up, mi - 1, has_left, has_right, nc - 1),
        (has_down, mi + 1, has_left, has_right, 0),
    )
    late = (lax.rem(mi, 4) == 3) & has_down
    late_side = (has_up & (lax.rem(mi, 4) != 0), late)
    early_side = (has_up & (lax.rem(mi, 4) == 0), has_down & (lax.rem(mi, 4) != 3))
    own_end = (0, nc - 1)

    def partners(v, signal):
        has, i, left, right, end = sides[v]
        signal(i, end)
        signal(i, mj)

        @pl.when(left)
        def _():
            signal(i, mj - 1)

        @pl.when(right)
        def _():
            signal(i, mj + 1)

        @pl.when(mj == own_end[v])
        def _():
            @pl.loop(0, nc)
            def _(k):
                signal(i, k)

    def count(v):
        one = 2 + has_left.astype(jnp.int32) + has_right.astype(jnp.int32)
        return one + nc * (mj == own_end[v]).astype(jnp.int32)

    def tell_late_one(i, j):
        @pl.when(j != lead)
        def _():
            tell(i, j)

    for v in range(2):

        @pl.when(early_side[v])
        def _(v=v):
            partners(v, tell_late_one)

    @pl.when(is_lead)
    def _():
        pl.semaphore_wait(barrier, nc - 1)
        near = [lead - 1, lead + 1]
        for k in near + [k for k in others(lead) if k not in near]:
            pl.semaphore_signal(row_sem, inc=1, device_id=(mi, k), device_id_type=MESH)

    row_c, col_c = iota((W, W), 0), iota((W, W), 1)
    same_block = (tenth(row_c) == tenth(col_c)) & (row_c < TILE) & (col_c < TILE)
    same_block_v[...] = jnp.where(same_block, 1.0, 0.0).astype(jnp.bfloat16)
    row_p, col_p = iota((128, 128), 0), iota((128, 128), 1)
    to_block = []
    for at, end, shift in ((3, 113, 0), (3, 53, 11), (3, 113, 5)):
        mine = (row_p >= at) & (row_p < end) & (tenth(row_p + 7) == col_p + 1 - shift)
        if shift == 11:
            mine = mine | ((row_p >= 59) & (row_p < 109) & (tenth(row_p - 49) == col_p + 1))
        to_block.append(jnp.where(mine, 1.0, 0.0).astype(jnp.bfloat16))
    to_block_v[...] = jnp.concatenate(to_block, 0)

    lane = iota((8, 128), 1)
    lane16 = iota((CR, 128), 1)
    sub16 = iota((CR, 128), 0)

    def piece(k, i, s, send, arrive):
        return pltpu.make_async_remote_copy(
            src_ref=zsend.at[k],
            dst_ref=zrecv.at[s],
            send_sem=send,
            recv_sem=arrive,
            device_id=(i, k),
            device_id_type=MESH,
        )

    def row_pieces():
        return pltpu.make_async_remote_copy(
            src_ref=zsend.at[: nc - 1],
            dst_ref=zrecv.at[: nc - 1],
            send_sem=zs_sem,
            recv_sem=zr_sem.at[0],
            device_id=(mi, mj),
            device_id_type=MESH,
        )

    first_up = has_up & (mj == 0)
    last_down = has_down & (mj == nc - 1)

    def first_run(a):
        return pltpu.roll(a, HALO, 1)

    def second_run(a, b):
        return jnp.where(lane16 < 21, pltpu.roll(a, 21, 1), pltpu.roll(b, 21, 1))

    def third_run(a):
        return pltpu.roll(a, 59, 1)

    def fourth_run(a, b):
        return jnp.where(lane16 < 81, pltpu.roll(a, 81, 1), pltpu.roll(b, 81, 1))

    def rows_of(f, rr):
        return [nat.at[2 * f + half][pl.ds(rr, CR, stride=REFINE), :] for half in range(2)]

    def field(f):
        return (dirs, ROWS) if f == DIR else (stat.at[f], 0)

    def vertical(v, i):
        return pltpu.make_async_remote_copy(
            src_ref=vsend.at[v],
            dst_ref=vrecv.at[v],
            send_sem=vs_sem.at[v],
            recv_sem=vr_sem.at[v],
            device_id=(i, mj),
            device_id_type=MESH,
        )

    def corner(v, s, i, j):
        return pltpu.make_async_remote_copy(
            src_ref=csend.at[v, s],
            dst_ref=crecv.at[v, s],
            send_sem=cs_sem.at[v, s],
            recv_sem=cr_sem.at[v, s],
            device_id=(i, j),
            device_id_type=MESH,
        )

    incoming = sum(late_side[v].astype(jnp.int32) * count(v) for v in range(2))

    any_late = late_side[0] | late_side[1]
    passes_on = (mj == lead - 1) | (mj == lead + 1)

    def rows_ready():
        pl.semaphore_wait(barrier, incoming)

    def pass_on():
        pl.semaphore_signal(relay_sem, inc=1, device_id=(mi, lead), device_id_type=MESH)

    def send_ends(v):
        @pl.when(mj == own_end[v])
        def _():
            @pl.loop(0, nc)
            def _(k):
                piece(k, sides[v][1], CR + v, zh_sem, zr_sem.at[1 + v]).start()

    def send_rows(v):
        _, i, left, right, _ = sides[v]
        vertical(v, i).start()

        @pl.when(left)
        def _():
            corner(v, 0, i, mj - 1).start()

        @pl.when(right)
        def _():
            corner(v, 1, i, mj + 1).start()

    def tell_early(v):
        def signal(i, j):
            pl.semaphore_signal(late_sem.at[1 - v], inc=1, device_id=(i, j), device_id_type=MESH)

        partners(v, signal)

    def coarse_part():
        for copy in copies[:5]:
            copy.wait()
        rain_x, por_x = rain[...], por[...]
        top_sat = (liq[0] + ice[0]) / por_x
        capacity = infil[...] * jnp.maximum(1.0 - top_sat, 0.1)
        excess = rain_x * rain_x / (rain_x + capacity)
        top = liq[0] + (rain_x - excess) / (1000.0 * thickness[0])
        strip = [excess, por_x, top] + [liq[k] for k in range(1, LAYERS)] + [ice[k] for k in range(LAYERS)]

        slot = lax.shift_right_logical(lane * 2731, 16)
        t = lane - slot * 24
        for half in range(2):
            base = (iota((8, 128), 0) + 8 * half) * 16 - 1 + t
            inside = jnp.clip(base, 0, W - 1)
            index = inside & 127
            low = inside < 128
            for group in range(2):
                packed = jnp.zeros((8, 128), jnp.float32)
                for n in range(5):
                    x = strip[group * 5 + n]
                    a = jnp.broadcast_to(x[:, :128], (8, 128))
                    b = jnp.broadcast_to(x[:, 128:], (8, 128))
                    packed = jnp.where(slot == n, jnp.where(low, take(a, index), take(b, index)), packed)
                for s in range(8):
                    zsend[8 * half + s, :, 128 * group : 128 * group + 128] = packed[s : s + 1]

        zrecv[mj] = zsend[mj]

        @pl.when(jnp.logical_not(has_down))
        def _():
            zrecv[CR] = zsend[mj]

        @pl.when(jnp.logical_not(has_up))
        def _():
            zrecv[CR + 1] = zsend[mj]

    def tile_arrived():
        for copy in copies[5:]:
            copy.wait()

    def vertical_part():
        no_lanes = jnp.zeros((CR, 96), jnp.float32)

        def in_halves(x):
            return x[:, :128], jnp.concatenate([x[:, 128:], no_lanes[: x.shape[0]]], 1)

        edges, totals = [], []
        for v in range(2):
            r = v * (TILE - CR)
            kind_x = kind_v[r : r + CR]
            edge = [
                dir_v[r : r + CR].astype(jnp.float32),
                jnp.where(kind_x == 2, 0.0, orate_v[r : r + CR].astype(jnp.float32)),
                jnp.where(kind_x == 0, 1.0, 0.0),
                lrate_v[r : r + CR].astype(jnp.float32),
                weight_v[r : r + CR].astype(jnp.float32),
            ]
            edge = [in_halves(x) for x in edge]
            mine = sub16 >= CR - REFINE if v else sub16 < REFINE
            total = [jnp.sum(jnp.where(mine, x, 0.0), 0, keepdims=True) for x in edge[SHARE]]
            edges.append(edge)
            totals.append(jnp.concatenate(total, 1))
        totals.append(jnp.zeros((6, W), jnp.float32))
        per_mean = 100.0 / jnp.where(iota((8, W), 1) < TILE, dot3(jnp.concatenate(totals, 0), same_block_v[...]), 1.0)
        place = lane16 - HALO * sub16
        for v in (1, 0):
            r = v * (CR - HALO)
            for half in range(2):
                scale = per_mean[v : v + 1, 128 * half : 128 * half + 128]
                for f in range(FIELDS):
                    x = edges[v][f][half][r : r + HALO]
                    vsend[v, half, HALO * f : HALO * f + HALO] = x * scale if f == SHARE else x
                vsend[v, half, HALO * FIELDS :] = jnp.zeros((1, 128), jnp.float32)
            a, b = vsend[v, 0], vsend[v, 1]
            if v == 0:
                vsend[v, 0], vsend[v, 1] = third_run(a), fourth_run(a, b)
            else:
                vsend[v, 0], vsend[v, 1] = first_run(a), second_run(a, b)
            for n, (x, at) in enumerate(((a, 0), (b, 29))):
                end = jnp.where((place >= 0) & (place < HALO), take(x, jnp.clip(place + at, 0, 127)), 0.0)
                csend[v, n] = jnp.sum(end, 0, keepdims=True)

    def tile_part():
        kind_x = kind_v[...]
        natural = (
            dir_v[...].astype(jnp.float32),
            jnp.where(kind_x == 2, 0.0, orate_v[...].astype(jnp.float32)),
            jnp.where(kind_x == 0, 1.0, 0.0),
            lrate_v[...].astype(jnp.float32),
            weight_v[...].astype(jnp.float32),
            jnp.where(kind_x == 1, 1.0, 0.0),
        )
        no_lanes = jnp.zeros((TILE, 96), jnp.float32)
        for f in range(FIELDS + 1):
            nat[2 * f] = natural[f][:, :128]
            nat[2 * f + 1] = jnp.concatenate([natural[f][:, 128:], no_lanes], 1)

        weights = [rows_of(SHARE, rr) for rr in range(REFINE)]
        total = [functools.reduce(lambda a, b: a + b, [w[half] for w in weights]) for half in range(2)]
        block_sum = dot3(jnp.concatenate(total, 1), same_block_v[...])
        per_mean = 100.0 / jnp.where(iota((CR, W), 1) < TILE, block_sum, 1.0)
        shares = [[w[half] * per_mean[:, 128 * half : 128 * half + 128] for half in range(2)] for w in weights]
        for rr in range(REFINE):
            for half in range(2):
                share_v[2 * rr + half] = shares[rr][half]

    def send_pieces():
        for k in others(mj):
            piece(k, mi, mj, zs_sem, zr_sem.at[0]).start()

    def meet_early():
        @pl.when(passes_on)
        def _():
            pl.semaphore_wait(row_sem, 1)

        @pl.when(jnp.logical_not(is_lead))
        def _():
            rows_ready()

        @pl.when(passes_on)
        def _():
            pass_on()

        @pl.when(is_lead)
        def _():
            pl.semaphore_wait(relay_sem, 2)

        for v in (1, 0):

            @pl.when(late_side[v])
            def _(v=v):
                tell_early(v)

    def send_late():
        for v in (1, 0):

            @pl.when(late_side[v])
            def _(v=v):
                send_rows(v)

    @pl.when(late)
    def _():
        tile_arrived()
        vertical_part()
        meet_early()
        send_late()

    coarse_part()

    @pl.when(late)
    def _():
        send_ends(1)
        send_ends(0)

    @pl.when(is_lead)
    def _():
        send_pieces()

    @pl.when(jnp.logical_not(late))
    def _():
        tile_arrived()

    tile_part()

    @pl.when(any_late & jnp.logical_not(late))
    def _():
        meet_early()
        send_ends(0)

    shares = [[share_v[2 * rr + half] for half in range(2)] for rr in range(REFINE)]

    def slab_place(rr, f):
        n = rr * FIELDS + f
        return n // 18, HALO * (n % 9) + 64 * (n % 18 // 9)

    slabs = [jnp.zeros((CR, 128), jnp.float32)] * 3
    for rr in range(REFINE):
        for f in range(FIELDS):
            a, b = shares[rr] if f == SHARE else rows_of(f, rr)
            x = jnp.where(lane16 < HALO, a, jnp.where((lane16 >= 29) & (lane16 < 32), b, 0.0))
            n, at = slab_place(rr, f)
            slabs[n] = slabs[n] + (pltpu.roll(x, at, 1) if at else x)
    for n in range(3):
        hsend[n] = slabs[n]

    def sideways(n, j):
        return pltpu.make_async_remote_copy(
            src_ref=hsend,
            dst_ref=hrecv.at[n],
            send_sem=hs_sem.at[n],
            recv_sem=hr_sem.at[n],
            device_id=(mi, j),
            device_id_type=MESH,
        )

    @pl.when(jnp.logical_not(is_lead))
    def _():
        @pl.when(jnp.logical_not(any_late & passes_on))
        def _():
            pl.semaphore_wait(row_sem, 1)

        send_pieces()

    @pl.when(has_left)
    def _():
        sideways(0, mj - 1).start()

    @pl.when(has_right)
    def _():
        sideways(1, mj + 1).start()

    @pl.when(jnp.logical_not(late))
    def _():
        vertical_part()
        send_late()

    for p in range(PAIRS):
        for f in range(FIELDS + 1):
            if f == SHARE:
                (a, b), (c, d) = shares[p], shares[p + PAIRS]
            else:
                (a, b), (c, d) = rows_of(f, p), rows_of(f, p + PAIRS)
            ref, off = field(f)
            r = off + p * ROWS
            ref[r : r + CR] = first_run(a)
            ref[r + CR : r + 2 * CR] = jnp.where(lane16 < SPLIT, second_run(a, b), third_run(c))
            ref[r + 2 * CR : r + ROWS] = fourth_run(c, d)

    def strip_own(f, v, out):
        ref, off = field(f)
        for half in range(2):
            at = 8 * half + (0 if v else HALO)
            r = off + (v + half) * CR + v * (CR - 1)
            out[at : at + PAIRS] = ref[pl.ds(r, PAIRS, stride=ROWS), :]

    lane8, sub8 = iota((8, 128), 1), iota((8, 128), 0)
    schannel[...] = jnp.zeros(schannel.shape, jnp.float32)
    for v in range(2):
        strip_own(CHANNEL, v, schannel.at[v])

    row48, lane48 = iota((ROWS, 128), 0), iota((ROWS, 128), 1)
    in_first = (row48 == 0) | ((row48 == CR) & (lane48 < SPLIT))
    in_last = (row48 == ROWS - 1) | ((row48 == 2 * CR - 1) & (lane48 >= SPLIT))
    for p in range(PAIRS):
        out = in_first if p < 2 else in_last if p > 2 else in_first | in_last
        r = p * ROWS
        stat[CHANNEL, r : r + ROWS] = jnp.where(out, 0.0, stat[CHANNEL, r : r + ROWS])

    def send_early(v):
        @pl.when(early_side[v])
        def _():
            pl.semaphore_wait(late_sem.at[v], count(v))
            send_rows(v)
            send_ends(v)

    send_early(1)

    for v, (has, i, left, right, end) in enumerate(sides):

        @pl.when(jnp.logical_not(has))
        def _(v=v):
            vrecv[1 - v] = jnp.zeros(vrecv.shape[1:], jnp.float32)

        @pl.when(jnp.logical_not(has & left))
        def _(v=v):
            crecv[1 - v, 1] = jnp.zeros((1, 128), jnp.float32)

        @pl.when(jnp.logical_not(has & right))
        def _(v=v):
            crecv[1 - v, 0] = jnp.zeros((1, 128), jnp.float32)

    @pl.when(jnp.logical_not(has_right))
    def _():
        hrecv[0] = jnp.zeros(hrecv.shape[1:], jnp.float32)

    @pl.when(jnp.logical_not(has_left))
    def _():
        hrecv[1] = jnp.zeros(hrecv.shape[1:], jnp.float32)

    def columns(n):
        lanes = iota((n, 128), 1)
        return (
            tenth(lanes + 7),
            tenth(jnp.where(lanes < SPLIT, lanes + 117, lanes - 49)),
            jnp.minimum(tenth(lanes + 57), 17),
        )

    def layers_of(wide):
        por_w = wide[1]
        liquid, ice_w, room, per_pore = [], [], [], []
        for k in range(LAYERS):
            depth = 1000.0 * thickness[k]
            liquid.append(wide[2 + k] * depth)
            ice_w.append(wide[2 + LAYERS + k] * depth)
            room.append((por_w - wide[2 + LAYERS + k]) * depth)
            per_pore.append((math.sqrt(layer_speed[k]) / depth) / por_w)
        return liquid, ice_w, room, per_pore

    @pl.when(has_right)
    def _():
        sideways(0, mj).wait_recv()

    @pl.when(has_left)
    def _():
        sideways(1, mj).wait_recv()

    def span(at):
        return (lane16 >= at) & (lane16 < at + HALO)

    for p in range(PAIRS):
        for f in range(FIELDS):
            ref, off = field(f)
            r = off + p * ROWS
            for rr, (left_row, left_at), (right_row, right_at) in (
                (p, (r, 0), (r + CR, SPLIT - HALO)),
                (p + PAIRS, (r + CR, SPLIT), (r + 2 * CR, 113)),
            ):
                n, at = slab_place(rr, f)
                from_left = pltpu.roll(hrecv[1, n], (left_at - 29 - at) % 128, 1)
                from_right = pltpu.roll(hrecv[0, n], (right_at - at) % 128, 1)
                ref[left_row : left_row + CR] = jnp.where(
                    span(left_at), from_left, ref[left_row : left_row + CR]
                )
                ref[right_row : right_row + CR] = jnp.where(
                    span(right_at), from_right, ref[right_row : right_row + CR]
                )

    END = ROWS * (PAIRS + 1)
    sub_up = functools.partial(pltpu.roll, shift=1, axis=0)

    def sub_down(x):
        return pltpu.roll(x, x.shape[0] - 1, 0)

    def across(x):
        x0, x1, x2 = x[:CR], x[CR : 2 * CR], x[2 * CR :]
        return (
            jnp.where(lane16 < 53, pltpu.roll(x1, 72, 1), pltpu.roll(x2, 50, 1)),
            pltpu.roll(x2, 68, 1),
            pltpu.roll(x0, SPLIT, 1),
            jnp.where(lane16 < 63, pltpu.roll(x0, 78, 1), pltpu.roll(x1, 60, 1)),
        )

    def wrap(ref):
        a, b, c, d = across(ref[END - ROWS : END])
        ref[:CR] = sub_up(a)
        ref[CR : 2 * CR] = jnp.where(lane16 < SPLIT, sub_up(b), c)
        ref[2 * CR : ROWS] = d
        a, b, c, d = across(ref[ROWS : 2 * ROWS])
        ref[END : END + CR] = a
        ref[END + CR : END + 2 * CR] = jnp.where(lane16 < SPLIT, b, sub_down(c))
        ref[END + 2 * CR : END + ROWS] = sub_down(d)

    wrap(dirs)
    sums[...] = jnp.zeros(sums.shape, jnp.float32)

    row_pieces().wait_recv()

    def rows_at(group, slots):
        return jnp.concatenate([zrecv[n, :, 128 * group : 128 * group + 128] for n in slots], 0)

    packed_rows = [rows_at(g, range(CR)) for g in range(2)]
    wide = [
        jnp.concatenate([take(packed_rows[f // 5], c + 24 * (f % 5)) for c in columns(CR)], 0) for f in range(COARSE)
    ]
    liquid_w, ice_w, room, per_pore = layers_of(wide)
    for n, x in enumerate(ice_w + room + per_pore + liquid_w + wide[:1]):
        coarse[n] = x

    def finish(b, step):
        top, bottom = ROWS + HALO * ROWS, ROWS + ROWS + CR - 1
        for f in range(FIELDS):
            wrap(moving.at[b, f])
            enter[step, 0, f, 6:7] = moving[b, f, top : top + 1]
            enter[step, 0, f, 14:15] = moving[b, f, top + CR : top + CR + 1]
            enter[step, 1, f, 1:2] = moving[b, f, bottom + CR : bottom + CR + 1]
            enter[step, 1, f, 9:10] = moving[b, f, bottom + 2 * CR : bottom + 2 * CR + 1]

    def main_in(b, r, c):
        masks = inflow_masks(*[dirs[pl.ds(r + n * ROWS, CR), :] for n in range(3)])
        arriving = [
            inflow(masks, *[moving[b, f, pl.ds(r + n * ROWS, CR), :] for n in range(3)])
            for f in range(FIELDS)
        ]
        left = [rest[f, pl.ds(r, CR), :] for f in range(FIELDS)]
        return settle(left, arriving, [coarse[LAYERS + k, c : c + CR] for k in range(LAYERS)])

    def main_out(b, r, c, h, liquid):
        move, left, taken = outflow(
            h,
            liquid,
            stat[ORATE, pl.ds(r, CR), :],
            stat[LAND, pl.ds(r, CR), :],
            stat[CHANNEL, pl.ds(r, CR), :],
            stat[LRATE, pl.ds(r, CR), :],
            [coarse[k, c : c + CR] for k in range(LAYERS)],
            [coarse[2 * LAYERS + k, c : c + CR] for k in range(LAYERS)],
        )
        for f in range(FIELDS):
            moving[b, f, pl.ds(r + ROWS, CR), :] = move[f]
            rest[f, pl.ds(r, CR), :] = left[f]
        sums[LAYERS + 1, c : c + CR] += taken

    def row_at(p, c):
        return p * ROWS + c

    for c in range(0, ROWS, CR):
        liquid = [coarse[3 * LAYERS + k, c : c + CR] for k in range(LAYERS)]
        drain = []
        for k in range(LAYERS):
            sat = (liquid[k] + coarse[k, c : c + CR]) * coarse[2 * LAYERS + k, c : c + CR]
            sat = jnp.minimum(sat, math.sqrt(layer_speed[k]))
            drain.append(liquid[k] * (sat * sat))
        taken_c = jnp.zeros((CR, 128), jnp.float32)
        for p in OUTER_FIRST:
            r = row_at(p, c)
            h = coarse[4 * LAYERS, c : c + CR] * stat[SHARE, r : r + CR]
            q = stat[ORATE, r : r + CR] * h * (h / (h + 2.0))
            moving[0, 0, r + ROWS : r + ROWS + CR] = q * stat[LAND, r : r + CR]
            rest[0, r : r + CR] = h - q
            taken_c = taken_c + q * stat[CHANNEL, r : r + CR]
            for k in range(LAYERS):
                lateral = stat[LRATE, r : r + CR] * drain[k]
                moving[0, 1 + k, r + ROWS : r + ROWS + CR] = lateral
                rest[1 + k, r : r + CR] = liquid[k] - lateral
        sums[LAYERS + 1, c : c + CR] = taken_c

    finish(0, 0)

    for b in range(2):

        for p in INNER_FIRST:
            for c in range(0, ROWS, CR):
                r = row_at(p, c)
                main_out(1 - b, r, c, *main_in(b, r, c))

        finish(1 - b, 1 + b)

    for p in INNER_FIRST:
        for c in range(0, ROWS, CR):
            h, liquid = main_in(0, row_at(p, c), c)
            out = [in_first[c : c + CR]] * (p < HALO and c < 2 * CR) + [in_last[c : c + CR]] * (p >= PAIRS - HALO and c > 0)
            for n, x in enumerate(liquid + [h]):
                for mine in out:
                    x = jnp.where(mine, 0.0, x)
                sums[n, c : c + CR] += x

    scales = [0.01 / (1000.0 * x) for x in thickness] + [0.01, 0.01]

    def three(n):
        return jnp.concatenate([sums[n, c : c + CR] for c in range(0, ROWS, CR)], 1) * scales[n]

    means = dot2(jnp.concatenate([three(n) for n in range(LAYERS + 2)], 0), to_block_v[...])
    back = means[:CR]
    for n in range(1, LAYERS + 2):
        back = back + pltpu.roll(means[n * CR : (n + 1) * CR], 16 * n, 1)
    for s in range(1, CR - 1):
        bsend[s] = back[s : s + 1]

    def answer(k, s):
        return pltpu.make_async_remote_copy(
            src_ref=bsend.at[k],
            dst_ref=brecv.at[s],
            send_sem=bs_sem,
            recv_sem=br_sem,
            device_id=(mi, k),
            device_id_type=MESH,
        )

    def answers():
        return pltpu.make_async_remote_copy(
            src_ref=bsend.at[: nc - 1],
            dst_ref=brecv.at[: nc - 1],
            send_sem=bs_sem,
            recv_sem=br_sem,
            device_id=(mi, mj),
            device_id_type=MESH,
        )

    for k in others(mj):

        @pl.when((k != 0) & (k != nc - 1))
        def _(k=k):
            answer(k, mj).start()

    def strip(v):
        has, _, left, right, _ = sides[v]
        for f in range(FIELDS):
            strip_own(f, v, sstat.at[f])

        @pl.when(has)
        def _():
            vertical(1 - v, mi).wait_recv()
            piece(0, mi, CR + 1 - v, zh_sem, zr_sem.at[2 - v]).wait_recv()

        @pl.when(has & left)
        def _():
            corner(1 - v, 1, mi, mj).wait_recv()

        @pl.when(has & right)
        def _():
            corner(1 - v, 0, mi, mj).wait_recv()

        halo, far = vrecv.at[1 - v], (PAIRS if v else 0)
        for half, at in enumerate((SPLIT, 113) if v else (0, SPLIT - HALO)):
            index = jnp.clip(HALO * sub16 + lane16 - at, 0, 127)
            side = take(jnp.broadcast_to(crecv[1 - v, 1 - half], (CR, 128)), index)
            halo[half] = jnp.where(span(at), side, halo[half])
        for f in range(FIELDS):
            for half in range(2):
                at = 8 * half + far
                sstat[f, at : at + HALO] = halo[half, HALO * f : HALO * f + HALO]

        sub = sub8 >= PAIRS if v else sub8 < HALO
        groups = [
            jnp.where(sub, zrecv[CR + 1 - v, :, at : at + 128], zrecv[v * (CR - 1), :, at : at + 128])
            for at in (0, 128)
        ]
        tables = columns(8)[v : v + 2]
        wide = [jnp.concatenate([take(groups[f // 5], c + 24 * (f % 5)) for c in tables], 0) for f in range(COARSE)]
        liquid, ice_w, room, per_pore = layers_of(wide)
        sdir = sstat[DIR]
        masks = inflow_masks(sub_up(sdir), sdir, sub_down(sdir))
        entering = (sub16 & 7) == (1 if v else 6)
        h = wide[0] * sstat[SHARE]
        channel = jnp.zeros((CR, 128), jnp.float32)
        for step in range(3):
            move, rest_s, taken = outflow(
                h, liquid, sstat[ORATE], sstat[LAND], schannel[v], sstat[LRATE], ice_w, per_pore
            )
            channel = channel + taken
            move = [jnp.where(entering, enter[step, v, f], m) for f, m in enumerate(move)]
            arriving = [inflow(masks, sub_up(m), m, sub_down(m)) for m in move]
            h, liquid = settle(rest_s, arriving, room)

        first_row = 2 if v else HALO
        mine = ((sub16 & 7) >= first_row) & ((sub16 & 7) < first_row + HALO)
        mine = mine & ((sub16 >= 8) | (lane16 >= SPLIT)) if v else mine & ((sub16 < 8) | (lane16 < SPLIT))
        rows = []
        for n, x in enumerate(liquid + [h, channel]):
            x = jnp.where(mine, x, 0.0) * scales[n]
            rows.append(jnp.concatenate([jnp.sum(x[at : at + 8], 0, keepdims=True) for at in (0, 8)], 1))
        rows.append(jnp.zeros((2, 2 * 128), jnp.float32))
        part = dot2(jnp.concatenate(rows, 0), to_block_v[128 * v : 128 * v + 256])
        part = pltpu.roll(part, 0, 1, stride=16, stride_axis=0)
        s = v * (CR - 1)
        bsend[s] = back[s : s + 1] + jnp.sum(part, 0, keepdims=True)

        @pl.when(mj != s)
        def _():
            answer(s, mj).start()

    send_early(0)
    strip(0)
    strip(1)

    brecv[mj] = bsend[mj]

    row_pieces().wait_send()

    @pl.when(first_up | last_down)
    def _():
        pltpu.make_async_remote_copy(
            src_ref=zsend,
            dst_ref=zrecv.at[:nc],
            send_sem=zh_sem,
            recv_sem=zr_sem.at[1],
            device_id=(mi, mj),
            device_id_type=MESH,
        ).wait_send()

    for v, (has, i, left, right, end) in enumerate(sides):

        @pl.when(has)
        def _(v=v, i=i):
            vertical(v, i).wait_send()

        @pl.when(has & left)
        def _(v=v, i=i):
            corner(v, 0, i, mj - 1).wait_send()

        @pl.when(has & right)
        def _(v=v, i=i):
            corner(v, 1, i, mj + 1).wait_send()

    @pl.when(has_left)
    def _():
        sideways(0, mj - 1).wait_send()

    @pl.when(has_right)
    def _():
        sideways(1, mj + 1).wait_send()

    answers().wait_recv()

    gather = jnp.minimum(iota((8, 128), 0) * 16 + (lane & 15), 127)
    owner = lax.shift_right_logical(lane, 4)
    for half in range(2):
        out = jnp.zeros((8, 128), jnp.float32)
        for s in range(8):
            x = jnp.broadcast_to(brecv[8 * half + s], (8, 128))
            out = jnp.where(owner == s, take(x, gather), out)
        lanes = slice(128 * half, 128 * half + 128)
        for k in range(LAYERS):
            out_liq[k, :, lanes] = out[k : k + 1]
        out_h[:, lanes] = out[LAYERS : LAYERS + 1]
        out_c[:, lanes] = out[LAYERS + 1 : LAYERS + 2]

    answers().wait_send()


def store(a, b, c, out_a, out_b, out_c, sem):
    copies = [
        pltpu.make_async_copy(src, dst, sem.at[n])
        for n, (src, dst) in enumerate(((a, out_a), (b, out_b), (c, out_c)))
    ]
    for copy in copies:
        copy.start()
    for copy in copies:
        copy.wait()


def solution(mesh):
    nr, nc = mesh.shape["rows"], mesh.shape["cols"]
    f32, bf16 = jnp.float32, jnp.bfloat16

    def step(*args):
        v = pltpu.VMEM
        dma = pltpu.SemaphoreType.DMA
        args = [pltpu.with_memory_space_constraint(x, pltpu.HBM) for x in args]
        results = pl.pallas_call(
            functools.partial(kernel, nr, nc),
            out_shape=(v((LAYERS, 1, W), f32), v((1, W), f32), v((1, W), f32)),
            in_specs=[pl.BlockSpec(memory_space=pltpu.HBM)] * 10,
            out_specs=[pl.BlockSpec(memory_space=pltpu.VMEM)] * 3,
            scratch_shapes=[
                v((1, W), f32),
                v((1, W), f32),
                v((1, W), f32),
                v((LAYERS, 1, W), f32),
                v((LAYERS, 1, W), f32),
                v((TILE, TILE), jnp.int32),
                v((TILE, TILE), jnp.int32),
                v((TILE, TILE), bf16),
                v((TILE, TILE), bf16),
                v((TILE, TILE), bf16),
                v((W, W), bf16),
                v((3 * 128, 128), bf16),
                v((2 * FIELDS + 2, TILE, 128), f32),
                v((2 * REFINE, CR, 128), f32),
                v((FIELDS + 1, 8 * ROWS, 128), f32),
                v((9 * ROWS, 128), f32),
                v((4 * LAYERS + 1, ROWS, 128), f32),
                v((2, FIELDS, (PAIRS + 2) * ROWS, 128), f32),
                v((FIELDS, PAIRS * ROWS, 128), f32),
                v((LAYERS + 2, ROWS, 128), f32),
                v((FIELDS, CR, 128), f32),
                v((2, CR, 128), f32),
                v((3, 2, FIELDS, CR, 128), f32),
                v((CR, 1, W), f32),
                v((CR + 2, 1, W), f32),
                v((2, 2, CR, 128), f32),
                v((2, 2, CR, 128), f32),
                v((2, 2, 1, 128), f32),
                v((2, 2, 1, 128), f32),
                v((3, CR, 128), f32),
                v((2, 3, CR, 128), f32),
                v((CR, 1, 128), f32),
                v((CR, 1, 128), f32),
                dma((10,)),
                dma(()),
                dma(()),
                dma((3,)),
                dma((2,)),
                dma((2,)),
                dma((2, 2)),
                dma((2, 2)),
                dma((2,)),
                dma((2,)),
                dma(()),
                dma(()),
                pltpu.SemaphoreType.REGULAR,
                pltpu.SemaphoreType.REGULAR,
                pltpu.SemaphoreType.REGULAR((2,)),
            ],
            compiler_params=pltpu.CompilerParams(
                collective_id=0, has_side_effects=True, vmem_limit_bytes=62 * 1024 * 1024
            ),
        )(*args)
        return pl.pallas_call(
            store,
            out_shape=(
                jax.ShapeDtypeStruct((LAYERS, 1, W), f32),
                jax.ShapeDtypeStruct((1, W), f32),
                jax.ShapeDtypeStruct((1, W), f32),
            ),
            in_specs=[pl.BlockSpec(memory_space=pltpu.VMEM)] * 3,
            out_specs=[pl.BlockSpec(memory_space=pltpu.HBM)] * 3,
            scratch_shapes=[dma((3,))],
        )(*[pltpu.with_memory_space_constraint(x, pltpu.VMEM) for x in results])

    return jax.shard_map(
        step,
        mesh=mesh,
        in_specs=(
            P(("rows", "cols"), None),
            P(("rows", "cols"), None),
            P(("rows", "cols"), None),
            P(None, ("rows", "cols"), None),
            P(None, ("rows", "cols"), None),
            P("rows", "cols"),
            P("rows", "cols"),
            P("rows", "cols"),
            P("rows", "cols"),
            P("rows", "cols"),
        ),
        out_specs=(
            P(None, ("rows", "cols"), None),
            P(("rows", "cols"), None),
            P(("rows", "cols"), None),
        ),
        check_vma=False,
    )
```

```python
import functools
import math

import jax
import jax.numpy as jnp
from jax import lax
from jax.experimental import pallas as pl
from jax.experimental.pallas import tpu as pltpu
from jax.sharding import PartitionSpec as P

MESH = pl.DeviceIdType.MESH
REFINE = 10
LAYERS = 4
TILE = 160
CR = 16
W = 256
HALO = 3
PAIRS = REFINE // 2
INNER_FIRST = tuple(range(1, PAIRS - 1)) + (0, PAIRS - 1)
OUTER_FIRST = (0, PAIRS - 1) + tuple(range(1, PAIRS - 1))
ROWS = 3 * CR
SPLIT = 56

thickness = (0.1, 0.3, 0.6, 1.0)
layer_speed = (1.0, 0.8, 0.6, 0.4)

DIR, ORATE, LAND, LRATE, SHARE, CHANNEL = range(6)
FIELDS = 5
COARSE = 10


FAR_FIRST = sorted(
    ((z, y, c) for z in range(2) for y in range(4) for c in range(2) if z + y + c),
    key=lambda p: -(p[0] + min(p[1], 4 - p[1])),
)


def others(j):
    z, y, c = j // 8, (j // 2) % 4, j % 2
    return [((z + dz) % 2) * 8 + ((y + dy) % 4) * 2 + (c + dc) % 2 for dz, dy, dc in FAR_FIRST]


def iota(shape, dim):
    return lax.broadcasted_iota(jnp.int32, shape, dim)


def take(x, index):
    return jnp.take_along_axis(x, index, axis=1, mode="promise_in_bounds")


def tenth(x):
    return lax.shift_right_logical(x * 6554, 16)


def split3(x):
    hi = x.astype(jnp.bfloat16)
    r = x - hi.astype(jnp.float32)
    mid = r.astype(jnp.bfloat16)
    lo = (r - mid.astype(jnp.float32)).astype(jnp.bfloat16)
    return jnp.concatenate([hi, mid, lo], 0)


def split2(x):
    hi = x.astype(jnp.bfloat16)
    lo = (x - hi.astype(jnp.float32)).astype(jnp.bfloat16)
    return jnp.concatenate([hi, lo], 0)


def dot3(x, ones):
    n = x.shape[0]
    y = jnp.dot(split3(x), ones, preferred_element_type=jnp.float32)
    return y[:n] + y[n : 2 * n] + y[2 * n :]


def dot2(x, ones):
    n = x.shape[0]
    y = jnp.dot(split2(x), ones, preferred_element_type=jnp.float32)
    return y[:n] + y[n:]


def inflow_masks(d_up, d_mid, d_down):
    return (
        d_up == 1.0,
        d_mid == 0.0,
        d_down == 7.0,
        d_up == 3.0,
        d_mid == 4.0,
        d_down == 5.0,
        d_up == 2.0,
        d_down == 6.0,
    )


def inflow(masks, up, mid, down):
    e0, e1, e2, w0, w1, w2, s0, s1 = masks
    zero = jnp.zeros_like(up)
    east = jnp.where(e0, up, zero) + jnp.where(e1, mid, zero) + jnp.where(e2, down, zero)
    west = jnp.where(w0, up, zero) + jnp.where(w1, mid, zero) + jnp.where(w2, down, zero)
    same = jnp.where(s0, up, zero) + jnp.where(s1, down, zero)
    return same + pltpu.roll(east, 1, 1) + pltpu.roll(west, 127, 1)


def outflow(h, liquid, orate, land, channel, lrate, ice, per_pore):
    q = orate * h * (h / (h + 2.0))
    moving = [q * land]
    rest = [h - q]
    for k in range(LAYERS):
        sat = jnp.minimum((liquid[k] + ice[k]) * per_pore[k], math.sqrt(layer_speed[k]))
        lateral = (lrate * liquid[k]) * (sat * sat)
        moving.append(lateral)
        rest.append(liquid[k] - lateral)
    return moving, rest, q * channel


def settle(rest, arriving, room):
    h = rest[0] + arriving[0]
    liquid = []
    for k in range(LAYERS):
        u = rest[1 + k] + arriving[1 + k]
        h = h + jnp.maximum(u - room[k], 0.0)
        liquid.append(jnp.minimum(u, room[k]))
    return h, liquid


def kernel(
    nr,
    nc,
    rain_h,
    infil_h,
    por_h,
    liq_h,
    ice_h,
    dir_h,
    kind_h,
    orate_h,
    lrate_h,
    weight_h,
    out_liq,
    out_h,
    out_c,
    rain,
    infil,
    por,
    liq,
    ice,
    dir_v,
    kind_v,
    orate_v,
    lrate_v,
    weight_v,
    same_block_v,
    to_block_v,
    nat,
    share_v,
    stat,
    dirs,
    coarse,
    moving,
    rest,
    sums,
    sstat,
    schannel,
    enter,
    zsend,
    zrecv,
    vsend,
    vrecv,
    csend,
    crecv,
    hsend,
    hrecv,
    bsend,
    brecv,
    in_sem,
    zs_sem,
    zh_sem,
    zr_sem,
    vs_sem,
    vr_sem,
    cs_sem,
    cr_sem,
    hs_sem,
    hr_sem,
    bs_sem,
    br_sem,
    row_sem,
    relay_sem,
    late_sem,
):
    mi = lax.axis_index("rows")
    mj = lax.axis_index("cols")
    has_up, has_down = mi > 0, mi < nr - 1
    has_left, has_right = mj > 0, mj < nc - 1

    barrier = pltpu.get_barrier_semaphore()
    lead = nc - 2
    is_lead = mj == lead

    def tell(i, j):
        pl.semaphore_signal(barrier, inc=1, device_id=(i, j), device_id_type=MESH)

    @pl.when(jnp.logical_not(is_lead))
    def _():
        tell(mi, lead)

    copies = [
        pltpu.make_async_copy(src, dst, in_sem.at[n])
        for n, (src, dst) in enumerate(
            (
                (rain_h, rain),
                (infil_h, infil),
                (por_h, por),
                (liq_h, liq),
                (ice_h, ice),
                (weight_h, weight_v),
                (dir_h, dir_v),
                (kind_h, kind_v),
                (orate_h, orate_v),
                (lrate_h, lrate_v),
            )
        )
    ]
    for copy in copies:
        copy.start()

    sides = (
        (has_up, mi - 1, has_left, has_right, nc - 1),
        (has_down, mi + 1, has_left, has_right, 0),
    )
    late = (lax.rem(mi, 4) == 3) & has_down
    late_side = (has_up & (lax.rem(mi, 4) != 0), late)
    early_side = (has_up & (lax.rem(mi, 4) == 0), has_down & (lax.rem(mi, 4) != 3))
    own_end = (0, nc - 1)

    def partners(v, signal):
        has, i, left, right, end = sides[v]
        signal(i, end)
        signal(i, mj)

        @pl.when(left)
        def _():
            signal(i, mj - 1)

        @pl.when(right)
        def _():
            signal(i, mj + 1)

        @pl.when(mj == own_end[v])
        def _():
            @pl.loop(0, nc)
            def _(k):
                signal(i, k)

    def count(v):
        one = 2 + has_left.astype(jnp.int32) + has_right.astype(jnp.int32)
        return one + nc * (mj == own_end[v]).astype(jnp.int32)

    def tell_late_one(i, j):
        @pl.when(j != lead)
        def _():
            tell(i, j)

    for v in range(2):

        @pl.when(early_side[v])
        def _(v=v):
            partners(v, tell_late_one)

    @pl.when(is_lead)
    def _():
        pl.semaphore_wait(barrier, nc - 1)
        near = [lead - 1, lead + 1]
        for k in near + [k for k in others(lead) if k not in near]:
            pl.semaphore_signal(row_sem, inc=1, device_id=(mi, k), device_id_type=MESH)

    row_c, col_c = iota((W, W), 0), iota((W, W), 1)
    same_block = (tenth(row_c) == tenth(col_c)) & (row_c < TILE) & (col_c < TILE)
    same_block_v[...] = jnp.where(same_block, 1.0, 0.0).astype(jnp.bfloat16)
    row_p, col_p = iota((128, 128), 0), iota((128, 128), 1)
    to_block = []
    for at, end, shift in ((3, 113, 0), (3, 53, 11), (3, 113, 5)):
        mine = (row_p >= at) & (row_p < end) & (tenth(row_p + 7) == col_p + 1 - shift)
        if shift == 11:
            mine = mine | ((row_p >= 59) & (row_p < 109) & (tenth(row_p - 49) == col_p + 1))
        to_block.append(jnp.where(mine, 1.0, 0.0).astype(jnp.bfloat16))
    to_block_v[...] = jnp.concatenate(to_block, 0)

    lane = iota((8, 128), 1)
    lane16 = iota((CR, 128), 1)
    sub16 = iota((CR, 128), 0)

    def piece(k, i, s, send, arrive):
        return pltpu.make_async_remote_copy(
            src_ref=zsend.at[k],
            dst_ref=zrecv.at[s],
            send_sem=send,
            recv_sem=arrive,
            device_id=(i, k),
            device_id_type=MESH,
        )

    def row_pieces():
        return pltpu.make_async_remote_copy(
            src_ref=zsend.at[: nc - 1],
            dst_ref=zrecv.at[: nc - 1],
            send_sem=zs_sem,
            recv_sem=zr_sem.at[0],
            device_id=(mi, mj),
            device_id_type=MESH,
        )

    first_up = has_up & (mj == 0)
    last_down = has_down & (mj == nc - 1)

    def first_run(a):
        return pltpu.roll(a, HALO, 1)

    def second_run(a, b):
        return jnp.where(lane16 < 21, pltpu.roll(a, 21, 1), pltpu.roll(b, 21, 1))

    def third_run(a):
        return pltpu.roll(a, 59, 1)

    def fourth_run(a, b):
        return jnp.where(lane16 < 81, pltpu.roll(a, 81, 1), pltpu.roll(b, 81, 1))

    def rows_of(f, rr):
        return [nat.at[2 * f + half][pl.ds(rr, CR, stride=REFINE), :] for half in range(2)]

    def field(f):
        return (dirs, ROWS) if f == DIR else (stat.at[f], 0)

    def vertical(v, i):
        return pltpu.make_async_remote_copy(
            src_ref=vsend.at[v],
            dst_ref=vrecv.at[v],
            send_sem=vs_sem.at[v],
            recv_sem=vr_sem.at[v],
            device_id=(i, mj),
            device_id_type=MESH,
        )

    def corner(v, s, i, j):
        return pltpu.make_async_remote_copy(
            src_ref=csend.at[v, s],
            dst_ref=crecv.at[v, s],
            send_sem=cs_sem.at[v, s],
            recv_sem=cr_sem.at[v, s],
            device_id=(i, j),
            device_id_type=MESH,
        )

    incoming = sum(late_side[v].astype(jnp.int32) * count(v) for v in range(2))

    any_late = late_side[0] | late_side[1]
    passes_on = (mj == lead - 1) | (mj == lead + 1)

    def rows_ready():
        pl.semaphore_wait(barrier, incoming)

    def pass_on():
        pl.semaphore_signal(relay_sem, inc=1, device_id=(mi, lead), device_id_type=MESH)

    def send_ends(v):
        @pl.when(mj == own_end[v])
        def _():
            @pl.loop(0, nc)
            def _(k):
                piece(k, sides[v][1], CR + v, zh_sem, zr_sem.at[1 + v]).start()

    def send_rows(v):
        _, i, left, right, _ = sides[v]
        vertical(v, i).start()

        @pl.when(left)
        def _():
            corner(v, 0, i, mj - 1).start()

        @pl.when(right)
        def _():
            corner(v, 1, i, mj + 1).start()

    def tell_early(v):
        def signal(i, j):
            pl.semaphore_signal(late_sem.at[1 - v], inc=1, device_id=(i, j), device_id_type=MESH)

        partners(v, signal)

    def coarse_part():
        for copy in copies[:5]:
            copy.wait()
        rain_x, por_x = rain[...], por[...]
        top_sat = (liq[0] + ice[0]) / por_x
        capacity = infil[...] * jnp.maximum(1.0 - top_sat, 0.1)
        excess = rain_x * rain_x / (rain_x + capacity)
        top = liq[0] + (rain_x - excess) / (1000.0 * thickness[0])
        strip = [excess, por_x, top] + [liq[k] for k in range(1, LAYERS)] + [ice[k] for k in range(LAYERS)]

        slot = lax.shift_right_logical(lane * 2731, 16)
        t = lane - slot * 24
        for half in range(2):
            base = (iota((8, 128), 0) + 8 * half) * 16 - 1 + t
            inside = jnp.clip(base, 0, W - 1)
            index = inside & 127
            low = inside < 128
            for group in range(2):
                packed = jnp.zeros((8, 128), jnp.float32)
                for n in range(5):
                    x = strip[group * 5 + n]
                    a = jnp.broadcast_to(x[:, :128], (8, 128))
                    b = jnp.broadcast_to(x[:, 128:], (8, 128))
                    packed = jnp.where(slot == n, jnp.where(low, take(a, index), take(b, index)), packed)
                for s in range(8):
                    zsend[8 * half + s, :, 128 * group : 128 * group + 128] = packed[s : s + 1]

        zrecv[mj] = zsend[mj]

        @pl.when(jnp.logical_not(has_down))
        def _():
            zrecv[CR] = zsend[mj]

        @pl.when(jnp.logical_not(has_up))
        def _():
            zrecv[CR + 1] = zsend[mj]

    def tile_arrived():
        for copy in copies[5:]:
            copy.wait()

    def vertical_part():
        no_lanes = jnp.zeros((CR, 96), jnp.float32)

        def in_halves(x):
            return x[:, :128], jnp.concatenate([x[:, 128:], no_lanes[: x.shape[0]]], 1)

        edges, totals = [], []
        for v in range(2):
            r = v * (TILE - CR)
            kind_x = kind_v[r : r + CR]
            edge = [
                dir_v[r : r + CR].astype(jnp.float32),
                jnp.where(kind_x == 2, 0.0, orate_v[r : r + CR].astype(jnp.float32)),
                jnp.where(kind_x == 0, 1.0, 0.0),
                lrate_v[r : r + CR].astype(jnp.float32),
                weight_v[r : r + CR].astype(jnp.float32),
            ]
            edge = [in_halves(x) for x in edge]
            mine = sub16 >= CR - REFINE if v else sub16 < REFINE
            total = [jnp.sum(jnp.where(mine, x, 0.0), 0, keepdims=True) for x in edge[SHARE]]
            edges.append(edge)
            totals.append(jnp.concatenate(total, 1))
        totals.append(jnp.zeros((6, W), jnp.float32))
        per_mean = 100.0 / jnp.where(iota((8, W), 1) < TILE, dot3(jnp.concatenate(totals, 0), same_block_v[...]), 1.0)
        place = lane16 - HALO * sub16
        for v in (1, 0):
            r = v * (CR - HALO)
            for half in range(2):
                scale = per_mean[v : v + 1, 128 * half : 128 * half + 128]
                for f in range(FIELDS):
                    x = edges[v][f][half][r : r + HALO]
                    vsend[v, half, HALO * f : HALO * f + HALO] = x * scale if f == SHARE else x
                vsend[v, half, HALO * FIELDS :] = jnp.zeros((1, 128), jnp.float32)
            a, b = vsend[v, 0], vsend[v, 1]
            if v == 0:
                vsend[v, 0], vsend[v, 1] = third_run(a), fourth_run(a, b)
            else:
                vsend[v, 0], vsend[v, 1] = first_run(a), second_run(a, b)
            for n, (x, at) in enumerate(((a, 0), (b, 29))):
                end = jnp.where((place >= 0) & (place < HALO), take(x, jnp.clip(place + at, 0, 127)), 0.0)
                csend[v, n] = jnp.sum(end, 0, keepdims=True)

    def tile_part():
        kind_x = kind_v[...]
        natural = (
            dir_v[...].astype(jnp.float32),
            jnp.where(kind_x == 2, 0.0, orate_v[...].astype(jnp.float32)),
            jnp.where(kind_x == 0, 1.0, 0.0),
            lrate_v[...].astype(jnp.float32),
            weight_v[...].astype(jnp.float32),
            jnp.where(kind_x == 1, 1.0, 0.0),
        )
        no_lanes = jnp.zeros((TILE, 96), jnp.float32)
        for f in range(FIELDS + 1):
            nat[2 * f] = natural[f][:, :128]
            nat[2 * f + 1] = jnp.concatenate([natural[f][:, 128:], no_lanes], 1)

        weights = [rows_of(SHARE, rr) for rr in range(REFINE)]
        total = [functools.reduce(lambda a, b: a + b, [w[half] for w in weights]) for half in range(2)]
        block_sum = dot3(jnp.concatenate(total, 1), same_block_v[...])
        per_mean = 100.0 / jnp.where(iota((CR, W), 1) < TILE, block_sum, 1.0)
        shares = [[w[half] * per_mean[:, 128 * half : 128 * half + 128] for half in range(2)] for w in weights]
        for rr in range(REFINE):
            for half in range(2):
                share_v[2 * rr + half] = shares[rr][half]

    def send_pieces():
        for k in others(mj):
            piece(k, mi, mj, zs_sem, zr_sem.at[0]).start()

    def meet_early():
        @pl.when(passes_on)
        def _():
            pl.semaphore_wait(row_sem, 1)

        @pl.when(jnp.logical_not(is_lead))
        def _():
            rows_ready()

        @pl.when(passes_on)
        def _():
            pass_on()

        @pl.when(is_lead)
        def _():
            pl.semaphore_wait(relay_sem, 2)

        for v in (1, 0):

            @pl.when(late_side[v])
            def _(v=v):
                tell_early(v)

    def send_late():
        for v in (1, 0):

            @pl.when(late_side[v])
            def _(v=v):
                send_rows(v)

    @pl.when(late)
    def _():
        tile_arrived()
        vertical_part()
        meet_early()
        send_late()

    coarse_part()

    @pl.when(late)
    def _():
        send_ends(1)
        send_ends(0)

    @pl.when(is_lead)
    def _():
        send_pieces()

    @pl.when(jnp.logical_not(late))
    def _():
        tile_arrived()

    tile_part()

    @pl.when(any_late & jnp.logical_not(late))
    def _():
        meet_early()
        send_ends(0)

    shares = [[share_v[2 * rr + half] for half in range(2)] for rr in range(REFINE)]

    def slab_place(rr, f):
        n = rr * FIELDS + f
        return n // 18, HALO * (n % 9) + 64 * (n % 18 // 9)

    slabs = [jnp.zeros((CR, 128), jnp.float32)] * 3
    for rr in range(REFINE):
        for f in range(FIELDS):
            a, b = shares[rr] if f == SHARE else rows_of(f, rr)
            x = jnp.where(lane16 < HALO, a, jnp.where((lane16 >= 29) & (lane16 < 32), b, 0.0))
            n, at = slab_place(rr, f)
            slabs[n] = slabs[n] + (pltpu.roll(x, at, 1) if at else x)
    for n in range(3):
        hsend[n] = slabs[n]

    def sideways(n, j):
        return pltpu.make_async_remote_copy(
            src_ref=hsend,
            dst_ref=hrecv.at[n],
            send_sem=hs_sem.at[n],
            recv_sem=hr_sem.at[n],
            device_id=(mi, j),
            device_id_type=MESH,
        )

    @pl.when(jnp.logical_not(is_lead))
    def _():
        @pl.when(jnp.logical_not(any_late & passes_on))
        def _():
            pl.semaphore_wait(row_sem, 1)

        send_pieces()

    @pl.when(has_left)
    def _():
        sideways(0, mj - 1).start()

    @pl.when(has_right)
    def _():
        sideways(1, mj + 1).start()

    @pl.when(jnp.logical_not(late))
    def _():
        vertical_part()
        send_late()

    for p in range(PAIRS):
        for f in range(FIELDS + 1):
            if f == SHARE:
                (a, b), (c, d) = shares[p], shares[p + PAIRS]
            else:
                (a, b), (c, d) = rows_of(f, p), rows_of(f, p + PAIRS)
            ref, off = field(f)
            r = off + p * ROWS
            ref[r : r + CR] = first_run(a)
            ref[r + CR : r + 2 * CR] = jnp.where(lane16 < SPLIT, second_run(a, b), third_run(c))
            ref[r + 2 * CR : r + ROWS] = fourth_run(c, d)

    def strip_own(f, v, out):
        ref, off = field(f)
        for half in range(2):
            at = 8 * half + (0 if v else HALO)
            r = off + (v + half) * CR + v * (CR - 1)
            out[at : at + PAIRS] = ref[pl.ds(r, PAIRS, stride=ROWS), :]

    lane8, sub8 = iota((8, 128), 1), iota((8, 128), 0)
    schannel[...] = jnp.zeros(schannel.shape, jnp.float32)
    for v in range(2):
        strip_own(CHANNEL, v, schannel.at[v])

    row48, lane48 = iota((ROWS, 128), 0), iota((ROWS, 128), 1)
    in_first = (row48 == 0) | ((row48 == CR) & (lane48 < SPLIT))
    in_last = (row48 == ROWS - 1) | ((row48 == 2 * CR - 1) & (lane48 >= SPLIT))
    for p in range(PAIRS):
        out = in_first if p < 2 else in_last if p > 2 else in_first | in_last
        r = p * ROWS
        stat[CHANNEL, r : r + ROWS] = jnp.where(out, 0.0, stat[CHANNEL, r : r + ROWS])

    def send_early(v):
        @pl.when(early_side[v])
        def _():
            pl.semaphore_wait(late_sem.at[v], count(v))
            send_rows(v)
            send_ends(v)

    send_early(1)

    for v, (has, i, left, right, end) in enumerate(sides):

        @pl.when(jnp.logical_not(has))
        def _(v=v):
            vrecv[1 - v] = jnp.zeros(vrecv.shape[1:], jnp.float32)

        @pl.when(jnp.logical_not(has & left))
        def _(v=v):
            crecv[1 - v, 1] = jnp.zeros((1, 128), jnp.float32)

        @pl.when(jnp.logical_not(has & right))
        def _(v=v):
            crecv[1 - v, 0] = jnp.zeros((1, 128), jnp.float32)

    @pl.when(jnp.logical_not(has_right))
    def _():
        hrecv[0] = jnp.zeros(hrecv.shape[1:], jnp.float32)

    @pl.when(jnp.logical_not(has_left))
    def _():
        hrecv[1] = jnp.zeros(hrecv.shape[1:], jnp.float32)

    def columns(n):
        lanes = iota((n, 128), 1)
        return (
            tenth(lanes + 7),
            tenth(jnp.where(lanes < SPLIT, lanes + 117, lanes - 49)),
            jnp.minimum(tenth(lanes + 57), 17),
        )

    def layers_of(wide):
        por_w = wide[1]
        liquid, ice_w, room, per_pore = [], [], [], []
        for k in range(LAYERS):
            depth = 1000.0 * thickness[k]
            liquid.append(wide[2 + k] * depth)
            ice_w.append(wide[2 + LAYERS + k] * depth)
            room.append((por_w - wide[2 + LAYERS + k]) * depth)
            per_pore.append((math.sqrt(layer_speed[k]) / depth) / por_w)
        return liquid, ice_w, room, per_pore

    @pl.when(has_right)
    def _():
        sideways(0, mj).wait_recv()

    @pl.when(has_left)
    def _():
        sideways(1, mj).wait_recv()

    def span(at):
        return (lane16 >= at) & (lane16 < at + HALO)

    for p in range(PAIRS):
        for f in range(FIELDS):
            ref, off = field(f)
            r = off + p * ROWS
            for rr, (left_row, left_at), (right_row, right_at) in (
                (p, (r, 0), (r + CR, SPLIT - HALO)),
                (p + PAIRS, (r + CR, SPLIT), (r + 2 * CR, 113)),
            ):
                n, at = slab_place(rr, f)
                from_left = pltpu.roll(hrecv[1, n], (left_at - 29 - at) % 128, 1)
                from_right = pltpu.roll(hrecv[0, n], (right_at - at) % 128, 1)
                ref[left_row : left_row + CR] = jnp.where(
                    span(left_at), from_left, ref[left_row : left_row + CR]
                )
                ref[right_row : right_row + CR] = jnp.where(
                    span(right_at), from_right, ref[right_row : right_row + CR]
                )

    END = ROWS * (PAIRS + 1)
    sub_up = functools.partial(pltpu.roll, shift=1, axis=0)

    def sub_down(x):
        return pltpu.roll(x, x.shape[0] - 1, 0)

    def across(x):
        x0, x1, x2 = x[:CR], x[CR : 2 * CR], x[2 * CR :]
        return (
            jnp.where(lane16 < 53, pltpu.roll(x1, 72, 1), pltpu.roll(x2, 50, 1)),
            pltpu.roll(x2, 68, 1),
            pltpu.roll(x0, SPLIT, 1),
            jnp.where(lane16 < 63, pltpu.roll(x0, 78, 1), pltpu.roll(x1, 60, 1)),
        )

    def wrap(ref):
        a, b, c, d = across(ref[END - ROWS : END])
        ref[:CR] = sub_up(a)
        ref[CR : 2 * CR] = jnp.where(lane16 < SPLIT, sub_up(b), c)
        ref[2 * CR : ROWS] = d
        a, b, c, d = across(ref[ROWS : 2 * ROWS])
        ref[END : END + CR] = a
        ref[END + CR : END + 2 * CR] = jnp.where(lane16 < SPLIT, b, sub_down(c))
        ref[END + 2 * CR : END + ROWS] = sub_down(d)

    wrap(dirs)
    sums[...] = jnp.zeros(sums.shape, jnp.float32)

    row_pieces().wait_recv()

    def rows_at(group, slots):
        return jnp.concatenate([zrecv[n, :, 128 * group : 128 * group + 128] for n in slots], 0)

    packed_rows = [rows_at(g, range(CR)) for g in range(2)]
    wide = [
        jnp.concatenate([take(packed_rows[f // 5], c + 24 * (f % 5)) for c in columns(CR)], 0) for f in range(COARSE)
    ]
    liquid_w, ice_w, room, per_pore = layers_of(wide)
    for n, x in enumerate(ice_w + room + per_pore + liquid_w + wide[:1]):
        coarse[n] = x

    def finish(b, step):
        top, bottom = ROWS + HALO * ROWS, ROWS + ROWS + CR - 1
        for f in range(FIELDS):
            wrap(moving.at[b, f])
            enter[step, 0, f, 6:7] = moving[b, f, top : top + 1]
            enter[step, 0, f, 14:15] = moving[b, f, top + CR : top + CR + 1]
            enter[step, 1, f, 1:2] = moving[b, f, bottom + CR : bottom + CR + 1]
            enter[step, 1, f, 9:10] = moving[b, f, bottom + 2 * CR : bottom + 2 * CR + 1]

    def main_in(b, r, c):
        masks = inflow_masks(*[dirs[pl.ds(r + n * ROWS, CR), :] for n in range(3)])
        arriving = [
            inflow(masks, *[moving[b, f, pl.ds(r + n * ROWS, CR), :] for n in range(3)])
            for f in range(FIELDS)
        ]
        left = [rest[f, pl.ds(r, CR), :] for f in range(FIELDS)]
        return settle(left, arriving, [coarse[LAYERS + k, c : c + CR] for k in range(LAYERS)])

    def main_out(b, r, c, h, liquid):
        move, left, taken = outflow(
            h,
            liquid,
            stat[ORATE, pl.ds(r, CR), :],
            stat[LAND, pl.ds(r, CR), :],
            stat[CHANNEL, pl.ds(r, CR), :],
            stat[LRATE, pl.ds(r, CR), :],
            [coarse[k, c : c + CR] for k in range(LAYERS)],
            [coarse[2 * LAYERS + k, c : c + CR] for k in range(LAYERS)],
        )
        for f in range(FIELDS):
            moving[b, f, pl.ds(r + ROWS, CR), :] = move[f]
            rest[f, pl.ds(r, CR), :] = left[f]
        sums[LAYERS + 1, c : c + CR] += taken

    def row_at(p, c):
        return p * ROWS + c

    for c in range(0, ROWS, CR):
        liquid = [coarse[3 * LAYERS + k, c : c + CR] for k in range(LAYERS)]
        drain = []
        for k in range(LAYERS):
            sat = (liquid[k] + coarse[k, c : c + CR]) * coarse[2 * LAYERS + k, c : c + CR]
            sat = jnp.minimum(sat, math.sqrt(layer_speed[k]))
            drain.append(liquid[k] * (sat * sat))
        taken_c = jnp.zeros((CR, 128), jnp.float32)
        for p in OUTER_FIRST:
            r = row_at(p, c)
            h = coarse[4 * LAYERS, c : c + CR] * stat[SHARE, r : r + CR]
            q = stat[ORATE, r : r + CR] * h * (h / (h + 2.0))
            moving[0, 0, r + ROWS : r + ROWS + CR] = q * stat[LAND, r : r + CR]
            rest[0, r : r + CR] = h - q
            taken_c = taken_c + q * stat[CHANNEL, r : r + CR]
            for k in range(LAYERS):
                lateral = stat[LRATE, r : r + CR] * drain[k]
                moving[0, 1 + k, r + ROWS : r + ROWS + CR] = lateral
                rest[1 + k, r : r + CR] = liquid[k] - lateral
        sums[LAYERS + 1, c : c + CR] = taken_c

    finish(0, 0)

    for b in range(2):

        for p in INNER_FIRST:
            for c in range(0, ROWS, CR):
                r = row_at(p, c)
                main_out(1 - b, r, c, *main_in(b, r, c))

        finish(1 - b, 1 + b)

    for p in INNER_FIRST:
        for c in range(0, ROWS, CR):
            h, liquid = main_in(0, row_at(p, c), c)
            out = [in_first[c : c + CR]] * (p < HALO and c < 2 * CR) + [in_last[c : c + CR]] * (p >= PAIRS - HALO and c > 0)
            for n, x in enumerate(liquid + [h]):
                for mine in out:
                    x = jnp.where(mine, 0.0, x)
                sums[n, c : c + CR] += x

    scales = [0.01 / (1000.0 * x) for x in thickness] + [0.01, 0.01]

    def three(n):
        return jnp.concatenate([sums[n, c : c + CR] for c in range(0, ROWS, CR)], 1) * scales[n]

    means = dot2(jnp.concatenate([three(n) for n in range(LAYERS + 2)], 0), to_block_v[...])
    back = means[:CR]
    for n in range(1, LAYERS + 2):
        back = back + pltpu.roll(means[n * CR : (n + 1) * CR], 16 * n, 1)
    for s in range(1, CR - 1):
        bsend[s] = back[s : s + 1]

    def answer(k, s):
        return pltpu.make_async_remote_copy(
            src_ref=bsend.at[k],
            dst_ref=brecv.at[s],
            send_sem=bs_sem,
            recv_sem=br_sem,
            device_id=(mi, k),
            device_id_type=MESH,
        )

    def answers():
        return pltpu.make_async_remote_copy(
            src_ref=bsend.at[: nc - 1],
            dst_ref=brecv.at[: nc - 1],
            send_sem=bs_sem,
            recv_sem=br_sem,
            device_id=(mi, mj),
            device_id_type=MESH,
        )

    def inner(n):
        return 1 + lax.rem(mj + n, CR - 2)

    for n in (11, 3, 10, 2, 7, 6, 8, 9, 5, 4, 1, 0, 12):
        answer(inner(n), mj).start()

    @pl.when((mj == 0) | (mj == nc - 1))
    def _():
        answer(inner(CR - 3), mj).start()

    def strip(v):
        has, _, left, right, _ = sides[v]
        for f in range(FIELDS):
            strip_own(f, v, sstat.at[f])

        @pl.when(has)
        def _():
            vertical(1 - v, mi).wait_recv()
            piece(0, mi, CR + 1 - v, zh_sem, zr_sem.at[2 - v]).wait_recv()

        @pl.when(has & left)
        def _():
            corner(1 - v, 1, mi, mj).wait_recv()

        @pl.when(has & right)
        def _():
            corner(1 - v, 0, mi, mj).wait_recv()

        halo, far = vrecv.at[1 - v], (PAIRS if v else 0)
        for half, at in enumerate((SPLIT, 113) if v else (0, SPLIT - HALO)):
            index = jnp.clip(HALO * sub16 + lane16 - at, 0, 127)
            side = take(jnp.broadcast_to(crecv[1 - v, 1 - half], (CR, 128)), index)
            halo[half] = jnp.where(span(at), side, halo[half])
        for f in range(FIELDS):
            for half in range(2):
                at = 8 * half + far
                sstat[f, at : at + HALO] = halo[half, HALO * f : HALO * f + HALO]

        sub = sub8 >= PAIRS if v else sub8 < HALO
        groups = [
            jnp.where(sub, zrecv[CR + 1 - v, :, at : at + 128], zrecv[v * (CR - 1), :, at : at + 128])
            for at in (0, 128)
        ]
        tables = columns(8)[v : v + 2]
        wide = [jnp.concatenate([take(groups[f // 5], c + 24 * (f % 5)) for c in tables], 0) for f in range(COARSE)]
        liquid, ice_w, room, per_pore = layers_of(wide)
        sdir = sstat[DIR]
        masks = inflow_masks(sub_up(sdir), sdir, sub_down(sdir))
        entering = (sub16 & 7) == (1 if v else 6)
        h = wide[0] * sstat[SHARE]
        channel = jnp.zeros((CR, 128), jnp.float32)
        for step in range(3):
            move, rest_s, taken = outflow(
                h, liquid, sstat[ORATE], sstat[LAND], schannel[v], sstat[LRATE], ice_w, per_pore
            )
            channel = channel + taken
            move = [jnp.where(entering, enter[step, v, f], m) for f, m in enumerate(move)]
            arriving = [inflow(masks, sub_up(m), m, sub_down(m)) for m in move]
            h, liquid = settle(rest_s, arriving, room)

        first_row = 2 if v else HALO
        mine = ((sub16 & 7) >= first_row) & ((sub16 & 7) < first_row + HALO)
        mine = mine & ((sub16 >= 8) | (lane16 >= SPLIT)) if v else mine & ((sub16 < 8) | (lane16 < SPLIT))
        rows = []
        for n, x in enumerate(liquid + [h, channel]):
            x = jnp.where(mine, x, 0.0) * scales[n]
            rows.append(jnp.concatenate([jnp.sum(x[at : at + 8], 0, keepdims=True) for at in (0, 8)], 1))
        rows.append(jnp.zeros((2, 2 * 128), jnp.float32))
        part = dot2(jnp.concatenate(rows, 0), to_block_v[128 * v : 128 * v + 256])
        part = pltpu.roll(part, 0, 1, stride=16, stride_axis=0)
        s = v * (CR - 1)
        bsend[s] = back[s : s + 1] + jnp.sum(part, 0, keepdims=True)

        @pl.when(mj != s)
        def _():
            answer(s, mj).start()

    strip(0)
    send_early(0)
    strip(1)

    brecv[mj] = bsend[mj]

    row_pieces().wait_send()

    @pl.when(first_up | last_down)
    def _():
        pltpu.make_async_remote_copy(
            src_ref=zsend,
            dst_ref=zrecv.at[:nc],
            send_sem=zh_sem,
            recv_sem=zr_sem.at[1],
            device_id=(mi, mj),
            device_id_type=MESH,
        ).wait_send()

    for v, (has, i, left, right, end) in enumerate(sides):

        @pl.when(has)
        def _(v=v, i=i):
            vertical(v, i).wait_send()

        @pl.when(has & left)
        def _(v=v, i=i):
            corner(v, 0, i, mj - 1).wait_send()

        @pl.when(has & right)
        def _(v=v, i=i):
            corner(v, 1, i, mj + 1).wait_send()

    @pl.when(has_left)
    def _():
        sideways(0, mj - 1).wait_send()

    @pl.when(has_right)
    def _():
        sideways(1, mj + 1).wait_send()

    answers().wait_recv()

    gather = jnp.minimum(iota((8, 128), 0) * 16 + (lane & 15), 127)
    owner = lax.shift_right_logical(lane, 4)
    for half in range(2):
        out = jnp.zeros((8, 128), jnp.float32)
        for s in range(8):
            x = jnp.broadcast_to(brecv[8 * half + s], (8, 128))
            out = jnp.where(owner == s, take(x, gather), out)
        lanes = slice(128 * half, 128 * half + 128)
        for k in range(LAYERS):
            out_liq[k, :, lanes] = out[k : k + 1]
        out_h[:, lanes] = out[LAYERS : LAYERS + 1]
        out_c[:, lanes] = out[LAYERS + 1 : LAYERS + 2]

    answers().wait_send()


def store(a, b, c, out_a, out_b, out_c, sem):
    copies = [
        pltpu.make_async_copy(src, dst, sem.at[n])
        for n, (src, dst) in enumerate(((a, out_a), (b, out_b), (c, out_c)))
    ]
    for copy in copies:
        copy.start()
    for copy in copies:
        copy.wait()


def solution(mesh):
    nr, nc = mesh.shape["rows"], mesh.shape["cols"]
    f32, bf16 = jnp.float32, jnp.bfloat16

    def step(*args):
        v = pltpu.VMEM
        dma = pltpu.SemaphoreType.DMA
        args = [pltpu.with_memory_space_constraint(x, pltpu.HBM) for x in args]
        results = pl.pallas_call(
            functools.partial(kernel, nr, nc),
            out_shape=(v((LAYERS, 1, W), f32), v((1, W), f32), v((1, W), f32)),
            in_specs=[pl.BlockSpec(memory_space=pltpu.HBM)] * 10,
            out_specs=[pl.BlockSpec(memory_space=pltpu.VMEM)] * 3,
            scratch_shapes=[
                v((1, W), f32),
                v((1, W), f32),
                v((1, W), f32),
                v((LAYERS, 1, W), f32),
                v((LAYERS, 1, W), f32),
                v((TILE, TILE), jnp.int32),
                v((TILE, TILE), jnp.int32),
                v((TILE, TILE), bf16),
                v((TILE, TILE), bf16),
                v((TILE, TILE), bf16),
                v((W, W), bf16),
                v((3 * 128, 128), bf16),
                v((2 * FIELDS + 2, TILE, 128), f32),
                v((2 * REFINE, CR, 128), f32),
                v((FIELDS + 1, 8 * ROWS, 128), f32),
                v((9 * ROWS, 128), f32),
                v((4 * LAYERS + 1, ROWS, 128), f32),
                v((2, FIELDS, (PAIRS + 2) * ROWS, 128), f32),
                v((FIELDS, PAIRS * ROWS, 128), f32),
                v((LAYERS + 2, ROWS, 128), f32),
                v((FIELDS, CR, 128), f32),
                v((2, CR, 128), f32),
                v((3, 2, FIELDS, CR, 128), f32),
                v((CR, 1, W), f32),
                v((CR + 2, 1, W), f32),
                v((2, 2, CR, 128), f32),
                v((2, 2, CR, 128), f32),
                v((2, 2, 1, 128), f32),
                v((2, 2, 1, 128), f32),
                v((3, CR, 128), f32),
                v((2, 3, CR, 128), f32),
                v((CR, 1, 128), f32),
                v((CR, 1, 128), f32),
                dma((10,)),
                dma(()),
                dma(()),
                dma((3,)),
                dma((2,)),
                dma((2,)),
                dma((2, 2)),
                dma((2, 2)),
                dma((2,)),
                dma((2,)),
                dma(()),
                dma(()),
                pltpu.SemaphoreType.REGULAR,
                pltpu.SemaphoreType.REGULAR,
                pltpu.SemaphoreType.REGULAR((2,)),
            ],
            compiler_params=pltpu.CompilerParams(
                collective_id=0, has_side_effects=True, vmem_limit_bytes=62 * 1024 * 1024
            ),
        )(*args)
        return pl.pallas_call(
            store,
            out_shape=(
                jax.ShapeDtypeStruct((LAYERS, 1, W), f32),
                jax.ShapeDtypeStruct((1, W), f32),
                jax.ShapeDtypeStruct((1, W), f32),
            ),
            in_specs=[pl.BlockSpec(memory_space=pltpu.VMEM)] * 3,
            out_specs=[pl.BlockSpec(memory_space=pltpu.HBM)] * 3,
            scratch_shapes=[dma((3,))],
        )(*[pltpu.with_memory_space_constraint(x, pltpu.VMEM) for x in results])

    return jax.shard_map(
        step,
        mesh=mesh,
        in_specs=(
            P(("rows", "cols"), None),
            P(("rows", "cols"), None),
            P(("rows", "cols"), None),
            P(None, ("rows", "cols"), None),
            P(None, ("rows", "cols"), None),
            P("rows", "cols"),
            P("rows", "cols"),
            P("rows", "cols"),
            P("rows", "cols"),
            P("rows", "cols"),
        ),
        out_specs=(
            P(None, ("rows", "cols"), None),
            P(("rows", "cols"), None),
            P(("rows", "cols"), None),
        ),
        check_vma=False,
    )
```

```python
import functools
import math

import jax
import jax.numpy as jnp
from jax import lax
from jax.experimental import pallas as pl
from jax.experimental.pallas import tpu as pltpu
from jax.sharding import PartitionSpec as P

MESH = pl.DeviceIdType.MESH
REFINE = 10
LAYERS = 4
TILE = 160
CR = 16
W = 256
HALO = 3
PAIRS = REFINE // 2
INNER_FIRST = tuple(range(1, PAIRS - 1)) + (0, PAIRS - 1)
OUTER_FIRST = (0, PAIRS - 1) + tuple(range(1, PAIRS - 1))
ROWS = 3 * CR
SPLIT = 56

thickness = (0.1, 0.3, 0.6, 1.0)
layer_speed = (1.0, 0.8, 0.6, 0.4)

DIR, ORATE, LAND, LRATE, SHARE, CHANNEL = range(6)
FIELDS = 5
COARSE = 10


FAR_FIRST = sorted(
    ((z, y, c) for z in range(2) for y in range(4) for c in range(2) if z + y + c),
    key=lambda p: -(p[0] + min(p[1], 4 - p[1])),
)


def others(j):
    z, y, c = j // 8, (j // 2) % 4, j % 2
    return [((z + dz) % 2) * 8 + ((y + dy) % 4) * 2 + (c + dc) % 2 for dz, dy, dc in FAR_FIRST]


def iota(shape, dim):
    return lax.broadcasted_iota(jnp.int32, shape, dim)


def take(x, index):
    return jnp.take_along_axis(x, index, axis=1, mode="promise_in_bounds")


def tenth(x):
    return lax.shift_right_logical(x * 6554, 16)


def split3(x):
    hi = x.astype(jnp.bfloat16)
    r = x - hi.astype(jnp.float32)
    mid = r.astype(jnp.bfloat16)
    lo = (r - mid.astype(jnp.float32)).astype(jnp.bfloat16)
    return jnp.concatenate([hi, mid, lo], 0)


def split2(x):
    hi = x.astype(jnp.bfloat16)
    lo = (x - hi.astype(jnp.float32)).astype(jnp.bfloat16)
    return jnp.concatenate([hi, lo], 0)


def dot3(x, ones):
    n = x.shape[0]
    y = jnp.dot(split3(x), ones, preferred_element_type=jnp.float32)
    return y[:n] + y[n : 2 * n] + y[2 * n :]


def dot2(x, ones):
    n = x.shape[0]
    y = jnp.dot(split2(x), ones, preferred_element_type=jnp.float32)
    return y[:n] + y[n:]


def inflow_masks(d_up, d_mid, d_down):
    return (
        d_up == 1.0,
        d_mid == 0.0,
        d_down == 7.0,
        d_up == 3.0,
        d_mid == 4.0,
        d_down == 5.0,
        d_up == 2.0,
        d_down == 6.0,
    )


def inflow(masks, up, mid, down):
    e0, e1, e2, w0, w1, w2, s0, s1 = masks
    zero = jnp.zeros_like(up)
    east = jnp.where(e0, up, zero) + jnp.where(e1, mid, zero) + jnp.where(e2, down, zero)
    west = jnp.where(w0, up, zero) + jnp.where(w1, mid, zero) + jnp.where(w2, down, zero)
    same = jnp.where(s0, up, zero) + jnp.where(s1, down, zero)
    return same + pltpu.roll(east, 1, 1) + pltpu.roll(west, 127, 1)


def outflow(h, liquid, orate, land, channel, lrate, ice, per_pore):
    q = orate * h * (h / (h + 2.0))
    moving = [q * land]
    rest = [h - q]
    for k in range(LAYERS):
        sat = jnp.minimum((liquid[k] + ice[k]) * per_pore[k], math.sqrt(layer_speed[k]))
        lateral = (lrate * liquid[k]) * (sat * sat)
        moving.append(lateral)
        rest.append(liquid[k] - lateral)
    return moving, rest, q * channel


def settle(rest, arriving, room):
    h = rest[0] + arriving[0]
    liquid = []
    for k in range(LAYERS):
        u = rest[1 + k] + arriving[1 + k]
        h = h + jnp.maximum(u - room[k], 0.0)
        liquid.append(jnp.minimum(u, room[k]))
    return h, liquid


def kernel(
    nr,
    nc,
    rain_h,
    infil_h,
    por_h,
    liq_h,
    ice_h,
    dir_h,
    kind_h,
    orate_h,
    lrate_h,
    weight_h,
    out_liq,
    out_h,
    out_c,
    rain,
    infil,
    por,
    liq,
    ice,
    dir_v,
    kind_v,
    orate_v,
    lrate_v,
    weight_v,
    same_block_v,
    to_block_v,
    nat,
    share_v,
    stat,
    dirs,
    coarse,
    moving,
    rest,
    sums,
    sstat,
    schannel,
    enter,
    zsend,
    zrecv,
    vsend,
    vrecv,
    csend,
    crecv,
    hsend,
    hrecv,
    bsend,
    brecv,
    in_sem,
    zs_sem,
    zh_sem,
    zr_sem,
    vs_sem,
    vr_sem,
    cs_sem,
    cr_sem,
    hs_sem,
    hr_sem,
    bs_sem,
    br_sem,
    row_sem,
    relay_sem,
    late_sem,
):
    mi = lax.axis_index("rows")
    mj = lax.axis_index("cols")
    has_up, has_down = mi > 0, mi < nr - 1
    has_left, has_right = mj > 0, mj < nc - 1

    barrier = pltpu.get_barrier_semaphore()
    lead = nc - 2
    is_lead = mj == lead

    def tell(i, j):
        pl.semaphore_signal(barrier, inc=1, device_id=(i, j), device_id_type=MESH)

    @pl.when(jnp.logical_not(is_lead))
    def _():
        tell(mi, lead)

    copies = [
        pltpu.make_async_copy(src, dst, in_sem.at[n])
        for n, (src, dst) in enumerate(
            (
                (rain_h, rain),
                (infil_h, infil),
                (por_h, por),
                (liq_h, liq),
                (ice_h, ice),
                (weight_h, weight_v),
                (dir_h, dir_v),
                (kind_h, kind_v),
                (orate_h, orate_v),
                (lrate_h, lrate_v),
            )
        )
    ]
    for copy in copies:
        copy.start()

    sides = (
        (has_up, mi - 1, has_left, has_right, nc - 1),
        (has_down, mi + 1, has_left, has_right, 0),
    )
    late = (lax.rem(mi, 4) == 3) & has_down
    late_side = (has_up & (lax.rem(mi, 4) != 0), late)
    early_side = (has_up & (lax.rem(mi, 4) == 0), has_down & (lax.rem(mi, 4) != 3))
    own_end = (0, nc - 1)

    def partners(v, signal):
        has, i, left, right, end = sides[v]
        signal(i, end)
        signal(i, mj)

        @pl.when(left)
        def _():
            signal(i, mj - 1)

        @pl.when(right)
        def _():
            signal(i, mj + 1)

        @pl.when(mj == own_end[v])
        def _():
            @pl.loop(0, nc)
            def _(k):
                signal(i, k)

    def count(v):
        one = 2 + has_left.astype(jnp.int32) + has_right.astype(jnp.int32)
        return one + nc * (mj == own_end[v]).astype(jnp.int32)

    def tell_late_one(i, j):
        @pl.when(j != lead)
        def _():
            tell(i, j)

    for v in range(2):

        @pl.when(early_side[v])
        def _(v=v):
            partners(v, tell_late_one)

    @pl.when(is_lead)
    def _():
        pl.semaphore_wait(barrier, nc - 1)
        near = [lead - 1, lead + 1]
        for k in near + [k for k in others(lead) if k not in near]:
            pl.semaphore_signal(row_sem, inc=1, device_id=(mi, k), device_id_type=MESH)

    row_c, col_c = iota((W, W), 0), iota((W, W), 1)
    same_block = (tenth(row_c) == tenth(col_c)) & (row_c < TILE) & (col_c < TILE)
    same_block_v[...] = jnp.where(same_block, 1.0, 0.0).astype(jnp.bfloat16)
    row_p, col_p = iota((128, 128), 0), iota((128, 128), 1)
    to_block = []
    for at, end, shift in ((3, 113, 0), (3, 53, 11), (3, 113, 5)):
        mine = (row_p >= at) & (row_p < end) & (tenth(row_p + 7) == col_p + 1 - shift)
        if shift == 11:
            mine = mine | ((row_p >= 59) & (row_p < 109) & (tenth(row_p - 49) == col_p + 1))
        to_block.append(jnp.where(mine, 1.0, 0.0).astype(jnp.bfloat16))
    to_block_v[...] = jnp.concatenate(to_block, 0)

    lane = iota((8, 128), 1)
    lane16 = iota((CR, 128), 1)
    sub16 = iota((CR, 128), 0)

    def piece(k, i, s, send, arrive):
        return pltpu.make_async_remote_copy(
            src_ref=zsend.at[k],
            dst_ref=zrecv.at[s],
            send_sem=send,
            recv_sem=arrive,
            device_id=(i, k),
            device_id_type=MESH,
        )

    def row_pieces():
        return pltpu.make_async_remote_copy(
            src_ref=zsend.at[: nc - 1],
            dst_ref=zrecv.at[: nc - 1],
            send_sem=zs_sem,
            recv_sem=zr_sem.at[0],
            device_id=(mi, mj),
            device_id_type=MESH,
        )

    first_up = has_up & (mj == 0)
    last_down = has_down & (mj == nc - 1)

    def first_run(a):
        return pltpu.roll(a, HALO, 1)

    def second_run(a, b):
        return jnp.where(lane16 < 21, pltpu.roll(a, 21, 1), pltpu.roll(b, 21, 1))

    def third_run(a):
        return pltpu.roll(a, 59, 1)

    def fourth_run(a, b):
        return jnp.where(lane16 < 81, pltpu.roll(a, 81, 1), pltpu.roll(b, 81, 1))

    def rows_of(f, rr):
        return [nat.at[2 * f + half][pl.ds(rr, CR, stride=REFINE), :] for half in range(2)]

    def field(f):
        return (dirs, ROWS) if f == DIR else (stat.at[f], 0)

    def vertical(v, i):
        return pltpu.make_async_remote_copy(
            src_ref=vsend.at[v],
            dst_ref=vrecv.at[v],
            send_sem=vs_sem.at[v],
            recv_sem=vr_sem.at[v],
            device_id=(i, mj),
            device_id_type=MESH,
        )

    def corner(v, s, i, j):
        return pltpu.make_async_remote_copy(
            src_ref=csend.at[v, s],
            dst_ref=crecv.at[v, s],
            send_sem=cs_sem.at[v, s],
            recv_sem=cr_sem.at[v, s],
            device_id=(i, j),
            device_id_type=MESH,
        )

    incoming = sum(late_side[v].astype(jnp.int32) * count(v) for v in range(2))

    any_late = late_side[0] | late_side[1]
    passes_on = (mj == lead - 1) | (mj == lead + 1)

    def rows_ready():
        pl.semaphore_wait(barrier, incoming)

    def pass_on():
        pl.semaphore_signal(relay_sem, inc=1, device_id=(mi, lead), device_id_type=MESH)

    def send_ends(v):
        @pl.when(mj == own_end[v])
        def _():
            @pl.loop(0, nc)
            def _(k):
                piece(k, sides[v][1], CR + v, zh_sem, zr_sem.at[1 + v]).start()

    def send_rows(v):
        _, i, left, right, _ = sides[v]
        vertical(v, i).start()

        @pl.when(left)
        def _():
            corner(v, 0, i, mj - 1).start()

        @pl.when(right)
        def _():
            corner(v, 1, i, mj + 1).start()

    def tell_early(v):
        def signal(i, j):
            pl.semaphore_signal(late_sem.at[1 - v], inc=1, device_id=(i, j), device_id_type=MESH)

        partners(v, signal)

    def coarse_part():
        for copy in copies[:5]:
            copy.wait()
        rain_x, por_x = rain[...], por[...]
        top_sat = (liq[0] + ice[0]) / por_x
        capacity = infil[...] * jnp.maximum(1.0 - top_sat, 0.1)
        excess = rain_x * rain_x / (rain_x + capacity)
        top = liq[0] + (rain_x - excess) / (1000.0 * thickness[0])
        strip = [excess, por_x, top] + [liq[k] for k in range(1, LAYERS)] + [ice[k] for k in range(LAYERS)]

        slot = lax.shift_right_logical(lane * 2731, 16)
        t = lane - slot * 24
        for half in range(2):
            base = (iota((8, 128), 0) + 8 * half) * 16 - 1 + t
            inside = jnp.clip(base, 0, W - 1)
            index = inside & 127
            low = inside < 128
            for group in range(2):
                packed = jnp.zeros((8, 128), jnp.float32)
                for n in range(5):
                    x = strip[group * 5 + n]
                    a = jnp.broadcast_to(x[:, :128], (8, 128))
                    b = jnp.broadcast_to(x[:, 128:], (8, 128))
                    packed = jnp.where(slot == n, jnp.where(low, take(a, index), take(b, index)), packed)
                for s in range(8):
                    zsend[8 * half + s, :, 128 * group : 128 * group + 128] = packed[s : s + 1]

        zrecv[mj] = zsend[mj]

        @pl.when(jnp.logical_not(has_down))
        def _():
            zrecv[CR] = zsend[mj]

        @pl.when(jnp.logical_not(has_up))
        def _():
            zrecv[CR + 1] = zsend[mj]

    def tile_arrived():
        for copy in copies[5:]:
            copy.wait()

    def vertical_part():
        no_lanes = jnp.zeros((CR, 96), jnp.float32)

        def in_halves(x):
            return x[:, :128], jnp.concatenate([x[:, 128:], no_lanes[: x.shape[0]]], 1)

        edges, totals = [], []
        for v in range(2):
            r = v * (TILE - CR)
            kind_x = kind_v[r : r + CR]
            edge = [
                dir_v[r : r + CR].astype(jnp.float32),
                jnp.where(kind_x == 2, 0.0, orate_v[r : r + CR].astype(jnp.float32)),
                jnp.where(kind_x == 0, 1.0, 0.0),
                lrate_v[r : r + CR].astype(jnp.float32),
                weight_v[r : r + CR].astype(jnp.float32),
            ]
            edge = [in_halves(x) for x in edge]
            mine = sub16 >= CR - REFINE if v else sub16 < REFINE
            total = [jnp.sum(jnp.where(mine, x, 0.0), 0, keepdims=True) for x in edge[SHARE]]
            edges.append(edge)
            totals.append(jnp.concatenate(total, 1))
        totals.append(jnp.zeros((6, W), jnp.float32))
        per_mean = 100.0 / jnp.where(iota((8, W), 1) < TILE, dot3(jnp.concatenate(totals, 0), same_block_v[...]), 1.0)
        place = lane16 - HALO * sub16
        for v in (1, 0):
            r = v * (CR - HALO)
            for half in range(2):
                scale = per_mean[v : v + 1, 128 * half : 128 * half + 128]
                for f in range(FIELDS):
                    x = edges[v][f][half][r : r + HALO]
                    vsend[v, half, HALO * f : HALO * f + HALO] = x * scale if f == SHARE else x
                vsend[v, half, HALO * FIELDS :] = jnp.zeros((1, 128), jnp.float32)
            a, b = vsend[v, 0], vsend[v, 1]
            if v == 0:
                vsend[v, 0], vsend[v, 1] = third_run(a), fourth_run(a, b)
            else:
                vsend[v, 0], vsend[v, 1] = first_run(a), second_run(a, b)
            for n, (x, at) in enumerate(((a, 0), (b, 29))):
                end = jnp.where((place >= 0) & (place < HALO), take(x, jnp.clip(place + at, 0, 127)), 0.0)
                csend[v, n] = jnp.sum(end, 0, keepdims=True)

    def tile_part():
        kind_x = kind_v[...]
        natural = (
            dir_v[...].astype(jnp.float32),
            jnp.where(kind_x == 2, 0.0, orate_v[...].astype(jnp.float32)),
            jnp.where(kind_x == 0, 1.0, 0.0),
            lrate_v[...].astype(jnp.float32),
            weight_v[...].astype(jnp.float32),
            jnp.where(kind_x == 1, 1.0, 0.0),
        )
        no_lanes = jnp.zeros((TILE, 96), jnp.float32)
        for f in range(FIELDS + 1):
            nat[2 * f] = natural[f][:, :128]
            nat[2 * f + 1] = jnp.concatenate([natural[f][:, 128:], no_lanes], 1)

        weights = [rows_of(SHARE, rr) for rr in range(REFINE)]
        total = [functools.reduce(lambda a, b: a + b, [w[half] for w in weights]) for half in range(2)]
        block_sum = dot3(jnp.concatenate(total, 1), same_block_v[...])
        per_mean = 100.0 / jnp.where(iota((CR, W), 1) < TILE, block_sum, 1.0)
        shares = [[w[half] * per_mean[:, 128 * half : 128 * half + 128] for half in range(2)] for w in weights]
        for rr in range(REFINE):
            for half in range(2):
                share_v[2 * rr + half] = shares[rr][half]

    def send_pieces():
        for k in others(mj):
            piece(k, mi, mj, zs_sem, zr_sem.at[0]).start()

    def meet_early():
        @pl.when(passes_on)
        def _():
            pl.semaphore_wait(row_sem, 1)

        @pl.when(jnp.logical_not(is_lead))
        def _():
            rows_ready()

        @pl.when(passes_on)
        def _():
            pass_on()

        @pl.when(is_lead)
        def _():
            pl.semaphore_wait(relay_sem, 2)

        for v in (1, 0):

            @pl.when(late_side[v])
            def _(v=v):
                tell_early(v)

    def send_late():
        for v in (1, 0):

            @pl.when(late_side[v])
            def _(v=v):
                send_rows(v)

    @pl.when(late)
    def _():
        tile_arrived()
        vertical_part()
        meet_early()
        send_late()

    coarse_part()

    @pl.when(late)
    def _():
        send_ends(1)
        send_ends(0)

    @pl.when(is_lead)
    def _():
        send_pieces()

    @pl.when(jnp.logical_not(late))
    def _():
        tile_arrived()

    tile_part()

    @pl.when(any_late & jnp.logical_not(late))
    def _():
        meet_early()
        send_ends(0)

    shares = [[share_v[2 * rr + half] for half in range(2)] for rr in range(REFINE)]

    def slab_place(rr, f):
        n = rr * FIELDS + f
        return n // 18, HALO * (n % 9) + 64 * (n % 18 // 9)

    slabs = [jnp.zeros((CR, 128), jnp.float32)] * 3
    for rr in range(REFINE):
        for f in range(FIELDS):
            a, b = shares[rr] if f == SHARE else rows_of(f, rr)
            x = jnp.where(lane16 < HALO, a, jnp.where((lane16 >= 29) & (lane16 < 32), b, 0.0))
            n, at = slab_place(rr, f)
            slabs[n] = slabs[n] + (pltpu.roll(x, at, 1) if at else x)
    for n in range(3):
        hsend[n] = slabs[n]

    def sideways(n, j):
        return pltpu.make_async_remote_copy(
            src_ref=hsend,
            dst_ref=hrecv.at[n],
            send_sem=hs_sem.at[n],
            recv_sem=hr_sem.at[n],
            device_id=(mi, j),
            device_id_type=MESH,
        )

    @pl.when(jnp.logical_not(is_lead))
    def _():
        @pl.when(jnp.logical_not(any_late & passes_on))
        def _():
            pl.semaphore_wait(row_sem, 1)

        send_pieces()

    @pl.when(has_left)
    def _():
        sideways(0, mj - 1).start()

    @pl.when(has_right)
    def _():
        sideways(1, mj + 1).start()

    @pl.when(jnp.logical_not(late))
    def _():
        vertical_part()
        send_late()

    for p in range(PAIRS):
        for f in range(FIELDS + 1):
            if f == SHARE:
                (a, b), (c, d) = shares[p], shares[p + PAIRS]
            else:
                (a, b), (c, d) = rows_of(f, p), rows_of(f, p + PAIRS)
            ref, off = field(f)
            r = off + p * ROWS
            ref[r : r + CR] = first_run(a)
            ref[r + CR : r + 2 * CR] = jnp.where(lane16 < SPLIT, second_run(a, b), third_run(c))
            ref[r + 2 * CR : r + ROWS] = fourth_run(c, d)

    def strip_own(f, v, out):
        ref, off = field(f)
        for half in range(2):
            at = 8 * half + (0 if v else HALO)
            r = off + (v + half) * CR + v * (CR - 1)
            out[at : at + PAIRS] = ref[pl.ds(r, PAIRS, stride=ROWS), :]

    lane8, sub8 = iota((8, 128), 1), iota((8, 128), 0)
    schannel[...] = jnp.zeros(schannel.shape, jnp.float32)
    for v in range(2):
        strip_own(CHANNEL, v, schannel.at[v])

    row48, lane48 = iota((ROWS, 128), 0), iota((ROWS, 128), 1)
    in_first = (row48 == 0) | ((row48 == CR) & (lane48 < SPLIT))
    in_last = (row48 == ROWS - 1) | ((row48 == 2 * CR - 1) & (lane48 >= SPLIT))
    for p in range(PAIRS):
        out = in_first if p < 2 else in_last if p > 2 else in_first | in_last
        r = p * ROWS
        stat[CHANNEL, r : r + ROWS] = jnp.where(out, 0.0, stat[CHANNEL, r : r + ROWS])

    def send_early(v):
        @pl.when(early_side[v])
        def _():
            pl.semaphore_wait(late_sem.at[v], count(v))
            send_rows(v)
            send_ends(v)

    for v, (has, i, left, right, end) in enumerate(sides):

        @pl.when(jnp.logical_not(has))
        def _(v=v):
            vrecv[1 - v] = jnp.zeros(vrecv.shape[1:], jnp.float32)

        @pl.when(jnp.logical_not(has & left))
        def _(v=v):
            crecv[1 - v, 1] = jnp.zeros((1, 128), jnp.float32)

        @pl.when(jnp.logical_not(has & right))
        def _(v=v):
            crecv[1 - v, 0] = jnp.zeros((1, 128), jnp.float32)

    @pl.when(jnp.logical_not(has_right))
    def _():
        hrecv[0] = jnp.zeros(hrecv.shape[1:], jnp.float32)

    @pl.when(jnp.logical_not(has_left))
    def _():
        hrecv[1] = jnp.zeros(hrecv.shape[1:], jnp.float32)

    def columns(n):
        lanes = iota((n, 128), 1)
        return (
            tenth(lanes + 7),
            tenth(jnp.where(lanes < SPLIT, lanes + 117, lanes - 49)),
            jnp.minimum(tenth(lanes + 57), 17),
        )

    def layers_of(wide):
        por_w = wide[1]
        liquid, ice_w, room, per_pore = [], [], [], []
        for k in range(LAYERS):
            depth = 1000.0 * thickness[k]
            liquid.append(wide[2 + k] * depth)
            ice_w.append(wide[2 + LAYERS + k] * depth)
            room.append((por_w - wide[2 + LAYERS + k]) * depth)
            per_pore.append((math.sqrt(layer_speed[k]) / depth) / por_w)
        return liquid, ice_w, room, per_pore

    @pl.when(has_right)
    def _():
        sideways(0, mj).wait_recv()

    @pl.when(has_left)
    def _():
        sideways(1, mj).wait_recv()

    def span(at):
        return (lane16 >= at) & (lane16 < at + HALO)

    for p in range(PAIRS):
        for f in range(FIELDS):
            ref, off = field(f)
            r = off + p * ROWS
            for rr, (left_row, left_at), (right_row, right_at) in (
                (p, (r, 0), (r + CR, SPLIT - HALO)),
                (p + PAIRS, (r + CR, SPLIT), (r + 2 * CR, 113)),
            ):
                n, at = slab_place(rr, f)
                from_left = pltpu.roll(hrecv[1, n], (left_at - 29 - at) % 128, 1)
                from_right = pltpu.roll(hrecv[0, n], (right_at - at) % 128, 1)
                ref[left_row : left_row + CR] = jnp.where(
                    span(left_at), from_left, ref[left_row : left_row + CR]
                )
                ref[right_row : right_row + CR] = jnp.where(
                    span(right_at), from_right, ref[right_row : right_row + CR]
                )

    END = ROWS * (PAIRS + 1)
    sub_up = functools.partial(pltpu.roll, shift=1, axis=0)

    def sub_down(x):
        return pltpu.roll(x, x.shape[0] - 1, 0)

    def across(x):
        x0, x1, x2 = x[:CR], x[CR : 2 * CR], x[2 * CR :]
        return (
            jnp.where(lane16 < 53, pltpu.roll(x1, 72, 1), pltpu.roll(x2, 50, 1)),
            pltpu.roll(x2, 68, 1),
            pltpu.roll(x0, SPLIT, 1),
            jnp.where(lane16 < 63, pltpu.roll(x0, 78, 1), pltpu.roll(x1, 60, 1)),
        )

    def wrap(ref):
        a, b, c, d = across(ref[END - ROWS : END])
        ref[:CR] = sub_up(a)
        ref[CR : 2 * CR] = jnp.where(lane16 < SPLIT, sub_up(b), c)
        ref[2 * CR : ROWS] = d
        a, b, c, d = across(ref[ROWS : 2 * ROWS])
        ref[END : END + CR] = a
        ref[END + CR : END + 2 * CR] = jnp.where(lane16 < SPLIT, b, sub_down(c))
        ref[END + 2 * CR : END + ROWS] = sub_down(d)

    wrap(dirs)
    sums[...] = jnp.zeros(sums.shape, jnp.float32)

    send_early(1)
    row_pieces().wait_recv()

    def rows_at(group, slots):
        return jnp.concatenate([zrecv[n, :, 128 * group : 128 * group + 128] for n in slots], 0)

    packed_rows = [rows_at(g, range(CR)) for g in range(2)]
    wide = [
        jnp.concatenate([take(packed_rows[f // 5], c + 24 * (f % 5)) for c in columns(CR)], 0) for f in range(COARSE)
    ]
    liquid_w, ice_w, room, per_pore = layers_of(wide)
    for n, x in enumerate(ice_w + room + per_pore + liquid_w + wide[:1]):
        coarse[n] = x

    def finish(b, step):
        top, bottom = ROWS + HALO * ROWS, ROWS + ROWS + CR - 1
        for f in range(FIELDS):
            wrap(moving.at[b, f])
            enter[step, 0, f, 6:7] = moving[b, f, top : top + 1]
            enter[step, 0, f, 14:15] = moving[b, f, top + CR : top + CR + 1]
            enter[step, 1, f, 1:2] = moving[b, f, bottom + CR : bottom + CR + 1]
            enter[step, 1, f, 9:10] = moving[b, f, bottom + 2 * CR : bottom + 2 * CR + 1]

    def main_in(b, r, c):
        masks = inflow_masks(*[dirs[pl.ds(r + n * ROWS, CR), :] for n in range(3)])
        arriving = [
            inflow(masks, *[moving[b, f, pl.ds(r + n * ROWS, CR), :] for n in range(3)])
            for f in range(FIELDS)
        ]
        left = [rest[f, pl.ds(r, CR), :] for f in range(FIELDS)]
        return settle(left, arriving, [coarse[LAYERS + k, c : c + CR] for k in range(LAYERS)])

    def main_out(b, r, c, h, liquid):
        move, left, taken = outflow(
            h,
            liquid,
            stat[ORATE, pl.ds(r, CR), :],
            stat[LAND, pl.ds(r, CR), :],
            stat[CHANNEL, pl.ds(r, CR), :],
            stat[LRATE, pl.ds(r, CR), :],
            [coarse[k, c : c + CR] for k in range(LAYERS)],
            [coarse[2 * LAYERS + k, c : c + CR] for k in range(LAYERS)],
        )
        for f in range(FIELDS):
            moving[b, f, pl.ds(r + ROWS, CR), :] = move[f]
            rest[f, pl.ds(r, CR), :] = left[f]
        sums[LAYERS + 1, c : c + CR] += taken

    def row_at(p, c):
        return p * ROWS + c

    for c in range(0, ROWS, CR):
        liquid = [coarse[3 * LAYERS + k, c : c + CR] for k in range(LAYERS)]
        drain = []
        for k in range(LAYERS):
            sat = (liquid[k] + coarse[k, c : c + CR]) * coarse[2 * LAYERS + k, c : c + CR]
            sat = jnp.minimum(sat, math.sqrt(layer_speed[k]))
            drain.append(liquid[k] * (sat * sat))
        taken_c = jnp.zeros((CR, 128), jnp.float32)
        for p in OUTER_FIRST:
            r = row_at(p, c)
            h = coarse[4 * LAYERS, c : c + CR] * stat[SHARE, r : r + CR]
            q = stat[ORATE, r : r + CR] * h * (h / (h + 2.0))
            moving[0, 0, r + ROWS : r + ROWS + CR] = q * stat[LAND, r : r + CR]
            rest[0, r : r + CR] = h - q
            taken_c = taken_c + q * stat[CHANNEL, r : r + CR]
            for k in range(LAYERS):
                lateral = stat[LRATE, r : r + CR] * drain[k]
                moving[0, 1 + k, r + ROWS : r + ROWS + CR] = lateral
                rest[1 + k, r : r + CR] = liquid[k] - lateral
        sums[LAYERS + 1, c : c + CR] = taken_c

    finish(0, 0)

    for b in range(2):

        for p in INNER_FIRST:
            for c in range(0, ROWS, CR):
                r = row_at(p, c)
                main_out(1 - b, r, c, *main_in(b, r, c))

        finish(1 - b, 1 + b)

    for p in INNER_FIRST:
        for c in range(0, ROWS, CR):
            h, liquid = main_in(0, row_at(p, c), c)
            out = [in_first[c : c + CR]] * (p < HALO and c < 2 * CR) + [in_last[c : c + CR]] * (p >= PAIRS - HALO and c > 0)
            for n, x in enumerate(liquid + [h]):
                for mine in out:
                    x = jnp.where(mine, 0.0, x)
                sums[n, c : c + CR] += x

    scales = [0.01 / (1000.0 * x) for x in thickness] + [0.01, 0.01]

    def three(n):
        return jnp.concatenate([sums[n, c : c + CR] for c in range(0, ROWS, CR)], 1) * scales[n]

    means = dot2(jnp.concatenate([three(n) for n in range(LAYERS + 2)], 0), to_block_v[...])
    back = means[:CR]
    for n in range(1, LAYERS + 2):
        back = back + pltpu.roll(means[n * CR : (n + 1) * CR], 16 * n, 1)
    for s in range(1, CR - 1):
        bsend[s] = back[s : s + 1]

    def answer(k, s):
        return pltpu.make_async_remote_copy(
            src_ref=bsend.at[k],
            dst_ref=brecv.at[s],
            send_sem=bs_sem,
            recv_sem=br_sem,
            device_id=(mi, k),
            device_id_type=MESH,
        )

    def answers():
        return pltpu.make_async_remote_copy(
            src_ref=bsend.at[: nc - 1],
            dst_ref=brecv.at[: nc - 1],
            send_sem=bs_sem,
            recv_sem=br_sem,
            device_id=(mi, mj),
            device_id_type=MESH,
        )

    def inner(n):
        return 1 + lax.rem(mj + n, CR - 2)

    for n in (11, 3, 10, 2, 7, 6, 8, 9, 5, 4, 1, 0, 12):
        answer(inner(n), mj).start()

    @pl.when((mj == 0) | (mj == nc - 1))
    def _():
        answer(inner(CR - 3), mj).start()

    def strip(v):
        has, _, left, right, _ = sides[v]
        for f in range(FIELDS):
            strip_own(f, v, sstat.at[f])

        @pl.when(has)
        def _():
            vertical(1 - v, mi).wait_recv()
            piece(0, mi, CR + 1 - v, zh_sem, zr_sem.at[2 - v]).wait_recv()

        @pl.when(has & left)
        def _():
            corner(1 - v, 1, mi, mj).wait_recv()

        @pl.when(has & right)
        def _():
            corner(1 - v, 0, mi, mj).wait_recv()

        halo, far = vrecv.at[1 - v], (PAIRS if v else 0)
        for half, at in enumerate((SPLIT, 113) if v else (0, SPLIT - HALO)):
            index = jnp.clip(HALO * sub16 + lane16 - at, 0, 127)
            side = take(jnp.broadcast_to(crecv[1 - v, 1 - half], (CR, 128)), index)
            halo[half] = jnp.where(span(at), side, halo[half])
        for f in range(FIELDS):
            for half in range(2):
                at = 8 * half + far
                sstat[f, at : at + HALO] = halo[half, HALO * f : HALO * f + HALO]

        sub = sub8 >= PAIRS if v else sub8 < HALO
        groups = [
            jnp.where(sub, zrecv[CR + 1 - v, :, at : at + 128], zrecv[v * (CR - 1), :, at : at + 128])
            for at in (0, 128)
        ]
        tables = columns(8)[v : v + 2]
        wide = [jnp.concatenate([take(groups[f // 5], c + 24 * (f % 5)) for c in tables], 0) for f in range(COARSE)]
        liquid, ice_w, room, per_pore = layers_of(wide)
        sdir = sstat[DIR]
        masks = inflow_masks(sub_up(sdir), sdir, sub_down(sdir))
        entering = (sub16 & 7) == (1 if v else 6)
        h = wide[0] * sstat[SHARE]
        channel = jnp.zeros((CR, 128), jnp.float32)
        for step in range(3):
            move, rest_s, taken = outflow(
                h, liquid, sstat[ORATE], sstat[LAND], schannel[v], sstat[LRATE], ice_w, per_pore
            )
            channel = channel + taken
            move = [jnp.where(entering, enter[step, v, f], m) for f, m in enumerate(move)]
            arriving = [inflow(masks, sub_up(m), m, sub_down(m)) for m in move]
            h, liquid = settle(rest_s, arriving, room)

        first_row = 2 if v else HALO
        mine = ((sub16 & 7) >= first_row) & ((sub16 & 7) < first_row + HALO)
        mine = mine & ((sub16 >= 8) | (lane16 >= SPLIT)) if v else mine & ((sub16 < 8) | (lane16 < SPLIT))
        rows = []
        for n, x in enumerate(liquid + [h, channel]):
            x = jnp.where(mine, x, 0.0) * scales[n]
            rows.append(jnp.concatenate([jnp.sum(x[at : at + 8], 0, keepdims=True) for at in (0, 8)], 1))
        rows.append(jnp.zeros((2, 2 * 128), jnp.float32))
        part = dot2(jnp.concatenate(rows, 0), to_block_v[128 * v : 128 * v + 256])
        part = pltpu.roll(part, 0, 1, stride=16, stride_axis=0)
        s = v * (CR - 1)
        bsend[s] = back[s : s + 1] + jnp.sum(part, 0, keepdims=True)

        @pl.when(mj != s)
        def _():
            answer(s, mj).start()

    strip(0)
    send_early(0)
    strip(1)

    brecv[mj] = bsend[mj]

    row_pieces().wait_send()

    @pl.when(first_up | last_down)
    def _():
        pltpu.make_async_remote_copy(
            src_ref=zsend,
            dst_ref=zrecv.at[:nc],
            send_sem=zh_sem,
            recv_sem=zr_sem.at[1],
            device_id=(mi, mj),
            device_id_type=MESH,
        ).wait_send()

    for v, (has, i, left, right, end) in enumerate(sides):

        @pl.when(has)
        def _(v=v, i=i):
            vertical(v, i).wait_send()

        @pl.when(has & left)
        def _(v=v, i=i):
            corner(v, 0, i, mj - 1).wait_send()

        @pl.when(has & right)
        def _(v=v, i=i):
            corner(v, 1, i, mj + 1).wait_send()

    @pl.when(has_left)
    def _():
        sideways(0, mj - 1).wait_send()

    @pl.when(has_right)
    def _():
        sideways(1, mj + 1).wait_send()

    answers().wait_recv()

    gather = jnp.minimum(iota((8, 128), 0) * 16 + (lane & 15), 127)
    owner = lax.shift_right_logical(lane, 4)
    for half in range(2):
        out = jnp.zeros((8, 128), jnp.float32)
        for s in range(8):
            x = jnp.broadcast_to(brecv[8 * half + s], (8, 128))
            out = jnp.where(owner == s, take(x, gather), out)
        lanes = slice(128 * half, 128 * half + 128)
        for k in range(LAYERS):
            out_liq[k, :, lanes] = out[k : k + 1]
        out_h[:, lanes] = out[LAYERS : LAYERS + 1]
        out_c[:, lanes] = out[LAYERS + 1 : LAYERS + 2]

    answers().wait_send()


def store(a, b, c, out_a, out_b, out_c, sem):
    copies = [
        pltpu.make_async_copy(src, dst, sem.at[n])
        for n, (src, dst) in enumerate(((a, out_a), (b, out_b), (c, out_c)))
    ]
    for copy in copies:
        copy.start()
    for copy in copies:
        copy.wait()


def solution(mesh):
    nr, nc = mesh.shape["rows"], mesh.shape["cols"]
    f32, bf16 = jnp.float32, jnp.bfloat16

    def step(*args):
        v = pltpu.VMEM
        dma = pltpu.SemaphoreType.DMA
        args = [pltpu.with_memory_space_constraint(x, pltpu.HBM) for x in args]
        results = pl.pallas_call(
            functools.partial(kernel, nr, nc),
            out_shape=(v((LAYERS, 1, W), f32), v((1, W), f32), v((1, W), f32)),
            in_specs=[pl.BlockSpec(memory_space=pltpu.HBM)] * 10,
            out_specs=[pl.BlockSpec(memory_space=pltpu.VMEM)] * 3,
            scratch_shapes=[
                v((1, W), f32),
                v((1, W), f32),
                v((1, W), f32),
                v((LAYERS, 1, W), f32),
                v((LAYERS, 1, W), f32),
                v((TILE, TILE), jnp.int32),
                v((TILE, TILE), jnp.int32),
                v((TILE, TILE), bf16),
                v((TILE, TILE), bf16),
                v((TILE, TILE), bf16),
                v((W, W), bf16),
                v((3 * 128, 128), bf16),
                v((2 * FIELDS + 2, TILE, 128), f32),
                v((2 * REFINE, CR, 128), f32),
                v((FIELDS + 1, 8 * ROWS, 128), f32),
                v((9 * ROWS, 128), f32),
                v((4 * LAYERS + 1, ROWS, 128), f32),
                v((2, FIELDS, (PAIRS + 2) * ROWS, 128), f32),
                v((FIELDS, PAIRS * ROWS, 128), f32),
                v((LAYERS + 2, ROWS, 128), f32),
                v((FIELDS, CR, 128), f32),
                v((2, CR, 128), f32),
                v((3, 2, FIELDS, CR, 128), f32),
                v((CR, 1, W), f32),
                v((CR + 2, 1, W), f32),
                v((2, 2, CR, 128), f32),
                v((2, 2, CR, 128), f32),
                v((2, 2, 1, 128), f32),
                v((2, 2, 1, 128), f32),
                v((3, CR, 128), f32),
                v((2, 3, CR, 128), f32),
                v((CR, 1, 128), f32),
                v((CR, 1, 128), f32),
                dma((10,)),
                dma(()),
                dma(()),
                dma((3,)),
                dma((2,)),
                dma((2,)),
                dma((2, 2)),
                dma((2, 2)),
                dma((2,)),
                dma((2,)),
                dma(()),
                dma(()),
                pltpu.SemaphoreType.REGULAR,
                pltpu.SemaphoreType.REGULAR,
                pltpu.SemaphoreType.REGULAR((2,)),
            ],
            compiler_params=pltpu.CompilerParams(
                collective_id=0, has_side_effects=True, vmem_limit_bytes=62 * 1024 * 1024
            ),
        )(*args)
        return pl.pallas_call(
            store,
            out_shape=(
                jax.ShapeDtypeStruct((LAYERS, 1, W), f32),
                jax.ShapeDtypeStruct((1, W), f32),
                jax.ShapeDtypeStruct((1, W), f32),
            ),
            in_specs=[pl.BlockSpec(memory_space=pltpu.VMEM)] * 3,
            out_specs=[pl.BlockSpec(memory_space=pltpu.HBM)] * 3,
            scratch_shapes=[dma((3,))],
        )(*[pltpu.with_memory_space_constraint(x, pltpu.VMEM) for x in results])

    return jax.shard_map(
        step,
        mesh=mesh,
        in_specs=(
            P(("rows", "cols"), None),
            P(("rows", "cols"), None),
            P(("rows", "cols"), None),
            P(None, ("rows", "cols"), None),
            P(None, ("rows", "cols"), None),
            P("rows", "cols"),
            P("rows", "cols"),
            P("rows", "cols"),
            P("rows", "cols"),
            P("rows", "cols"),
        ),
        out_specs=(
            P(None, ("rows", "cols"), None),
            P(("rows", "cols"), None),
            P(("rows", "cols"), None),
        ),
        check_vma=False,
    )
```
